256 devices in a mesh: src: 32 (over y, z), tgt: 8 (over x, core).
Axes of the slice: x: 4, y: 4, z: 8, core: 2. Of those that a mesh axis runs over, the one named last changes fastest.
Arguments:
- source_points: bfloat16 [32768, 128], P('src'), may hold values from -2 to 2
- target_points: bfloat16 [32768, 128], P(('tgt', 'src')), may hold values from -2 to 2
- initial_potential: float32 [32768], P('tgt'), may hold values from -4 to 4
- pair_list: int32 [32, 8, 16], P('src', 'tgt'), may hold values from -1 to 15, as said below
- pair_count: int32 [32, 8], P('src', 'tgt'), may hold values from 2 to 16, as said below
Outputs:
- source_potential: float32 [32768], P('src')
- target_potential: float32 [32768], P('tgt')
The draws below stay inside these ranges and needn't reach their ends.
Inputs may be any that keep to these rules, and one draw needn't show every extreme that they name: `pair_count`: every source block and every target block is in at least one kept pair; the device with the most kept pairs holds all 16. `pair_list`: entries in slots below the device's pair_count are distinct local pair numbers b * 8 + c (b the source block, c the target block within the device's points); the other slots hold -1.
All inputs are finite; a program needn't handle non-finite values.
Results may differ from the reference program's by a relative error of at most 0.0003.
Values may be sent and summed in bfloat16 or wider, within the bound.
No kernel may reach another device: no remote copies, remote signals or barrier semaphores. Data moves between devices by JAX's collectives and lax.ppermute only.
A program may use at most 64 MiB of HBM per device.

```python
import math
import jax
import jax.numpy as jnp
from jax import lax

EMB = 128
BLOCK = 512
SB_DEV = 2
TB_DEV = 8
ITERS = 2
PAIRS_MAX = 16
NS = 32768
NT = 32768
N_SRC = 32
N_TGT = 8


def block_plan(key):
    key = jax.random.fold_in(key, 11)
    key_base, key_boost, key_top, key_order = jax.random.split(key, 4)
    base = jax.random.randint(key_base, (N_SRC, N_TGT), 2, PAIRS_MAX // 2 + 1)
    boost = jax.random.randint(key_boost, (N_SRC, N_TGT), 0, 8) == 0
    counts = jnp.where(boost, PAIRS_MAX, base).astype(jnp.int32).reshape(-1)
    chosen = jax.random.randint(key_top, (), 0, N_SRC * N_TGT)
    counts = counts.at[chosen].set(PAIRS_MAX).reshape(N_SRC, N_TGT)
    src_index = jnp.arange(N_SRC, dtype=jnp.int32)[:, None]
    tgt_index = jnp.arange(N_TGT, dtype=jnp.int32)[None, :]
    forced = tgt_index % SB_DEV * TB_DEV + src_index % TB_DEV
    slots = jnp.arange(PAIRS_MAX, dtype=jnp.int32)
    scores = jax.random.randint(key_order, (N_SRC, N_TGT, PAIRS_MAX), 0, 2 ** 20) * PAIRS_MAX + slots
    scores = jnp.where(slots[None, None, :] == forced[:, :, None], -1, scores)
    order = jnp.argsort(scores, axis=-1, stable=True).astype(jnp.int32)
    lists = jnp.where(slots[None, None, :] < counts[:, :, None], order, -1).astype(jnp.int32)
    return (lists, counts)


def draw_pair_list(key, part):
    lists, counts = block_plan(key)
    return lists


def draw_pair_count(key, part):
    lists, counts = block_plan(key)
    return counts


def point_cloud(key, count, radius_hi, offset):
    key_entries = jax.random.fold_in(key, 0)
    key_radius = jax.random.fold_in(key, 1)
    key_far = jax.random.fold_in(key, 3)
    entries = jnp.clip(jax.random.normal(key_entries, (count, EMB), jnp.float32), -4.0, 4.0)
    radius = jnp.exp(jax.random.uniform(key_radius, (count, 1), jnp.float32, 0.0, math.log(radius_hi)))
    far = jax.random.randint(key_far, (count, 1), 0, 32) == 0
    far = far.at[0, 0].set(True)
    values = 0.125 * radius * entries + jnp.where(far, offset, 0.0).astype(jnp.float32)
    return jnp.clip(values, -2.0, 2.0).astype(jnp.bfloat16)


def draw_source_points(key, part):
    key = jax.random.fold_in(key, 1)
    return point_cloud(key, NS, 3.0, 0.6)


def draw_target_points(key, part):
    key = jax.random.fold_in(key, 2)
    return point_cloud(key, NT, 3.0, -0.6)


def levels(key, extent, pieces, low, largest):
    level, own = 1.0, jax.random.fold_in(key, 6)
    for position, shards_of in pieces:
        draws = jnp.exp(jax.random.uniform(jax.random.fold_in(own, position), (shards_of,), jnp.float32, low / len(pieces), largest / len(pieces)))
        level = level * jnp.repeat(draws, extent[position] // shards_of).reshape([-1 if axis == position else 1 for axis in range(len(extent))])
    return level


def centred(rng, extent, deviation, bound, cuts=(), kind=jnp.bfloat16):
    drawn = jax.random.normal(rng, extent, jnp.float32) * deviation
    if len(cuts) > 0:
        drawn = levels(rng, extent, cuts, -0.22, 0.18) * drawn
    return jnp.clip(drawn, min=-bound, max=bound).astype(kind)


def setup_inputs(seed: int = 0) -> dict:
    streams_of = jax.random.split(jax.random.key(seed), 6)
    source_points = draw_source_points(jax.random.fold_in(streams_of[5], 71), 0)
    target_points = draw_target_points(jax.random.fold_in(streams_of[5], 71), 0)
    initial_potential = centred(streams_of[2], (NT,), 1.0, 4.0, ((0, 8),), jnp.float32)
    pair_list = draw_pair_list(jax.random.fold_in(streams_of[5], 71), 0)
    pair_count = draw_pair_count(jax.random.fold_in(streams_of[5], 71), 0)
    return {"source_points": source_points, "target_points": target_points, "initial_potential": initial_potential, "pair_list": pair_list, "pair_count": pair_count}


NEG_START = -1.0e30
EPS_REG = 0.2


def pair_cost(sources, targets, source_sq, target_sq, src_start, tgt_start):
    rows = lax.dynamic_slice_in_dim(sources, src_start, BLOCK, 0)
    cols = lax.dynamic_slice_in_dim(targets, tgt_start, BLOCK, 0)
    inner = jnp.dot(rows, cols.T, preferred_element_type=jnp.float32)
    row_sq = lax.dynamic_slice_in_dim(source_sq, src_start, BLOCK, 0)
    col_sq = lax.dynamic_slice_in_dim(target_sq, tgt_start, BLOCK, 0)
    return (row_sq[:, None] + col_sq[None, :]) - 2.0 * inner


def reference(source_points, target_points, initial_potential, pair_list, pair_count):
    n_source = source_points.shape[0]
    n_target = target_points.shape[0]
    source_sq = jnp.sum(jnp.square(source_points.astype(jnp.float32)), axis=1)
    target_sq = jnp.sum(jnp.square(target_points.astype(jnp.float32)), axis=1)
    slots = jnp.arange(PAIRS_MAX, dtype=jnp.int32)
    valid = (slots[None, None, :] < pair_count[:, :, None]).reshape(-1)
    local_pair = jnp.maximum(pair_list, 0).astype(jnp.int32)
    src_index = jnp.broadcast_to(jnp.arange(N_SRC, dtype=jnp.int32)[:, None, None], pair_list.shape)
    tgt_index = jnp.broadcast_to(jnp.arange(N_TGT, dtype=jnp.int32)[None, :, None], pair_list.shape)
    src_block = (src_index * SB_DEV + local_pair // TB_DEV).reshape(-1)
    tgt_block = (tgt_index * TB_DEV + local_pair % TB_DEV).reshape(-1)
    order = jnp.argsort(jnp.where(valid, 0, 1).astype(jnp.int32), stable=True)
    src_block = src_block[order].astype(jnp.int32)
    tgt_block = tgt_block[order].astype(jnp.int32)
    total = jnp.sum(valid.astype(jnp.int32))

    def sweep(potential, along_rows):
        length = n_source if along_rows else n_target
        start_state = (jnp.full((length,), NEG_START, jnp.float32), jnp.zeros((length,), jnp.float32))

        def advance(number, running):
            src_start = (src_block[number] * BLOCK).astype(jnp.int32)
            tgt_start = (tgt_block[number] * BLOCK).astype(jnp.int32)
            cost = pair_cost(source_points, target_points, source_sq, target_sq, src_start, tgt_start)
            if along_rows:
                shift = lax.dynamic_slice_in_dim(potential, tgt_start, BLOCK, 0)
                scores = (shift[None, :] - cost) / EPS_REG
                block_max = jnp.max(scores, axis=1)
                block_sum = jnp.sum(jnp.exp(scores - block_max[:, None]), axis=1)
                place = src_start
            else:
                shift = lax.dynamic_slice_in_dim(potential, src_start, BLOCK, 0)
                scores = (shift[:, None] - cost) / EPS_REG
                block_max = jnp.max(scores, axis=0)
                block_sum = jnp.sum(jnp.exp(scores - block_max[None, :]), axis=0)
                place = tgt_start
            old_max = lax.dynamic_slice_in_dim(running[0], place, BLOCK, 0)
            old_sum = lax.dynamic_slice_in_dim(running[1], place, BLOCK, 0)
            highest = jnp.maximum(old_max, block_max)
            new_sum = old_sum * jnp.exp(old_max - highest) + block_sum * jnp.exp(block_max - highest)
            return (lax.dynamic_update_slice_in_dim(running[0], highest, place, 0),
                    lax.dynamic_update_slice_in_dim(running[1], new_sum, place, 0))

        highest, summed = lax.fori_loop(0, total, advance, start_state)
        return highest + jnp.log(summed)

    target_potential = initial_potential
    source_potential = jnp.zeros((n_source,), jnp.float32)
    for iteration in range(ITERS):
        row_lse = sweep(target_potential, True)
        source_potential = EPS_REG * (-math.log(n_source) - row_lse)
        col_lse = sweep(source_potential, False)
        target_potential = EPS_REG * (-math.log(n_target) - col_lse)
    return source_potential, target_potential
```

```python
import functools
import math

import jax
import jax.numpy as jnp
from jax import lax
from jax.experimental import pallas as pl
from jax.experimental.pallas import tpu as pltpu
from jax.sharding import Mesh
from jax.sharding import PartitionSpec as P

BLOCK = 512
LANES = 128
EMB = 128
SB_DEV = 2
TB_DEV = 8
ITERS = 2
NEG_START = -1e30
EPS_REG = 0.2
LOG2E = math.log2(math.e)
SCALE = 2.0 * LOG2E / EPS_REG
GROUPS = BLOCK // LANES

bf16 = jnp.bfloat16
f32 = jnp.float32


def squares(points):
    values = points.astype(f32)
    sq = values * values
    high = sq.astype(bf16)
    low = (sq - high.astype(f32)).astype(bf16)
    parts = jnp.concatenate([high, low], axis=1)
    ones = jnp.ones((8, 2 * EMB), bf16)
    sums = lax.dot_general(ones, parts, (((1,), (1,)), ((), ())), preferred_element_type=f32)
    count = points.shape[0] // LANES
    return jnp.concatenate([sums[0:1, r * LANES:(r + 1) * LANES] for r in range(count)], axis=0)


def bias_columns(bias):
    high = bias.astype(bf16).astype(f32)
    rest = bias - high
    middle = rest.astype(bf16).astype(f32)
    low = rest - middle
    count = bias.shape[0]
    stacked = jnp.concatenate([high, middle, low, jnp.zeros((LANES - 3 * count, LANES), f32)], axis=0)
    return stacked.T.astype(bf16)


def combined(parts):
    highest = jnp.max(parts, axis=0)
    total = jnp.sum(jnp.exp2(parts - highest[None]), axis=0)
    return highest + jnp.log(total) * LOG2E


def half_bias(lse):
    return (-0.5 * EPS_REG / LOG2E) * (math.log2(32768) + lse)


def sweep(pairs_ref, count_ref, kept_ref, sum_ref, kept_bias, kept_count, acc_max, acc_sum, kept_first, out_ref):
    acc_max[...] = jnp.full(acc_max.shape, NEG_START, f32)
    acc_sum[...] = jnp.zeros(acc_sum.shape, f32)
    lane = lax.broadcasted_iota(jnp.int32, (LANES, LANES), 1) % kept_count
    ones = jnp.ones((BLOCK, LANES), bf16)

    def turn(number, carry):
        pair = pairs_ref[0, 0, number]
        first, second = pair // TB_DEV, pair % TB_DEV
        along, place = (first, second) if kept_first else (second, first)
        lhs = kept_ref[pl.ds(pl.multiple_of(along * BLOCK, BLOCK), BLOCK), :]
        bias = [jnp.where(lane == along * GROUPS + q, kept_bias, jnp.zeros_like(kept_bias)) for q in range(GROUPS)]
        lhs = jnp.concatenate([lhs, jnp.concatenate(bias, axis=0)], axis=1)
        rhs = sum_ref[pl.ds(pl.multiple_of(place * BLOCK, BLOCK), BLOCK), :]
        rhs = jnp.concatenate([rhs, ones], axis=1)
        scores = lax.dot_general(lhs, rhs, (((1,), (1,)), ((), ())), preferred_element_type=f32)
        old_max = acc_max[pl.ds(place, 1), :]
        highest = jnp.maximum(old_max, jnp.max(scores, axis=0, keepdims=True))
        block_sum = jnp.sum(jnp.exp2((scores - highest) * SCALE), axis=0, keepdims=True)
        acc_sum[pl.ds(place, 1), :] = acc_sum[pl.ds(place, 1), :] * jnp.exp2((old_max - highest) * SCALE) + block_sum
        acc_max[pl.ds(place, 1), :] = highest
        return carry

    lax.fori_loop(0, count_ref[0, 0], turn, 0)
    blocks = sum_ref.shape[0] // BLOCK
    total = acc_sum[...]
    lse = jnp.where(total > 0, acc_max[...] * SCALE + jnp.log(total) * LOG2E, NEG_START)
    dense = jnp.concatenate(
        [lse[b:b + 1, q * LANES:(q + 1) * LANES] for b in range(blocks) for q in range(GROUPS)], axis=0
    )
    for k in range(out_ref.shape[0]):
        out_ref[k] = dense


def first_rows(pairs_ref, count_ref, sources_ref, targets_ref, potential_ref, out_ref, acc_max, acc_sum):
    bias = 0.5 * (potential_ref[...] - squares(targets_ref[...]))
    sweep(pairs_ref, count_ref, targets_ref, sources_ref, bias_columns(bias), bias.shape[0], acc_max, acc_sum, False, out_ref)


def next_rows(pairs_ref, count_ref, sources_ref, targets_ref, parts_ref, out_ref, acc_max, acc_sum):
    bias = half_bias(combined(parts_ref[...]))
    sweep(pairs_ref, count_ref, targets_ref, sources_ref, bias_columns(bias), bias.shape[0], acc_max, acc_sum, False, out_ref)


def columns(pairs_ref, count_ref, sources_ref, targets_ref, parts_ref, out_ref, potential_ref, acc_max, acc_sum):
    bias = half_bias(combined(parts_ref[...]))
    potential_ref[...] = squares(sources_ref[...]) + 2.0 * bias
    sweep(pairs_ref, count_ref, sources_ref, targets_ref, bias_columns(bias), bias.shape[0], acc_max, acc_sum, True, out_ref)


def last_potential(targets_ref, parts_ref, potential_ref):
    potential_ref[...] = squares(targets_ref[...]) + 2.0 * half_bias(combined(parts_ref[...]))


SMEM = pl.BlockSpec(memory_space=pltpu.SMEM)
VMEM = pl.BlockSpec(memory_space=pltpu.VMEM)
PARAMS = pltpu.CompilerParams(vmem_limit_bytes=40 * 1024 * 1024)
STATS = [pltpu.VMEM((8, BLOCK), f32)] * 2


def spread(parts, axes):
    return lax.all_to_all(parts, axes, 0, 0, tiled=True)


def per_device(source_points, target_points, initial_potential, pair_list, pair_count):
    n_src = lax.axis_size(("y", "z"))
    n_tgt = lax.axis_size(("x", "c"))
    own = target_points.shape[0]
    targets = spread(jnp.broadcast_to(target_points[None], (n_src, own, EMB)), ("y", "z"))
    targets = targets.reshape(n_src * own, EMB)
    src_rows = source_points.shape[0] // LANES
    tgt_rows = targets.shape[0] // LANES

    def rows(kernel, operand):
        return pl.pallas_call(
            kernel,
            out_shape=jax.ShapeDtypeStruct((n_tgt, src_rows, LANES), f32),
            in_specs=[SMEM, SMEM, VMEM, VMEM, VMEM],
            out_specs=VMEM,
            scratch_shapes=STATS,
            compiler_params=PARAMS,
        )(pair_list, pair_count, source_points, targets, operand)

    col_parts = None
    for iteration in range(ITERS):
        if iteration == 0:
            row_parts = rows(first_rows, initial_potential.reshape(tgt_rows, LANES))
        else:
            row_parts = rows(next_rows, col_parts)
        row_parts = spread(row_parts, ("x", "c"))
        col_parts, source_potential = pl.pallas_call(
            columns,
            out_shape=[
                jax.ShapeDtypeStruct((n_src, tgt_rows, LANES), f32),
                jax.ShapeDtypeStruct((src_rows, LANES), f32),
            ],
            in_specs=[SMEM, SMEM, VMEM, VMEM, VMEM],
            out_specs=[VMEM, VMEM],
            scratch_shapes=STATS,
            compiler_params=PARAMS,
        )(pair_list, pair_count, source_points, targets, row_parts)
        col_parts = spread(col_parts, ("y", "z"))
    target_potential = pl.pallas_call(
        last_potential,
        out_shape=jax.ShapeDtypeStruct((tgt_rows, LANES), f32),
        in_specs=[VMEM, VMEM],
        out_specs=VMEM,
        compiler_params=PARAMS,
    )(targets, col_parts)
    return source_potential.reshape(-1), target_potential.reshape(-1)


def solution(mesh):
    fine = Mesh(mesh.devices.reshape(4, 8, 4, 2), ("y", "z", "x", "c"))
    src, tgt = ("y", "z"), ("x", "c")
    placed = (P(src, None), P(tgt + src, None), P(tgt), P(src, tgt, None), P(src, tgt))
    return jax.shard_map(
        per_device, mesh=fine, in_specs=placed, out_specs=(P(src), P(tgt)), check_vma=False
    )
```

```python
import functools
import math

import jax
import jax.numpy as jnp
from jax import lax
from jax.experimental import pallas as pl
from jax.experimental.pallas import tpu as pltpu
from jax.sharding import Mesh
from jax.sharding import PartitionSpec as P

BLOCK = 512
LANES = 128
EMB = 128
SB_DEV = 2
TB_DEV = 8
PAIRS_MAX = 16
ITERS = 2
NEG_START = -1e30
EPS_REG = 0.2
LOG2E = math.log2(math.e)
SCALE = 2.0 * LOG2E / EPS_REG
GROUPS = BLOCK // LANES

bf16 = jnp.bfloat16
f32 = jnp.float32


def squares(points):
    values = points.astype(f32)
    sq = values * values
    high = sq.astype(bf16)
    low = (sq - high.astype(f32)).astype(bf16)
    parts = jnp.concatenate([high, low], axis=1)
    ones = jnp.ones((8, 2 * EMB), bf16)
    sums = lax.dot_general(ones, parts, (((1,), (1,)), ((), ())), preferred_element_type=f32)
    count = points.shape[0] // LANES
    return jnp.concatenate([sums[0:1, r * LANES:(r + 1) * LANES] for r in range(count)], axis=0)


def bias_columns(bias):
    high = bias.astype(bf16).astype(f32)
    rest = bias - high
    middle = rest.astype(bf16).astype(f32)
    low = rest - middle
    count = bias.shape[0]
    stacked = jnp.concatenate([high, middle, low, jnp.zeros((LANES - 3 * count, LANES), f32)], axis=0)
    return stacked.T.astype(bf16)


def combined(parts):
    highest = jnp.max(parts, axis=0)
    total = jnp.sum(jnp.exp2(parts - highest[None]), axis=0)
    return highest + jnp.log(total) * LOG2E


def half_bias(lse):
    return (-0.5 * EPS_REG / LOG2E) * (math.log2(32768) + lse)


def clear(acc_max, acc_sum):
    acc_max[...] = jnp.full(acc_max.shape, NEG_START, f32)
    acc_sum[...] = jnp.zeros(acc_sum.shape, f32)


def sweep(pairs_ref, count, kept_ref, sum_ref, bias, acc_max, acc_sum, even, odd, kept_first, offset=0):
    kept_count = bias.shape[0]
    kept_bias = bias_columns(bias)
    lane = lax.broadcasted_iota(jnp.int32, (LANES, LANES), 1) & (kept_count - 1)
    ones = jnp.ones((BLOCK, LANES), bf16)
    total_pairs = count

    def where(number):
        pair = jnp.where(number < total_pairs, pairs_ref[jnp.minimum(number, PAIRS_MAX - 1)], 0)
        first, second = pair >> 3, pair & 7
        return (first, second) if kept_first else (jnp.where(number < total_pairs, second - offset, 0), first)

    def score(number, scores_ref):
        along, place = where(number)
        lhs = kept_ref[pl.ds(pl.multiple_of(along * BLOCK, BLOCK), BLOCK), :]
        bias = [jnp.where(lane == along * GROUPS + q, kept_bias, jnp.zeros_like(kept_bias)) for q in range(GROUPS)]
        lhs = jnp.concatenate([lhs, jnp.concatenate(bias, axis=0)], axis=1)
        rhs = sum_ref[pl.ds(pl.multiple_of(place * BLOCK, BLOCK), BLOCK), :]
        rhs = jnp.concatenate([rhs, ones], axis=1)
        scores = lax.dot_general(lhs, rhs, (((1,), (1,)), ((), ())), preferred_element_type=f32)
        scores_ref[...] = scores
        peak = scores_ref[0:8, :]
        for r in range(8, BLOCK, 8):
            peak = jnp.maximum(peak, scores_ref[r:r + 8, :])
        return jnp.where(number < total_pairs, jnp.max(peak, axis=0, keepdims=True), NEG_START)

    def fold(number, scores_ref, block_max):
        along, place = where(number)
        old_max = acc_max[pl.ds(place, 1), :]
        highest = jnp.maximum(old_max, block_max)
        shift = jnp.broadcast_to(highest, (8, BLOCK))
        partial = jnp.zeros((8, BLOCK), f32)
        for r in range(0, BLOCK, 8):
            partial = partial + jnp.exp2((scores_ref[r:r + 8, :] - shift) * SCALE)
        block_sum = jnp.sum(partial, axis=0, keepdims=True)
        block_sum = jnp.where(number < total_pairs, block_sum, 0.0)
        acc_sum[pl.ds(place, 1), :] = acc_sum[pl.ds(place, 1), :] * jnp.exp2((old_max - highest) * SCALE) + block_sum
        acc_max[pl.ds(place, 1), :] = highest

    def turn(k, even_max):
        odd_max = score(2 * k + 1, odd)
        fold(2 * k, even, even_max)
        even_max = score(2 * k + 2, even)
        fold(2 * k + 1, odd, odd_max)
        return even_max

    lax.fori_loop(0, (total_pairs + 1) >> 1, turn, score(0, even))


def finish(blocks, acc_max, acc_sum, out_ref):
    total = acc_sum[...]
    lse = jnp.where(total > 0, acc_max[...] * SCALE + jnp.log(total) * LOG2E, NEG_START)
    dense = jnp.concatenate(
        [lse[b:b + 1, q * LANES:(q + 1) * LANES] for b in range(blocks) for q in range(GROUPS)], axis=0
    )
    for k in range(out_ref.shape[0]):
        out_ref[k] = dense


def piece_rows(by, first, last, y_ref, pairs_ref, count_ref, sources_ref, piece_ref, potential_ref, *refs):
    if first:
        in_max = in_sum = None
    else:
        in_max, in_sum, *refs = refs
    if last:
        out_ref, acc_max, acc_sum, even, odd, chosen = refs
    else:
        acc_max, acc_sum, even, odd, chosen = refs
    if first:
        clear(acc_max, acc_sum)
    else:
        acc_max[...] = in_max[...]
        acc_sum[...] = in_sum[...]
    block0 = ((y_ref[0, 0] + 4 - by) & 3) * 2
    count = count_ref[0, 0]

    def pick(number, found):
        pair = pairs_ref[0, 0, number]
        chosen[found] = pair
        return found + jnp.where((pair & 6) == block0, 1, 0)

    found = lax.fori_loop(0, count, pick, 0)
    potential = potential_ref[pl.ds(pl.multiple_of(block0 * GROUPS, 8), 8), :]
    bias = 0.5 * (potential - squares(piece_ref[...]))
    sweep(chosen, found, piece_ref, sources_ref, bias, acc_max, acc_sum, even, odd, False, block0)
    if last:
        finish(SB_DEV, acc_max, acc_sum, out_ref)


def copied(pairs_ref, chosen):
    def one(number, carry):
        chosen[number] = pairs_ref[0, 0, number]
        return carry

    lax.fori_loop(0, PAIRS_MAX, one, 0)


def next_rows(pairs_ref, count_ref, sources_ref, targets_ref, parts_ref, out_ref, acc_max, acc_sum, even, odd, chosen):
    bias = half_bias(combined(parts_ref[...]))
    copied(pairs_ref, chosen)
    clear(acc_max, acc_sum)
    sweep(chosen, count_ref[0, 0], targets_ref, sources_ref, bias, acc_max, acc_sum, even, odd, False)
    finish(SB_DEV, acc_max, acc_sum, out_ref)


def first_columns(y_ref, pairs_ref, count_ref, sources_ref, own_ref, by1_ref, by2_ref, by3_ref, parts_ref, out_ref, targets_ref, *scratch):
    rows = own_ref.shape[0]
    for k, ref in enumerate((own_ref, by1_ref, by2_ref, by3_ref)):
        place = (y_ref[0, 0] + 4 - k) & 3
        targets_ref[pl.ds(pl.multiple_of(place * rows, rows), rows), :] = ref[...]
    half_columns(pairs_ref, count_ref, sources_ref, targets_ref, parts_ref, out_ref, *scratch)


def half_columns(pairs_ref, count_ref, sources_ref, targets_ref, parts_ref, out_ref, acc_max, acc_sum, even, odd, chosen):
    bias = half_bias(combined(parts_ref[...]))
    copied(pairs_ref, chosen)
    clear(acc_max, acc_sum)
    sweep(chosen, count_ref[0, 0], sources_ref, targets_ref, bias, acc_max, acc_sum, even, odd, True)
    finish(TB_DEV, acc_max, acc_sum, out_ref)
    return bias


def last_columns(pairs_ref, count_ref, sources_ref, targets_ref, parts_ref, out_ref, potential_ref, *scratch):
    bias = half_columns(pairs_ref, count_ref, sources_ref, targets_ref, parts_ref, out_ref, *scratch)
    potential_ref[...] = squares(sources_ref[...]) + 2.0 * bias


def last_potential(targets_ref, parts_ref, potential_ref):
    potential_ref[...] = squares(targets_ref[...]) + 2.0 * half_bias(combined(parts_ref[...]))


SMEM = pl.BlockSpec(memory_space=pltpu.SMEM)
VMEM = pl.BlockSpec(memory_space=pltpu.VMEM)
PARAMS = pltpu.CompilerParams(vmem_limit_bytes=24 * 1024 * 1024)
STATS = [pltpu.VMEM((8, BLOCK), f32)] * 2
WORK = [pltpu.VMEM((BLOCK, BLOCK), f32)] * 2 + [pltpu.SMEM((PAIRS_MAX,), jnp.int32)]


def spread(parts, axes):
    return lax.all_to_all(parts, axes, 0, 0, tiled=True)


def call(kernel, out_shape, smem, vmem, scratch):
    return pl.pallas_call(
        kernel,
        out_shape=out_shape,
        in_specs=[SMEM] * len(smem) + [VMEM] * len(vmem),
        out_specs=jax.tree.map(lambda _: VMEM, out_shape),
        scratch_shapes=scratch,
        compiler_params=PARAMS,
        cost_estimate=pl.CostEstimate(flops=1 << 30, bytes_accessed=1 << 22, transcendentals=1 << 20),
    )(*smem, *vmem)


def per_device(source_points, target_points, initial_potential, pair_list, pair_count):
    n_src = lax.axis_size(("y", "z"))
    n_tgt = lax.axis_size(("x", "c"))
    n_y, n_z = lax.axis_size("y"), lax.axis_size("z")
    own = target_points.shape[0]
    src_rows = source_points.shape[0] // LANES
    tgt_rows = own * n_src // LANES
    y = lax.axis_index("y").astype(jnp.int32).reshape(1, 1)

    piece = spread(jnp.broadcast_to(target_points[None], (n_z, own, EMB)), "z").reshape(n_z * own, EMB)
    shifted = [
        lax.ppermute(piece, "y", [(i, (i + k) % n_y) for i in range(n_y)]) for k in range(1, n_y)
    ]
    pieces = [piece] + shifted
    potential = initial_potential.reshape(tgt_rows, LANES)
    row_shape = jax.ShapeDtypeStruct((n_tgt, src_rows, LANES), f32)
    col_shape = jax.ShapeDtypeStruct((n_src, tgt_rows, LANES), f32)
    stat = jax.ShapeDtypeStruct((8, BLOCK), f32)
    stats = ()
    order = (0, 1, 3, 2)
    for k in order:
        first, last = k == order[0], k == order[-1]
        got = call(
            functools.partial(piece_rows, k, first, last),
            row_shape if last else [stat, stat],
            (y, pair_list, pair_count),
            (source_points, pieces[k], potential, *stats),
            STATS + WORK if last else WORK,
        )
        stats = got
    row_parts = spread(got, ("x", "c"))
    col_parts, targets = call(
        first_columns,
        [col_shape, jax.ShapeDtypeStruct((tgt_rows * LANES, EMB), bf16)],
        (y, pair_list, pair_count),
        (source_points, *pieces, row_parts),
        STATS + WORK,
    )
    for iteration in range(1, ITERS):
        col_parts = spread(col_parts, ("y", "z"))
        row_parts = call(
            next_rows, row_shape, (pair_list, pair_count), (source_points, targets, col_parts), STATS + WORK
        )
        row_parts = spread(row_parts, ("x", "c"))
        last = iteration == ITERS - 1
        out_shape = [col_shape, jax.ShapeDtypeStruct((src_rows, LANES), f32)]
        got = call(
            last_columns if last else half_columns,
            out_shape if last else col_shape,
            (pair_list, pair_count),
            (source_points, targets, row_parts),
            STATS + WORK,
        )
        col_parts = got[0] if last else got
    source_potential = got[1]
    col_parts = spread(col_parts, ("y", "z"))
    target_potential = call(
        last_potential, jax.ShapeDtypeStruct((tgt_rows, LANES), f32), (), (targets, col_parts), []
    )
    return source_potential.reshape(-1), target_potential.reshape(-1)


def solution(mesh):
    fine = Mesh(mesh.devices.reshape(4, 8, 4, 2), ("y", "z", "x", "c"))
    src, tgt = ("y", "z"), ("x", "c")
    placed = (P(src, None), P(tgt + src, None), P(tgt), P(src, tgt, None), P(src, tgt))
    return jax.shard_map(
        per_device, mesh=fine, in_specs=placed, out_specs=(P(src), P(tgt)), check_vma=False
    )
```

```python
import functools
import math

import jax
import jax.numpy as jnp
from jax import lax
from jax.experimental import pallas as pl
from jax.experimental.pallas import tpu as pltpu
from jax.sharding import Mesh
from jax.sharding import PartitionSpec as P

BLOCK = 512
LANES = 128
EMB = 128
SB_DEV = 2
TB_DEV = 8
PAIRS_MAX = 16
ITERS = 2
NEG_START = -1e30
EPS_REG = 0.2
LOG2E = math.log2(math.e)
SCALE = 2.0 * LOG2E / EPS_REG
GROUPS = BLOCK // LANES
HALF = BLOCK // 2
CHUNK = 32
CHUNKS = BLOCK // CHUNK
LAG = 12
PUSH_AT = 4

bf16 = jnp.bfloat16
f32 = jnp.float32


def squares(points):
    values = points.astype(f32)
    sq = values * values
    high = sq.astype(bf16)
    low = (sq - high.astype(f32)).astype(bf16)
    parts = jnp.concatenate([high, low], axis=1)
    ones = jnp.ones((16, 2 * EMB), bf16)
    groups = points.shape[0] // HALF
    slots = [(g % 2, g // 2 % 2) for g in range(groups)]

    def sums(products):
        for g, (mxu, stage) in enumerate(slots):
            pltpu.matmul_push_rhs(parts[g * HALF:(g + 1) * HALF], stage, mxu, transpose=True)
            pltpu.matmul_acc_lhs(products[g], ones, load_staged_rhs=stage)
        rows = []
        for g in range(groups):
            out = pltpu.matmul_pop(products[g])
            rows += [out[0:1, :LANES], out[0:1, LANES:]]
        return jnp.concatenate(rows, axis=0)

    return pl.run_scoped(sums, [pltpu.ACC(mxu)((16, HALF), f32) for mxu, _ in slots])


def bias_columns(bias):
    high = bias.astype(bf16).astype(f32)
    rest = bias - high
    middle = rest.astype(bf16).astype(f32)
    low = rest - middle
    count = bias.shape[0]
    stacked = jnp.concatenate([high, middle, low, jnp.zeros((LANES - 3 * count, LANES), f32)], axis=0)
    return stacked.T.astype(bf16)


def combined(parts):
    highest = jnp.max(parts, axis=0)
    total = jnp.sum(jnp.exp2(parts - highest[None]), axis=0)
    return highest + jnp.log(total) * LOG2E


def half_bias(lse):
    return (-0.5 * EPS_REG / LOG2E) * (math.log2(32768) + lse)


def clear(acc_max, acc_sum):
    acc_max[...] = jnp.full(acc_max.shape, NEG_START, f32)
    acc_sum[...] = jnp.zeros(acc_sum.shape, f32)


def sweep(*operands):
    products = [[pltpu.ACC(m)((CHUNK, HALF), f32) for _ in range(CHUNKS)] for m in range(2)]
    pl.run_scoped(functools.partial(sweep_with, *operands), products)


def sweep_with(pairs_ref, count, kept_ref, sum_ref, bias, acc_max, acc_sum, even, odd, kept_first, offset, mxus):
    kept_bias = bias_columns(bias)
    lane = lax.broadcasted_iota(jnp.int32, (CHUNK, LANES), 1) & (bias.shape[0] - 1)
    ones = jnp.ones((HALF, LANES), bf16)
    zeros = jnp.zeros((CHUNK, LANES), bf16)
    buffers = (even, odd)

    def where(number):
        real = number < count
        pair = jnp.where(real, pairs_ref[jnp.minimum(number, PAIRS_MAX - 1)], 0)
        first, second = pair >> 3, pair & 7
        return (first, second) if kept_first else (jnp.where(real, second - offset, 0), first)

    def push(number, parity):
        _, place = where(number)
        for m in range(2):
            rows = sum_ref[pl.ds(pl.multiple_of(place * BLOCK + m * HALF, HALF), HALF), :]
            pltpu.matmul_push_rhs(jnp.concatenate([rows, ones], axis=1), parity, m, transpose=True)

    def issue(along, parity, j):
        rows = kept_ref[pl.ds(pl.multiple_of(along * BLOCK + j * CHUNK, CHUNK), CHUNK), :]
        start = j * CHUNK % LANES
        mine = jnp.where(lane == along * GROUPS + j * CHUNK // LANES, kept_bias[start:start + CHUNK], zeros)
        lhs = jnp.concatenate([rows, mine], axis=1)
        for m in range(2):
            pltpu.matmul_acc_lhs(mxus[m][j], lhs, load_staged_rhs=parity if j == 0 else None)

    def take(parity, j, peak):
        for m in range(2):
            out = pltpu.matmul_pop(mxus[m][j])
            buffers[parity][j * CHUNK:(j + 1) * CHUNK, m * HALF:(m + 1) * HALF] = out
            for r in range(0, CHUNK, 8):
                peak[m] = jnp.maximum(peak[m], out[r:r + 8])

    def add(parity, j, shift, partial):
        for r in range(j * CHUNK, (j + 1) * CHUNK, 8):
            partial = partial + jnp.exp2((buffers[parity][r:r + 8, :] - shift) * SCALE)
        return partial

    def settle(number, peak):
        _, place = where(number)
        block_max = jnp.max(jnp.concatenate(peak, axis=1), axis=0, keepdims=True)
        old_max = acc_max[pl.ds(place, 1), :]
        highest = jnp.where(number < count, jnp.maximum(old_max, block_max), old_max)
        acc_max[pl.ds(place, 1), :] = highest
        acc_sum[pl.ds(place, 1), :] = acc_sum[pl.ds(place, 1), :] * jnp.exp2((old_max - highest) * SCALE)
        return jnp.broadcast_to(highest, (8, BLOCK))

    def fold(number, partial):
        _, place = where(number)
        block_sum = jnp.where((number >= 0) & (number < count), jnp.sum(partial, axis=0, keepdims=True), 0.0)
        place = jnp.where(number >= 0, place, 0)
        acc_sum[pl.ds(place, 1), :] = acc_sum[pl.ds(place, 1), :] + block_sum

    lowest = jnp.full((8, HALF), NEG_START, f32)
    nothing = jnp.zeros((8, BLOCK), f32)

    def body(i, parity, carry):
        peak0, peak1, shift, partial = carry
        peak = [peak0, peak1]
        along, _ = where(i + 1)
        for j in range(CHUNKS):
            issue(along, 1 - parity, j)
            if j == PUSH_AT:
                push(i + 2, parity)
            if j < LAG:
                take(parity, j + CHUNKS - LAG, peak)
                partial = add(1 - parity, j + CHUNKS - LAG, shift, partial)
                if j == LAG - 1:
                    fold(i - 1, partial)
                    shift = settle(i, peak)
                    peak = [lowest, lowest]
                    partial = nothing
            else:
                take(1 - parity, j - LAG, peak)
                partial = add(parity, j - LAG, shift, partial)
        return (*peak, shift, partial)

    push(0, 0)
    along, _ = where(0)
    peak = [lowest, lowest]
    for j in range(CHUNKS):
        issue(along, 0, j)
        if j == PUSH_AT:
            push(1, 1)
        if j >= LAG:
            take(0, j - LAG, peak)

    def turn(k, carry):
        return body(2 * k + 1, 1, body(2 * k, 0, carry))

    turns = (count + 1) >> 1
    carry = lax.fori_loop(0, turns, turn, (*peak, nothing, nothing))
    peak0, peak1, shift, partial = carry
    for j in range(LAG):
        take(0, j + CHUNKS - LAG, [peak0, peak1])
        partial = add(1, j + CHUNKS - LAG, shift, partial)
    fold(2 * turns - 1, partial)
    for m in range(2):
        pltpu.matmul_acc_lhs(mxus[m][0], jnp.zeros((CHUNK, 2 * LANES), bf16), load_staged_rhs=1)
        pltpu.matmul_pop(mxus[m][0])


def finish(blocks, acc_max, acc_sum, out_ref):
    total = acc_sum[...]
    lse = jnp.where(total > 0, acc_max[...] * SCALE + jnp.log(total) * LOG2E, NEG_START)
    dense = jnp.concatenate(
        [lse[b:b + 1, q * LANES:(q + 1) * LANES] for b in range(blocks) for q in range(GROUPS)], axis=0
    )
    for k in range(out_ref.shape[0]):
        out_ref[k] = dense


def piece_rows(by, first, last, y_ref, pairs_ref, count_ref, sources_ref, potential_ref, *refs):
    if last:
        low_ref, high_ref, *refs = refs
        *refs, piece_ref = refs
        piece_ref[0:BLOCK, :] = low_ref[...]
        piece_ref[BLOCK:2 * BLOCK, :] = high_ref[...]
    else:
        piece_ref, *refs = refs
    if not first:
        in_max, in_sum, *refs = refs
    squares_ref, *refs = refs
    if first:
        source_squares_ref, *refs = refs
        source_squares_ref[...] = squares(sources_ref[...])
    if last:
        out_ref, *refs = refs
    acc_max, acc_sum, even, odd, chosen = refs
    if first:
        clear(acc_max, acc_sum)
    else:
        acc_max[...] = in_max[...]
        acc_sum[...] = in_sum[...]
    block0 = ((y_ref[0, 0] + 4 - by) & 3) * 2
    count = count_ref[0, 0]

    def pick(number, found):
        pair = pairs_ref[0, 0, number]
        chosen[found] = pair
        return found + jnp.where((pair & 6) == block0, 1, 0)

    found = lax.fori_loop(0, count, pick, 0)
    potential = potential_ref[pl.ds(pl.multiple_of(block0 * GROUPS, 8), 8), :]
    squared = squares(piece_ref[...])
    squares_ref[...] = squared
    bias = 0.5 * (potential - squared)
    sweep(chosen, found, piece_ref, sources_ref, bias, acc_max, acc_sum, even, odd, False, block0)
    if last:
        finish(SB_DEV, acc_max, acc_sum, out_ref)


def copied(pairs_ref, chosen):
    def one(number, carry):
        chosen[number] = pairs_ref[0, 0, number]
        return carry

    lax.fori_loop(0, PAIRS_MAX, one, 0)


def next_rows(pairs_ref, count_ref, sources_ref, targets_ref, parts_ref, out_ref, acc_max, acc_sum, even, odd, chosen):
    bias = half_bias(combined(parts_ref[...]))
    copied(pairs_ref, chosen)
    clear(acc_max, acc_sum)
    sweep(chosen, count_ref[0, 0], targets_ref, sources_ref, bias, acc_max, acc_sum, even, odd, False, 0)
    finish(SB_DEV, acc_max, acc_sum, out_ref)


def first_columns(y_ref, pairs_ref, count_ref, sources_ref, own_ref, by1_ref, low2_ref, high2_ref, by3_ref, parts_ref, out_ref, targets_ref, *scratch):
    def place(by):
        return pl.multiple_of(((y_ref[0, 0] + 4 - by) & 3) * 2 * BLOCK, 2 * BLOCK)

    for by, ref in ((0, own_ref), (1, by1_ref), (3, by3_ref)):
        targets_ref[pl.ds(place(by), 2 * BLOCK), :] = ref[...]
    targets_ref[pl.ds(place(2), BLOCK), :] = low2_ref[...]
    targets_ref[pl.ds(place(2) + BLOCK, BLOCK), :] = high2_ref[...]
    half_columns(pairs_ref, count_ref, sources_ref, targets_ref, parts_ref, out_ref, *scratch)


def half_columns(pairs_ref, count_ref, sources_ref, targets_ref, parts_ref, out_ref, acc_max, acc_sum, even, odd, chosen):
    bias = half_bias(combined(parts_ref[...]))
    copied(pairs_ref, chosen)
    clear(acc_max, acc_sum)
    sweep(chosen, count_ref[0, 0], sources_ref, targets_ref, bias, acc_max, acc_sum, even, odd, True, 0)
    finish(TB_DEV, acc_max, acc_sum, out_ref)


def last_columns(pairs_ref, count_ref, sources_ref, targets_ref, squares_ref, parts_ref, out_ref, potential_ref, *scratch):
    potential_ref[...] = squares_ref[...] + 2.0 * half_bias(combined(parts_ref[...]))
    half_columns(pairs_ref, count_ref, sources_ref, targets_ref, parts_ref, out_ref, *scratch)


def last_potential(y_ref, own_ref, by1_ref, by2_ref, by3_ref, parts_ref, potential_ref):
    potential_ref[...] = 2.0 * half_bias(combined(parts_ref[...]))
    for by, ref in enumerate((own_ref, by1_ref, by2_ref, by3_ref)):
        rows = pl.ds(pl.multiple_of(((y_ref[0, 0] + 4 - by) & 3) * 8, 8), 8)
        potential_ref[rows, :] = potential_ref[rows, :] + ref[...]


SMEM = pl.BlockSpec(memory_space=pltpu.SMEM)
VMEM = pl.BlockSpec(memory_space=pltpu.VMEM)
PARAMS = pltpu.CompilerParams(vmem_limit_bytes=24 * 1024 * 1024)
STATS = [pltpu.VMEM((8, BLOCK), f32)] * 2


def work():
    return [pltpu.VMEM((BLOCK, BLOCK), f32)] * 2 + [pltpu.SMEM((PAIRS_MAX,), jnp.int32)]


def spread(parts, axes):
    return lax.all_to_all(parts, axes, 0, 0, tiled=True)


def call(kernel, out_shape, smem, vmem, scratch):
    return pl.pallas_call(
        kernel,
        out_shape=out_shape,
        in_specs=[SMEM] * len(smem) + [VMEM] * len(vmem),
        out_specs=jax.tree.map(lambda _: VMEM, out_shape),
        scratch_shapes=scratch,
        compiler_params=PARAMS,
        cost_estimate=pl.CostEstimate(flops=1 << 30, bytes_accessed=1 << 22, transcendentals=1 << 20),
    )(*smem, *vmem)


def per_device(source_points, target_points, initial_potential, pair_list, pair_count):
    n_src = lax.axis_size(("y", "z"))
    n_tgt = lax.axis_size(("x", "c"))
    n_y, n_z = lax.axis_size("y"), lax.axis_size("z")
    own = target_points.shape[0]
    src_rows = source_points.shape[0] // LANES
    tgt_rows = own * n_src // LANES
    y = lax.axis_index("y").astype(jnp.int32).reshape(1, 1)

    piece = spread(jnp.broadcast_to(target_points[None], (n_z, own, EMB)), "z").reshape(n_z * own, EMB)

    def along_y(array, by):
        return lax.ppermute(array, "y", [(i, (i + by) % n_y) for i in range(n_y)])

    by1, by3 = along_y(piece, 1), along_y(piece, n_y - 1)
    low2, high2 = along_y(by1[:BLOCK], 1), along_y(by3[BLOCK:], n_y - 1)
    potential = initial_potential.reshape(tgt_rows, LANES)
    row_shape = jax.ShapeDtypeStruct((n_tgt, src_rows, LANES), f32)
    col_shape = jax.ShapeDtypeStruct((n_src, tgt_rows, LANES), f32)
    stat = jax.ShapeDtypeStruct((8, BLOCK), f32)
    square_shape = jax.ShapeDtypeStruct((8, LANES), f32)
    whole_piece = pltpu.VMEM((2 * BLOCK, EMB), bf16)
    target_squares = {}
    lists = (y, pair_list, pair_count)
    target_squares[0], source_squares, *stats = call(
        functools.partial(piece_rows, 0, True, False),
        [square_shape, square_shape, stat, stat],
        lists,
        (source_points, potential, piece),
        work(),
    )
    for by, array in ((1, by1), (3, by3)):
        target_squares[by], *stats = call(
            functools.partial(piece_rows, by, False, False),
            [square_shape, stat, stat],
            lists,
            (source_points, potential, array, *stats),
            work(),
        )
    target_squares[2], row_parts = call(
        functools.partial(piece_rows, 2, False, True),
        [square_shape, row_shape],
        lists,
        (source_points, potential, low2, high2, *stats),
        STATS + work() + [whole_piece],
    )
    row_parts = spread(row_parts, ("x", "c"))
    col_parts, targets = call(
        first_columns,
        [col_shape, jax.ShapeDtypeStruct((tgt_rows * LANES, EMB), bf16)],
        lists,
        (source_points, piece, by1, low2, high2, by3, row_parts),
        STATS + work(),
    )
    for iteration in range(1, ITERS):
        col_parts = spread(col_parts, ("y", "z"))
        row_parts = call(
            next_rows, row_shape, (pair_list, pair_count), (source_points, targets, col_parts), STATS + work()
        )
        row_parts = spread(row_parts, ("x", "c"))
        if iteration < ITERS - 1:
            col_parts = call(
                half_columns, col_shape, (pair_list, pair_count), (source_points, targets, row_parts), STATS + work()
            )
        else:
            col_parts, source_potential = call(
                last_columns,
                [col_shape, square_shape],
                (pair_list, pair_count),
                (source_points, targets, source_squares, row_parts),
                STATS + work(),
            )
    col_parts = spread(col_parts, ("y", "z"))
    target_potential = call(
        last_potential,
        jax.ShapeDtypeStruct((tgt_rows, LANES), f32),
        (y,),
        (*(target_squares[by] for by in range(4)), col_parts),
        [],
    )
    return source_potential.reshape(-1), target_potential.reshape(-1)


def solution(mesh):
    fine = Mesh(mesh.devices.reshape(4, 8, 4, 2), ("y", "z", "x", "c"))
    src, tgt = ("y", "z"), ("x", "c")
    placed = (P(src, None), P(tgt + src, None), P(tgt), P(src, tgt, None), P(src, tgt))
    return jax.shard_map(
        per_device, mesh=fine, in_specs=placed, out_specs=(P(src), P(tgt)), check_vma=False
    )
```

```python
import functools
import math

import jax
import jax.numpy as jnp
from jax import lax
from jax.experimental import pallas as pl
from jax.experimental.pallas import tpu as pltpu
from jax.sharding import Mesh
from jax.sharding import PartitionSpec as P

BLOCK = 512
LANES = 128
EMB = 128
SRC_BLOCKS = 8
TGT_BLOCKS = 2
PAIRS_MAX = 16
ITERS = 2
NEG_START = -1e30
EPS_REG = 0.2
LOG2E = math.log2(math.e)
SCALE = 2.0 * LOG2E / EPS_REG
GROUPS = BLOCK // LANES
HALF = BLOCK // 2
CHUNK = 32
CHUNKS = BLOCK // CHUNK
LAG = 12
PUSH_AT = 4

bf16 = jnp.bfloat16
f32 = jnp.float32


def squares(points):
    values = points.astype(f32)
    sq = values * values
    high = sq.astype(bf16)
    low = (sq - high.astype(f32)).astype(bf16)
    parts = jnp.concatenate([high, low], axis=1)
    ones = jnp.ones((16, 2 * EMB), bf16)
    groups = points.shape[0] // HALF
    slots = [(g % 2, g // 2 % 2) for g in range(groups)]

    def sums(products):
        for g, (mxu, stage) in enumerate(slots):
            pltpu.matmul_push_rhs(parts[g * HALF:(g + 1) * HALF], stage, mxu, transpose=True)
            pltpu.matmul_acc_lhs(products[g], ones, load_staged_rhs=stage)
        rows = []
        for g in range(groups):
            out = pltpu.matmul_pop(products[g])
            rows += [out[0:1, :LANES], out[0:1, LANES:]]
        return jnp.concatenate(rows, axis=0)

    return pl.run_scoped(sums, [pltpu.ACC(mxu)((16, HALF), f32) for mxu, _ in slots])


def bias_columns(bias):
    high = bias.astype(bf16).astype(f32)
    rest = bias - high
    middle = rest.astype(bf16).astype(f32)
    low = rest - middle
    count = bias.shape[0]
    stacked = jnp.concatenate([high, middle, low, jnp.zeros((LANES - 3 * count, LANES), f32)], axis=0)
    return stacked.T.astype(bf16)


def combined(parts):
    highest = jnp.max(parts, axis=0)
    total = jnp.sum(jnp.exp2(parts - highest[None]), axis=0)
    return highest + jnp.log(total) * LOG2E


def half_bias(lse):
    return (-0.5 * EPS_REG / LOG2E) * (math.log2(32768) + lse)


def clear(acc_max, acc_sum):
    acc_max[...] = jnp.full(acc_max.shape, NEG_START, f32)
    acc_sum[...] = jnp.zeros(acc_sum.shape, f32)


def sweep(*operands):
    products = [[pltpu.ACC(m)((CHUNK, HALF), f32) for _ in range(CHUNKS)] for m in range(2)]
    pl.run_scoped(functools.partial(sweep_with, *operands), products)


def sweep_with(pairs_ref, count, kept_ref, sum_ref, bias, acc_max, acc_sum, even, odd, kept_first, mxus):
    kept_bias = bias_columns(bias)
    lane = lax.broadcasted_iota(jnp.int32, (CHUNK, LANES), 1) & (bias.shape[0] - 1)
    ones = jnp.ones((HALF, LANES), bf16)
    zeros = jnp.zeros((CHUNK, LANES), bf16)
    buffers = (even, odd)

    def where(number):
        real = number < count
        pair = jnp.where(real, pairs_ref[jnp.minimum(number, PAIRS_MAX - 1)], 0)
        first, second = pair >> 1, pair & 1
        return (first, second) if kept_first else (second, first)

    def push(number, parity):
        _, place = where(number)
        for m in range(2):
            rows = sum_ref[pl.ds(pl.multiple_of(place * BLOCK + m * HALF, HALF), HALF), :]
            pltpu.matmul_push_rhs(jnp.concatenate([rows, ones], axis=1), parity, m, transpose=True)

    def issue(along, parity, j):
        rows = kept_ref[pl.ds(pl.multiple_of(along * BLOCK + j * CHUNK, CHUNK), CHUNK), :]
        start = j * CHUNK % LANES
        mine = jnp.where(lane == along * GROUPS + j * CHUNK // LANES, kept_bias[start:start + CHUNK], zeros)
        lhs = jnp.concatenate([rows, mine], axis=1)
        for m in range(2):
            pltpu.matmul_acc_lhs(mxus[m][j], lhs, load_staged_rhs=parity if j == 0 else None)

    def take(parity, j, peak):
        for m in range(2):
            out = pltpu.matmul_pop(mxus[m][j])
            buffers[parity][j * CHUNK:(j + 1) * CHUNK, m * HALF:(m + 1) * HALF] = out
            for r in range(0, CHUNK, 8):
                peak[m] = jnp.maximum(peak[m], out[r:r + 8])

    def add(parity, j, shift, partial):
        for r in range(j * CHUNK, (j + 1) * CHUNK, 8):
            partial = partial + jnp.exp2((buffers[parity][r:r + 8, :] - shift) * SCALE)
        return partial

    def settle(number, peak):
        _, place = where(number)
        block_max = jnp.max(jnp.concatenate(peak, axis=1), axis=0, keepdims=True)
        old_max = acc_max[pl.ds(place, 1), :]
        highest = jnp.where(number < count, jnp.maximum(old_max, block_max), old_max)
        acc_max[pl.ds(place, 1), :] = highest
        acc_sum[pl.ds(place, 1), :] = acc_sum[pl.ds(place, 1), :] * jnp.exp2((old_max - highest) * SCALE)
        return jnp.broadcast_to(highest, (8, BLOCK))

    def fold(number, partial):
        _, place = where(number)
        block_sum = jnp.where((number >= 0) & (number < count), jnp.sum(partial, axis=0, keepdims=True), 0.0)
        place = jnp.where(number >= 0, place, 0)
        acc_sum[pl.ds(place, 1), :] = acc_sum[pl.ds(place, 1), :] + block_sum

    lowest = jnp.full((8, HALF), NEG_START, f32)
    nothing = jnp.zeros((8, BLOCK), f32)

    def body(i, parity, carry):
        peak0, peak1, shift, partial = carry
        peak = [peak0, peak1]
        along, _ = where(i + 1)
        for j in range(CHUNKS):
            issue(along, 1 - parity, j)
            if j == PUSH_AT:
                push(i + 2, parity)
            if j < LAG:
                take(parity, j + CHUNKS - LAG, peak)
                partial = add(1 - parity, j + CHUNKS - LAG, shift, partial)
                if j == LAG - 1:
                    fold(i - 1, partial)
                    shift = settle(i, peak)
                    peak = [lowest, lowest]
                    partial = nothing
            else:
                take(1 - parity, j - LAG, peak)
                partial = add(parity, j - LAG, shift, partial)
        return (*peak, shift, partial)

    push(0, 0)
    along, _ = where(0)
    peak = [lowest, lowest]
    for j in range(CHUNKS):
        issue(along, 0, j)
        if j == PUSH_AT:
            push(1, 1)
        if j >= LAG:
            take(0, j - LAG, peak)

    def turn(k, carry):
        return body(2 * k + 1, 1, body(2 * k, 0, carry))

    turns = (count + 1) >> 1
    carry = lax.fori_loop(0, turns, turn, (*peak, nothing, nothing))
    peak0, peak1, shift, partial = carry
    for j in range(LAG):
        take(0, j + CHUNKS - LAG, [peak0, peak1])
        partial = add(1, j + CHUNKS - LAG, shift, partial)
    fold(2 * turns - 1, partial)
    for m in range(2):
        pltpu.matmul_acc_lhs(mxus[m][0], jnp.zeros((CHUNK, 2 * LANES), bf16), load_staged_rhs=1)
        pltpu.matmul_pop(mxus[m][0])


def finish(blocks, acc_max, acc_sum, out_ref, offset):
    total = acc_sum[...]
    lse = jnp.where(total > 0, acc_max[...] * SCALE + jnp.log(total) * LOG2E, NEG_START)
    dense = jnp.concatenate(
        [lse[b:b + 1, q * LANES:(q + 1) * LANES] for b in range(blocks) for q in range(GROUPS)], axis=0
    )
    if offset is not None:
        dense = dense + offset
    for k in range(out_ref.shape[0]):
        out_ref[k] = dense


def bits(list_row, y_from, y):
    pair = list_row.astype(jnp.int32)
    number = y_from * 4 + ((pair >> 3) << 1) + (pair & 1)
    mine = (pair >= 0) & (((pair >> 1) & 3) == y)
    return jnp.where(mine, jnp.left_shift(jnp.ones_like(number), jnp.where(mine, number, 0)), 0).astype(f32)


def first_rows(y_ref, own_ref, by1_ref, by2_ref, by3_ref, targets_ref, potential_ref, out_ref, sources_ref, source_squares_ref, target_squares_ref, pairs_ref, *scratch):
    y = y_ref[0, 0]
    rows = targets_ref.shape[0]
    kept = jnp.zeros((1, LANES), f32)
    for by, ref in enumerate((own_ref, by1_ref, by2_ref, by3_ref)):
        y_from = (y + 4 - by) & 3
        kept = kept + bits(ref[rows:rows + 16, :].astype(f32)[0:1, :], y_from, y)
        sources_ref[pl.ds(pl.multiple_of(y_from * rows, rows), rows), :] = ref[0:rows, :]
    kept = jnp.sum(kept).astype(jnp.int32)

    def pick(number, found):
        pairs_ref[found] = number
        return found + ((kept >> number) & 1)

    found = lax.fori_loop(0, PAIRS_MAX, pick, 0)
    pairs_ref[PAIRS_MAX] = found
    source_squares_ref[...] = squares(own_ref[0:rows, :])
    squared = squares(targets_ref[...])
    target_squares_ref[...] = squared
    potential = potential_ref[pl.ds(pl.multiple_of(y * 8, 8), 8), :]
    bias = 0.5 * (potential - squared)
    half_step(pairs_ref, targets_ref, sources_ref, bias, False, out_ref, *scratch)


def half_step(pairs_ref, kept_ref, sum_ref, bias, kept_first, out_ref, acc_max, acc_sum, even, odd, offset=None):
    clear(acc_max, acc_sum)
    sweep(pairs_ref, pairs_ref[PAIRS_MAX], kept_ref, sum_ref, bias, acc_max, acc_sum, even, odd, kept_first)
    finish(sum_ref.shape[0] // BLOCK, acc_max, acc_sum, out_ref, offset)


def next_rows(pairs_ref, sources_ref, targets_ref, parts_ref, out_ref, *scratch):
    bias = half_bias(combined(parts_ref[...]))
    half_step(pairs_ref, targets_ref, sources_ref, bias, False, out_ref, *scratch)


def next_columns(pairs_ref, sources_ref, targets_ref, parts_ref, out_ref, *scratch):
    bias = half_bias(combined(parts_ref[...]))
    half_step(pairs_ref, sources_ref, targets_ref, bias, True, out_ref, *scratch)


def last_columns(pairs_ref, y_ref, sources_ref, targets_ref, source_squares_ref, target_squares_ref, parts_ref, out_ref, potential_ref, all_bias, *scratch):
    bias = half_bias(combined(parts_ref[...]))
    all_bias[...] = bias
    own = all_bias[pl.ds(pl.multiple_of(y_ref[0, 0] * 8, 8), 8), :]
    potential_ref[...] = source_squares_ref[...] + 2.0 * own
    offset = target_squares_ref[...] * (-LOG2E / EPS_REG)
    half_step(pairs_ref, sources_ref, targets_ref, bias, True, out_ref, *scratch, offset)


def last_potential(parts_ref, potential_ref):
    count = parts_ref.shape[0] // 4
    for y in range(4):
        lse = combined(parts_ref[y * count:(y + 1) * count])
        potential_ref[y * 8:(y + 1) * 8, :] = 2.0 * half_bias(lse)


SMEM = pl.BlockSpec(memory_space=pltpu.SMEM)
VMEM = pl.BlockSpec(memory_space=pltpu.VMEM)
PARAMS = pltpu.CompilerParams(vmem_limit_bytes=24 * 1024 * 1024)
WORK = [pltpu.VMEM((8, BLOCK), f32)] * 2 + [pltpu.VMEM((BLOCK, BLOCK), f32)] * 2


def spread(parts, axes):
    return lax.all_to_all(parts, axes, 0, 0, tiled=True)


def call(kernel, out_shape, smem, vmem, scratch, smem_outs=0):
    out_specs = jax.tree.map(lambda _: VMEM, out_shape)
    if smem_outs:
        out_specs = out_specs[:-smem_outs] + [SMEM] * smem_outs
    return pl.pallas_call(
        kernel,
        out_shape=out_shape,
        in_specs=[SMEM] * len(smem) + [VMEM] * len(vmem),
        out_specs=out_specs,
        scratch_shapes=scratch,
        compiler_params=PARAMS,
        cost_estimate=pl.CostEstimate(flops=1 << 30, bytes_accessed=1 << 22, transcendentals=1 << 20),
    )(*smem, *vmem)


def per_device(source_points, target_points, initial_potential, pair_list, pair_count):
    n_y, n_z = lax.axis_size("y"), lax.axis_size("z")
    n_rows = lax.axis_size(("x", "c", "y"))
    own = target_points.shape[0]
    src_rows = source_points.shape[0] // LANES
    tgt_rows = n_z * own // LANES
    y = lax.axis_index("y").astype(jnp.int32).reshape(1, 1)

    listed = jnp.pad(pair_list.reshape(1, PAIRS_MAX).astype(bf16), ((0, 15), (0, LANES - PAIRS_MAX)), constant_values=-1)
    sources = jnp.concatenate([source_points, listed], axis=0)
    by = [
        lax.ppermute(sources, "y", [(i, (i + k) % n_y) for i in range(n_y)]) for k in range(1, n_y)
    ]
    targets = spread(jnp.broadcast_to(target_points[None], (n_z, own, EMB)), "z").reshape(n_z * own, EMB)
    potential = initial_potential.reshape(n_y * tgt_rows, LANES)

    def shape(*dims):
        return jax.ShapeDtypeStruct(dims, f32)

    row_shape = shape(n_rows, n_y * src_rows, LANES)
    row_parts, sources, source_squares, target_squares, pairs = call(
        first_rows,
        [
            row_shape,
            jax.ShapeDtypeStruct((n_y * src_rows * LANES, EMB), bf16),
            shape(src_rows, LANES),
            shape(tgt_rows, LANES),
            jax.ShapeDtypeStruct((2 * PAIRS_MAX,), jnp.int32),
        ],
        (y,),
        (sources, *by, targets, potential),
        WORK,
        1,
    )
    for iteration in range(ITERS):
        if iteration > 0:
            row_parts = call(next_rows, row_shape, (pairs,), (sources, targets, col_parts), WORK)
        row_parts = spread(row_parts, ("x", "c", "y"))
        if iteration < ITERS - 1:
            col_parts = call(next_columns, shape(n_z, tgt_rows, LANES), (pairs,), (sources, targets, row_parts), WORK)
            col_parts = spread(col_parts, "z")
        else:
            col_parts, source_potential = call(
                last_columns,
                [shape(n_y * n_z, tgt_rows, LANES), shape(src_rows, LANES)],
                (pairs, y),
                (sources, targets, source_squares, target_squares, row_parts),
                [pltpu.VMEM((n_y * src_rows, LANES), f32)] + WORK,
            )
            col_parts = spread(col_parts, ("y", "z"))
    target_potential = call(last_potential, shape(n_y * tgt_rows, LANES), (), (col_parts,), [])
    return source_potential.reshape(-1), target_potential.reshape(-1)


def solution(mesh):
    fine = Mesh(mesh.devices.reshape(4, 8, 4, 2), ("y", "z", "x", "c"))
    src, tgt = ("y", "z"), ("x", "c")
    placed = (P(src, None), P(tgt + src, None), P(tgt), P(src, tgt, None), P(src, tgt))
    return jax.shard_map(
        per_device, mesh=fine, in_specs=placed, out_specs=(P(src), P(tgt)), check_vma=False
    )
```

```python
import functools
import math

import jax
import jax.numpy as jnp
from jax import lax
from jax.experimental import pallas as pl
from jax.experimental.pallas import tpu as pltpu
from jax.sharding import Mesh
from jax.sharding import PartitionSpec as P

BLOCK = 512
LANES = 128
EMB = 128
PAIRS_MAX = 16
ITERS = 2
NEG_START = -1e30
EPS_REG = 0.2
LOG2E = math.log2(math.e)
SCALE = 2.0 * LOG2E / EPS_REG
GROUPS = BLOCK // LANES
HALF = BLOCK // 2
CHUNK = 32
CHUNKS = BLOCK // CHUNK
LAG = 12
PUSH_AT = 4

bf16 = jnp.bfloat16
f32 = jnp.float32


def squares(points):
    values = points.astype(f32)
    sq = values * values
    high = sq.astype(bf16)
    low = (sq - high.astype(f32)).astype(bf16)
    parts = jnp.concatenate([high, low], axis=1)
    ones = jnp.ones((16, 2 * EMB), bf16)
    groups = points.shape[0] // HALF
    slots = [(g % 2, g // 2 % 2) for g in range(groups)]

    def sums(products):
        for g, (mxu, stage) in enumerate(slots):
            pltpu.matmul_push_rhs(parts[g * HALF:(g + 1) * HALF], stage, mxu, transpose=True)
            pltpu.matmul_acc_lhs(products[g], ones, load_staged_rhs=stage)
        rows = []
        for g in range(groups):
            out = pltpu.matmul_pop(products[g])
            rows += [out[0:1, :LANES], out[0:1, LANES:]]
        return jnp.concatenate(rows, axis=0)

    return pl.run_scoped(sums, [pltpu.ACC(mxu)((16, HALF), f32) for mxu, _ in slots])


def bias_columns(bias):
    high = bias.astype(bf16).astype(f32)
    rest = bias - high
    middle = rest.astype(bf16).astype(f32)
    low = rest - middle
    count = bias.shape[0]
    stacked = jnp.concatenate([high, middle, low, jnp.zeros((LANES - 3 * count, LANES), f32)], axis=0)
    return stacked.T.astype(bf16)


def combined(parts):
    highest = jnp.max(parts, axis=0)
    total = jnp.sum(jnp.exp2(parts - highest[None]), axis=0)
    return highest + jnp.log(total) * LOG2E


def half_bias(lse):
    return (-0.5 * EPS_REG / LOG2E) * (math.log2(32768) + lse)


def clear(acc_max, acc_sum):
    acc_max[...] = jnp.full(acc_max.shape, NEG_START, f32)
    acc_sum[...] = jnp.zeros(acc_sum.shape, f32)


def sweep(*operands):
    products = [[pltpu.ACC(m)((CHUNK, HALF), f32) for _ in range(CHUNKS)] for m in range(2)]
    pl.run_scoped(functools.partial(sweep_with, *operands), products)


def sweep_with(pairs_ref, count, kept_ref, sum_ref, bias, acc_max, acc_sum, even, odd, kept_first, mxus):
    kept_bias = bias_columns(bias)
    lane = lax.broadcasted_iota(jnp.int32, (CHUNK, LANES), 1) & (bias.shape[0] - 1)
    ones = jnp.ones((HALF, LANES), bf16)
    zeros = jnp.zeros((CHUNK, LANES), bf16)
    buffers = (even, odd)

    def where(number):
        real = number < count
        pair = jnp.where(real, pairs_ref[jnp.minimum(number, PAIRS_MAX - 1)], 0)
        first, second = pair >> 2, pair & 3
        return (first, second) if kept_first else (second, first)

    def push(number, parity):
        _, place = where(number)
        for m in range(2):
            rows = sum_ref[pl.ds(pl.multiple_of(place * BLOCK + m * HALF, HALF), HALF), :]
            pltpu.matmul_push_rhs(jnp.concatenate([rows, ones], axis=1), parity, m, transpose=True)

    def issue(along, parity, j):
        rows = kept_ref[pl.ds(pl.multiple_of(along * BLOCK + j * CHUNK, CHUNK), CHUNK), :]
        start = j * CHUNK % LANES
        mine = jnp.where(lane == along * GROUPS + j * CHUNK // LANES, kept_bias[start:start + CHUNK], zeros)
        lhs = jnp.concatenate([rows, mine], axis=1)
        for m in range(2):
            pltpu.matmul_acc_lhs(mxus[m][j], lhs, load_staged_rhs=parity if j == 0 else None)

    def take(parity, j, peak):
        for m in range(2):
            out = pltpu.matmul_pop(mxus[m][j])
            buffers[parity][j * CHUNK:(j + 1) * CHUNK, m * HALF:(m + 1) * HALF] = out
            for r in range(0, CHUNK, 8):
                peak[m] = jnp.maximum(peak[m], out[r:r + 8])

    def add(parity, j, shift, partial):
        for r in range(j * CHUNK, (j + 1) * CHUNK, 8):
            partial = partial + jnp.exp2((buffers[parity][r:r + 8, :] - shift) * SCALE)
        return partial

    def settle(number, peak):
        _, place = where(number)
        block_max = jnp.max(jnp.concatenate(peak, axis=1), axis=0, keepdims=True)
        old_max = acc_max[pl.ds(place, 1), :]
        highest = jnp.where(number < count, jnp.maximum(old_max, block_max), old_max)
        acc_max[pl.ds(place, 1), :] = highest
        acc_sum[pl.ds(place, 1), :] = acc_sum[pl.ds(place, 1), :] * jnp.exp2((old_max - highest) * SCALE)
        return jnp.broadcast_to(highest, (8, BLOCK))

    def fold(number, partial):
        _, place = where(number)
        block_sum = jnp.where((number >= 0) & (number < count), jnp.sum(partial, axis=0, keepdims=True), 0.0)
        place = jnp.where(number >= 0, place, 0)
        acc_sum[pl.ds(place, 1), :] = acc_sum[pl.ds(place, 1), :] + block_sum

    lowest = jnp.full((8, HALF), NEG_START, f32)
    nothing = jnp.zeros((8, BLOCK), f32)

    def body(i, parity, carry):
        peak0, peak1, shift, partial = carry
        peak = [peak0, peak1]
        along, _ = where(i + 1)
        for j in range(CHUNKS):
            issue(along, 1 - parity, j)
            if j == PUSH_AT:
                push(i + 2, parity)
            if j < LAG:
                take(parity, j + CHUNKS - LAG, peak)
                partial = add(1 - parity, j + CHUNKS - LAG, shift, partial)
                if j == LAG - 1:
                    fold(i - 1, partial)
                    shift = settle(i, peak)
                    peak = [lowest, lowest]
                    partial = nothing
            else:
                take(1 - parity, j - LAG, peak)
                partial = add(parity, j - LAG, shift, partial)
        return (*peak, shift, partial)

    push(0, 0)
    along, _ = where(0)
    peak = [lowest, lowest]
    for j in range(CHUNKS):
        issue(along, 0, j)
        if j == PUSH_AT:
            push(1, 1)
        if j >= LAG:
            take(0, j - LAG, peak)

    def turn(k, carry):
        return body(2 * k + 1, 1, body(2 * k, 0, carry))

    turns = (count + 1) >> 1
    carry = lax.fori_loop(0, turns, turn, (*peak, nothing, nothing))
    peak0, peak1, shift, partial = carry
    for j in range(LAG):
        take(0, j + CHUNKS - LAG, [peak0, peak1])
        partial = add(1, j + CHUNKS - LAG, shift, partial)
    fold(2 * turns - 1, partial)
    for m in range(2):
        pltpu.matmul_acc_lhs(mxus[m][0], jnp.zeros((CHUNK, 2 * LANES), bf16), load_staged_rhs=1)
        pltpu.matmul_pop(mxus[m][0])


def finished(acc_max, acc_sum):
    total = acc_sum[...]
    lse = jnp.where(total > 0, acc_max[...] * SCALE + jnp.log(total) * LOG2E, NEG_START)
    return jnp.concatenate([lse[b:b + 1, q * LANES:(q + 1) * LANES] for b in range(4) for q in range(GROUPS)], axis=0)


def bits(list_row, y_from, c_from, y, c):
    pair = list_row.astype(jnp.int32)
    number = y_from * 4 + c_from * 2 + (pair & 1)
    mine = (pair >> 3 == c) & (((pair >> 1) & 3) == y)
    return jnp.where(mine, jnp.left_shift(jnp.ones_like(pair), number), 0).astype(f32)


def first_rows(place_ref, own_ref, by1_ref, by2_ref, by3_ref, targets_ref, shared_ref, out_ref, sources_ref, source_squares_ref, target_squares_ref, pairs_ref, *scratch):
    y, c = place_ref[0], place_ref[1]
    kept = jnp.zeros((1, LANES), f32)
    for by, ref in enumerate((own_ref, by1_ref, by2_ref, by3_ref)):
        y_from = (y + 4 - by) & 3
        lists = ref[BLOCK:BLOCK + 16, :].astype(f32)
        for c_from in range(2):
            kept = kept + bits(lists[c_from:c_from + 1, :], y_from, c_from, y, c)
        sources_ref[pl.ds(pl.multiple_of(y_from * BLOCK, BLOCK), BLOCK), :] = ref[0:BLOCK, :]
    kept = jnp.sum(kept).astype(jnp.int32)

    def pick(number, found):
        pairs_ref[found] = number
        return found + ((kept >> number) & 1)

    found = lax.fori_loop(0, PAIRS_MAX, pick, 0)
    pairs_ref[PAIRS_MAX] = found
    source_squares_ref[...] = squares(own_ref[0:BLOCK, :])
    squared = squares(targets_ref[...])
    target_squares_ref[...] = squared
    rows = pl.ds(pl.multiple_of(y * 8, 8), 8)
    potential = jnp.concatenate([shared_ref[0, rows, :], shared_ref[1, rows, :]], axis=0)
    bias = 0.5 * (potential - squared)
    half_step(pairs_ref, targets_ref, sources_ref, bias, False, *scratch)
    spread_out(out_ref, scratch)


def half_step(pairs_ref, kept_ref, sum_ref, bias, kept_first, acc_max, acc_sum, even, odd):
    clear(acc_max, acc_sum)
    sweep(pairs_ref, pairs_ref[PAIRS_MAX], kept_ref, sum_ref, bias, acc_max, acc_sum, even, odd, kept_first)


def spread_out(out_ref, scratch):
    dense = finished(scratch[0], scratch[1])
    for k in range(out_ref.shape[0]):
        out_ref[k] = dense


def next_rows(pairs_ref, sources_ref, targets_ref, parts_ref, out_ref, *scratch):
    bias = half_bias(combined(parts_ref[...]))
    half_step(pairs_ref, targets_ref, sources_ref, bias, False, *scratch)
    spread_out(out_ref, scratch)


def next_columns(pairs_ref, sources_ref, targets_ref, parts_ref, out_ref, *scratch):
    bias = half_bias(combined(parts_ref[...]))
    half_step(pairs_ref, sources_ref, targets_ref, bias, True, *scratch)
    spread_out(out_ref, scratch)


def last_columns(pairs_ref, place_ref, sources_ref, targets_ref, source_squares_ref, target_squares_ref, parts_ref, out_ref, all_bias, *scratch):
    bias = half_bias(combined(parts_ref[...]))
    all_bias[...] = bias
    half_step(pairs_ref, sources_ref, targets_ref, bias, True, *scratch)
    out_ref[0:16, :] = finished(scratch[0], scratch[1]) - target_squares_ref[...] * (LOG2E / EPS_REG)
    own = all_bias[pl.ds(place_ref[0] * GROUPS, GROUPS), :]
    out_ref[16:16 + GROUPS, :] = source_squares_ref[...] + 2.0 * own
    out_ref[16 + GROUPS:24, :] = jnp.zeros((8 - GROUPS, LANES), f32)


def both_cores(place_ref, parts_ref, out_ref, potential_ref):
    rows = pl.ds(pl.multiple_of(place_ref[1] * 8, 8), 8)
    lse = combined(jnp.stack([parts_ref[0, rows, :], parts_ref[1, rows, :]]))
    for k in range(out_ref.shape[0]):
        out_ref[k] = lse
    for b in range(2):
        potential_ref[b * GROUPS:(b + 1) * GROUPS, :] = parts_ref[b, 16:16 + GROUPS, :]


def last_potential(parts_ref, potential_ref):
    count = parts_ref.shape[0] // 4
    for y in range(4):
        lse = combined(parts_ref[y * count:(y + 1) * count])
        potential_ref[y * 8:(y + 1) * 8, :] = 2.0 * half_bias(lse)


SMEM = pl.BlockSpec(memory_space=pltpu.SMEM)
VMEM = pl.BlockSpec(memory_space=pltpu.VMEM)
PARAMS = pltpu.CompilerParams(vmem_limit_bytes=24 * 1024 * 1024)
WORK = [pltpu.VMEM((8, BLOCK), f32)] * 2 + [pltpu.VMEM((BLOCK, BLOCK), f32)] * 2


def spread(parts, axes):
    return lax.all_to_all(parts, axes, 0, 0, tiled=True)


def call(kernel, out_shape, smem, vmem, scratch, smem_outs=0):
    out_specs = jax.tree.map(lambda _: VMEM, out_shape)
    if smem_outs:
        out_specs = out_specs[:-smem_outs] + [SMEM] * smem_outs
    return pl.pallas_call(
        kernel,
        out_shape=out_shape,
        in_specs=[SMEM] * len(smem) + [VMEM] * len(vmem),
        out_specs=out_specs,
        scratch_shapes=scratch,
        compiler_params=PARAMS,
        cost_estimate=pl.CostEstimate(flops=1 << 30, bytes_accessed=1 << 22, transcendentals=1 << 20),
    )(*smem, *vmem)


def per_device(source_points, target_points, initial_potential, pair_list, pair_count):
    n_y, n_z = lax.axis_size("y"), lax.axis_size("z")
    own = target_points.shape[0]
    tgt_rows = n_z * own // LANES
    y, c = lax.axis_index("y"), lax.axis_index("c")
    place = jnp.stack([y, c]).astype(jnp.int32)

    def shape(*dims):
        return jax.ShapeDtypeStruct(dims, f32)

    listed = jnp.pad(pair_list.reshape(1, PAIRS_MAX).astype(f32), ((0, 7), (0, LANES - PAIRS_MAX)), constant_values=-1)
    shared = jnp.concatenate([initial_potential.reshape(n_y * tgt_rows, LANES), listed], axis=0)
    shared = lax.all_gather(shared, "c")
    lists = jnp.pad(shared[:, n_y * tgt_rows, :].astype(bf16), ((0, 14), (0, 0)), constant_values=-1)
    sources = jnp.concatenate([lax.dynamic_slice_in_dim(source_points, c * BLOCK, BLOCK, 0), lists], axis=0)
    by = [
        lax.ppermute(sources, "y", [(i, (i + k) % n_y) for i in range(n_y)]) for k in range(1, n_y)
    ]
    targets = spread(jnp.broadcast_to(target_points[None], (n_z, own, EMB)), "z").reshape(n_z * own, EMB)
    targets = lax.all_gather(targets, "c", axis=0, tiled=True)
    row_shape = shape(16, 16, LANES)
    row_parts, sources, source_squares, target_squares, pairs = call(
        first_rows,
        [
            row_shape,
            jax.ShapeDtypeStruct((n_y * BLOCK, EMB), bf16),
            shape(GROUPS, LANES),
            shape(2 * tgt_rows, LANES),
            jax.ShapeDtypeStruct((2 * PAIRS_MAX,), jnp.int32),
        ],
        (place,),
        (sources, *by, targets, shared),
        WORK,
        1,
    )
    for iteration in range(ITERS):
        if iteration > 0:
            row_parts = call(next_rows, row_shape, (pairs,), (sources, targets, col_parts), WORK)
        row_parts = spread(row_parts, ("y", "x"))
        if iteration < ITERS - 1:
            col_parts = call(next_columns, row_shape, (pairs,), (sources, targets, row_parts), WORK)
            col_parts = spread(col_parts, ("z", "c"))
    parts = call(
        last_columns,
        shape(24, LANES),
        (pairs, place),
        (sources, targets, source_squares, target_squares, row_parts),
        [pltpu.VMEM((16, LANES), f32)] + WORK,
    )
    col_parts, source_potential = call(
        both_cores,
        [shape(n_y * n_z, tgt_rows, LANES), shape(2 * GROUPS, LANES)],
        (place,),
        (lax.all_gather(parts, "c"),),
        [],
    )
    col_parts = spread(col_parts, ("y", "z"))
    target_potential = call(last_potential, shape(n_y * tgt_rows, LANES), (), (col_parts,), [])
    return source_potential.reshape(-1), target_potential.reshape(-1)


def solution(mesh):
    fine = Mesh(mesh.devices.reshape(4, 8, 4, 2), ("y", "z", "x", "c"))
    src, tgt = ("y", "z"), ("x", "c")
    placed = (P(src, None), P(tgt + src, None), P(tgt), P(src, tgt, None), P(src, tgt))
    return jax.shard_map(
        per_device, mesh=fine, in_specs=placed, out_specs=(P(src), P(tgt)), check_vma=False
    )
```

```python
import functools
import math

import jax
import jax.numpy as jnp
from jax import lax
from jax.experimental import pallas as pl
from jax.experimental.pallas import tpu as pltpu
from jax.sharding import Mesh
from jax.sharding import PartitionSpec as P

BLOCK = 512
LANES = 128
EMB = 128
PAIRS_MAX = 16
ITERS = 2
NEG_START = -1e30
EPS_REG = 0.2
LOG2E = math.log2(math.e)
SCALE = 2.0 * LOG2E / EPS_REG
GROUPS = BLOCK // LANES
HALF = BLOCK // 2
CHUNK = 32
CHUNKS = BLOCK // CHUNK
LAG = 12
PUSH_AT = 4

bf16 = jnp.bfloat16
f32 = jnp.float32


def squares(points):
    values = points.astype(f32)
    sq = values * values
    high = sq.astype(bf16)
    low = (sq - high.astype(f32)).astype(bf16)
    parts = jnp.concatenate([high, low], axis=1)
    ones = jnp.ones((16, 2 * EMB), bf16)
    groups = points.shape[0] // HALF
    slots = [(g % 2, g // 2 % 2) for g in range(groups)]

    def sums(products):
        for g, (mxu, stage) in enumerate(slots):
            pltpu.matmul_push_rhs(parts[g * HALF:(g + 1) * HALF], stage, mxu, transpose=True)
            pltpu.matmul_acc_lhs(products[g], ones, load_staged_rhs=stage)
        rows = []
        for g in range(groups):
            out = pltpu.matmul_pop(products[g])
            rows += [out[0:1, :LANES], out[0:1, LANES:]]
        return jnp.concatenate(rows, axis=0)

    return pl.run_scoped(sums, [pltpu.ACC(mxu)((16, HALF), f32) for mxu, _ in slots])


def bias_columns(bias):
    high = bias.astype(bf16).astype(f32)
    rest = bias - high
    middle = rest.astype(bf16).astype(f32)
    low = rest - middle
    count = bias.shape[0]
    stacked = jnp.concatenate([high, middle, low, jnp.zeros((LANES - 3 * count, LANES), f32)], axis=0)
    return stacked.T.astype(bf16)


def combined(parts):
    highest = jnp.max(parts, axis=0)
    total = jnp.sum(jnp.exp2(parts - highest[None]), axis=0)
    return highest + jnp.log(total) * LOG2E


def half_bias(lse):
    return (-0.5 * EPS_REG / LOG2E) * (math.log2(32768) + lse)


def clear(acc_max, acc_sum):
    acc_max[...] = jnp.full(acc_max.shape, NEG_START, f32)
    acc_sum[...] = jnp.zeros(acc_sum.shape, f32)


def sweep(*operands):
    products = [[pltpu.ACC(m)((CHUNK, HALF), f32) for _ in range(CHUNKS)] for m in range(2)]
    pl.run_scoped(functools.partial(sweep_with, *operands), products)


def sweep_with(pairs_ref, count, kept_ref, sum_ref, bias, acc_max, acc_sum, even, odd, kept_first, mxus):
    kept_bias = bias_columns(bias)
    lane = lax.broadcasted_iota(jnp.int32, (CHUNK, LANES), 1) & (bias.shape[0] - 1)
    ones = jnp.ones((HALF, LANES), bf16)
    zeros = jnp.zeros((CHUNK, LANES), bf16)
    buffers = (even, odd)

    def where(number):
        real = number < count
        pair = jnp.where(real, pairs_ref[jnp.minimum(number, PAIRS_MAX - 1)], 0)
        first, second = pair >> 2, pair & 3
        return (first, second) if kept_first else (second, first)

    def push(number, parity):
        _, place = where(number)
        for m in range(2):
            rows = sum_ref[pl.ds(pl.multiple_of(place * BLOCK + m * HALF, HALF), HALF), :]
            pltpu.matmul_push_rhs(jnp.concatenate([rows, ones], axis=1), parity, m, transpose=True)

    def issue(along, parity, j):
        rows = kept_ref[pl.ds(pl.multiple_of(along * BLOCK + j * CHUNK, CHUNK), CHUNK), :]
        start = j * CHUNK % LANES
        mine = jnp.where(lane == along * GROUPS + j * CHUNK // LANES, kept_bias[start:start + CHUNK], zeros)
        lhs = jnp.concatenate([rows, mine], axis=1)
        for m in range(2):
            pltpu.matmul_acc_lhs(mxus[m][j], lhs, load_staged_rhs=parity if j == 0 else None)

    def take(parity, j, peak):
        for m in range(2):
            out = pltpu.matmul_pop(mxus[m][j])
            buffers[parity][j * CHUNK:(j + 1) * CHUNK, m * HALF:(m + 1) * HALF] = out
            for r in range(0, CHUNK, 8):
                peak[m] = jnp.maximum(peak[m], out[r:r + 8])

    def add(parity, j, shift, partial):
        for r in range(j * CHUNK, (j + 1) * CHUNK, 8):
            partial = partial + jnp.exp2((buffers[parity][r:r + 8, :] - shift) * SCALE)
        return partial

    def settle(number, peak):
        _, place = where(number)
        block_max = jnp.max(jnp.concatenate(peak, axis=1), axis=0, keepdims=True)
        old_max = acc_max[pl.ds(place, 1), :]
        highest = jnp.where(number < count, jnp.maximum(old_max, block_max), old_max)
        acc_max[pl.ds(place, 1), :] = highest
        acc_sum[pl.ds(place, 1), :] = acc_sum[pl.ds(place, 1), :] * jnp.exp2((old_max - highest) * SCALE)
        return jnp.broadcast_to(highest, (8, BLOCK))

    def fold(number, partial):
        _, place = where(number)
        block_sum = jnp.where((number >= 0) & (number < count), jnp.sum(partial, axis=0, keepdims=True), 0.0)
        place = jnp.where(number >= 0, place, 0)
        acc_sum[pl.ds(place, 1), :] = acc_sum[pl.ds(place, 1), :] + block_sum

    lowest = jnp.full((8, HALF), NEG_START, f32)
    nothing = jnp.zeros((8, BLOCK), f32)

    def body(i, parity, carry):
        peak0, peak1, shift, partial = carry
        peak = [peak0, peak1]
        along, _ = where(i + 1)
        for j in range(CHUNKS):
            issue(along, 1 - parity, j)
            if j == PUSH_AT:
                push(i + 2, parity)
            if j < LAG:
                take(parity, j + CHUNKS - LAG, peak)
                partial = add(1 - parity, j + CHUNKS - LAG, shift, partial)
                if j == LAG - 1:
                    fold(i - 1, partial)
                    shift = settle(i, peak)
                    peak = [lowest, lowest]
                    partial = nothing
            else:
                take(1 - parity, j - LAG, peak)
                partial = add(parity, j - LAG, shift, partial)
        return (*peak, shift, partial)

    push(0, 0)
    along, _ = where(0)
    peak = [lowest, lowest]
    for j in range(CHUNKS):
        issue(along, 0, j)
        if j == PUSH_AT:
            push(1, 1)
        if j >= LAG:
            take(0, j - LAG, peak)

    def turn(k, carry):
        return body(2 * k + 1, 1, body(2 * k, 0, carry))

    turns = (count + 1) >> 1
    carry = lax.fori_loop(0, turns, turn, (*peak, nothing, nothing))
    peak0, peak1, shift, partial = carry
    for j in range(LAG):
        take(0, j + CHUNKS - LAG, [peak0, peak1])
        partial = add(1, j + CHUNKS - LAG, shift, partial)
    fold(2 * turns - 1, partial)
    for m in range(2):
        pltpu.matmul_acc_lhs(mxus[m][0], jnp.zeros((CHUNK, 2 * LANES), bf16), load_staged_rhs=1)
        pltpu.matmul_pop(mxus[m][0])


def finished(acc_max, acc_sum):
    total = acc_sum[...]
    lse = jnp.where(total > 0, acc_max[...] * SCALE + jnp.log(total) * LOG2E, NEG_START)
    return jnp.concatenate([lse[b:b + 1, q * LANES:(q + 1) * LANES] for b in range(4) for q in range(GROUPS)], axis=0)


def bits(list_row, y_from, c_from, y, c):
    pair = list_row.astype(jnp.int32)
    number = y_from * 4 + c_from * 2 + (pair & 1)
    mine = (pair >> 3 == c) & (((pair >> 1) & 3) == y)
    return jnp.where(mine, jnp.left_shift(jnp.ones_like(pair), number), 0).astype(f32)


def first_rows(own_ref, by1_ref, by2_ref, by3_ref, shared_ref, potential_ref, out_ref, sources_ref, targets_ref, source_squares_ref, target_squares_ref, kept_ref, *scratch):
    y, c = lax.axis_index("y"), lax.axis_index("c")
    kept = jnp.zeros((1, LANES), f32)
    points = 2 * BLOCK
    for c_from in range(2):
        lists = shared_ref[c_from, points:points + 16, :].astype(f32)
        for by in range(4):
            kept = kept + bits(lists[by:by + 1, :], (y + 4 - by) & 3, c_from, y, c)
        targets_ref[c_from * points:(c_from + 1) * points, :] = shared_ref[c_from, 0:points, :]
    kept_ref[...] = jnp.broadcast_to(kept, kept_ref.shape)
    for by, ref in enumerate((own_ref, by1_ref, by2_ref, by3_ref)):
        sources_ref[pl.ds(pl.multiple_of(((y + 4 - by) & 3) * BLOCK, BLOCK), BLOCK), :] = ref[0:BLOCK, :]
    source_squares_ref[...] = squares(own_ref[0:BLOCK, :])
    squared = squares(targets_ref[...])
    target_squares_ref[...] = squared
    rows = pl.ds(pl.multiple_of(y * 8, 8), 8)
    potential = jnp.concatenate([potential_ref[0, rows, :], potential_ref[1, rows, :]], axis=0)
    bias = 0.5 * (potential - squared)
    half_step(kept_ref, targets_ref, sources_ref, bias, False, *scratch)
    spread_out(out_ref, scratch)


def half_step(kept_pairs_ref, kept_ref, sum_ref, bias, kept_first, acc_max, acc_sum, even, odd, chosen):
    clear(acc_max, acc_sum)
    kept = jnp.sum(kept_pairs_ref[0:1, :]).astype(jnp.int32)
    found = jnp.int32(0)
    for number in range(PAIRS_MAX):
        chosen[found] = number
        found = found + ((kept >> number) & 1)
    sweep(chosen, found, kept_ref, sum_ref, bias, acc_max, acc_sum, even, odd, kept_first)


def spread_out(out_ref, scratch):
    dense = finished(scratch[0], scratch[1])
    for k in range(out_ref.shape[0]):
        out_ref[k] = dense


def next_rows(kept_ref, sources_ref, targets_ref, parts_ref, out_ref, *scratch):
    bias = half_bias(combined(parts_ref[...]))
    half_step(kept_ref, targets_ref, sources_ref, bias, False, *scratch)
    spread_out(out_ref, scratch)


def next_columns(kept_ref, sources_ref, targets_ref, parts_ref, out_ref, *scratch):
    bias = half_bias(combined(parts_ref[...]))
    half_step(kept_ref, sources_ref, targets_ref, bias, True, *scratch)
    spread_out(out_ref, scratch)


def last_columns(kept_ref, sources_ref, targets_ref, source_squares_ref, target_squares_ref, parts_ref, out_ref, all_bias, *scratch):
    bias = half_bias(combined(parts_ref[...]))
    all_bias[...] = bias
    own = all_bias[pl.ds(lax.axis_index("y") * GROUPS, GROUPS), :]
    out_ref[16:16 + GROUPS, :] = source_squares_ref[...] + 2.0 * own
    out_ref[16 + GROUPS:24, :] = jnp.zeros((8 - GROUPS, LANES), f32)
    half_step(kept_ref, sources_ref, targets_ref, bias, True, *scratch)
    out_ref[0:16, :] = finished(scratch[0], scratch[1]) - target_squares_ref[...] * (LOG2E / EPS_REG)


def both_cores(parts_ref, out_ref):
    rows = pl.ds(pl.multiple_of(lax.axis_index("c") * 8, 8), 8)
    lse = combined(jnp.stack([parts_ref[0, rows, :], parts_ref[1, rows, :]]))
    for k in range(out_ref.shape[0]):
        out_ref[k] = lse


def last_potentials(parts_ref, cores_ref, source_ref, target_ref):
    for b in range(2):
        source_ref[b * GROUPS:(b + 1) * GROUPS, :] = cores_ref[b, 16:16 + GROUPS, :]
    count = parts_ref.shape[0] // 4
    for y in range(4):
        lse = combined(parts_ref[y * count:(y + 1) * count])
        target_ref[y * 8:(y + 1) * 8, :] = 2.0 * half_bias(lse)


VMEM = pl.BlockSpec(memory_space=pltpu.VMEM)
PARAMS = pltpu.CompilerParams(vmem_limit_bytes=24 * 1024 * 1024)
WORK = [pltpu.VMEM((8, BLOCK), f32)] * 2 + [pltpu.VMEM((BLOCK, BLOCK), f32)] * 2 + [pltpu.SMEM((PAIRS_MAX,), jnp.int32)]


def spread(parts, axes):
    return lax.all_to_all(parts, axes, 0, 0, tiled=True)


def call(kernel, out_shape, operands, scratch):
    return pl.pallas_call(
        kernel,
        out_shape=out_shape,
        in_specs=[VMEM] * len(operands),
        out_specs=jax.tree.map(lambda _: VMEM, out_shape),
        scratch_shapes=scratch,
        compiler_params=PARAMS,
        cost_estimate=pl.CostEstimate(flops=1 << 30, bytes_accessed=1 << 22, transcendentals=1 << 20),
    )(*operands)


def per_device(source_points, target_points, initial_potential, pair_list, pair_count):
    n_y, n_z = lax.axis_size("y"), lax.axis_size("z")
    own = target_points.shape[0]
    tgt_rows = n_z * own // LANES
    c = lax.axis_index("c")

    def shape(*dims):
        return jax.ShapeDtypeStruct(dims, f32)

    def points(*dims):
        return jax.ShapeDtypeStruct(dims, bf16)

    listed = jnp.pad(pair_list.reshape(1, PAIRS_MAX).astype(bf16), ((0, 15), (0, LANES - PAIRS_MAX)), constant_values=-1)
    sources = jnp.concatenate([lax.dynamic_slice_in_dim(source_points, c * BLOCK, BLOCK, 0), listed], axis=0)
    by = [
        lax.ppermute(sources, "y", [(i, (i + k) % n_y) for i in range(n_y)]) for k in range(1, n_y)
    ]
    targets = spread(jnp.broadcast_to(target_points[None], (n_z, own, EMB)), "z").reshape(n_z * own, EMB)
    lists = [part[BLOCK:BLOCK + 1] for part in (sources, *by)]
    targets = jnp.concatenate([targets, *lists, listed[4:]], axis=0)
    targets = lax.all_gather(targets, "c")
    potential = lax.all_gather(initial_potential.reshape(n_y * tgt_rows, LANES), "c")
    row_shape = shape(16, 16, LANES)
    row_parts, sources, targets, source_squares, target_squares, kept = call(
        first_rows,
        [
            row_shape,
            points(n_y * BLOCK, EMB),
            points(2 * n_z * own, EMB),
            shape(GROUPS, LANES),
            shape(2 * tgt_rows, LANES),
            shape(8, LANES),
        ],
        (sources, *by, targets, potential),
        WORK,
    )
    for iteration in range(ITERS):
        if iteration > 0:
            row_parts = call(next_rows, row_shape, (kept, sources, targets, col_parts), WORK)
        row_parts = spread(row_parts, ("y", "x"))
        if iteration < ITERS - 1:
            col_parts = call(next_columns, row_shape, (kept, sources, targets, row_parts), WORK)
            col_parts = spread(col_parts, ("z", "c"))
    parts = call(
        last_columns,
        shape(24, LANES),
        (kept, sources, targets, source_squares, target_squares, row_parts),
        [pltpu.VMEM((16, LANES), f32)] + WORK,
    )
    parts = lax.all_gather(parts, "c")
    col_parts = call(both_cores, shape(n_y * n_z, tgt_rows, LANES), (parts,), [])
    col_parts = spread(col_parts, ("y", "z"))
    source_potential, target_potential = call(
        last_potentials, [shape(2 * GROUPS, LANES), shape(n_y * tgt_rows, LANES)], (col_parts, parts), []
    )
    return source_potential.reshape(-1), target_potential.reshape(-1)


def solution(mesh):
    fine = Mesh(mesh.devices.reshape(4, 8, 4, 2), ("y", "z", "x", "c"))
    src, tgt = ("y", "z"), ("x", "c")
    placed = (P(src, None), P(tgt + src, None), P(tgt), P(src, tgt, None), P(src, tgt))
    return jax.shard_map(
        per_device, mesh=fine, in_specs=placed, out_specs=(P(src), P(tgt)), check_vma=False
    )
```

```python
import functools
import math

import jax
import jax.numpy as jnp
from jax import lax
from jax.experimental import pallas as pl
from jax.experimental.pallas import tpu as pltpu
from jax.sharding import Mesh
from jax.sharding import PartitionSpec as P

BLOCK = 512
LANES = 128
EMB = 128
PAIRS_MAX = 16
NEG_START = -1e30
EPS_REG = 0.2
LOG2E = math.log2(math.e)
LOG2_N = math.log2(32768)
SMALLEST = 2.0 ** -85
WIDEST = 85.0
SCALE = 2.0 * LOG2E / EPS_REG
GROUPS = BLOCK // LANES
HALF = BLOCK // 2
CHUNK = 32
CHUNKS = BLOCK // CHUNK
LAG = 12
PUSH_AT = 4

bf16 = jnp.bfloat16
f32 = jnp.float32


def lane_sums(terms):
    ones = jnp.ones((16, 2 * EMB), bf16)
    groups = terms[0].shape[0] // HALF

    def sums(products):
        for k in range(0, len(terms), 2):
            parts = jnp.concatenate(terms[k:k + 2], axis=1)
            for g in range(groups):
                stage = g // 2 % 2
                pltpu.matmul_push_rhs(parts[g * HALF:(g + 1) * HALF], stage, g % 2, transpose=True)
                pltpu.matmul_acc_lhs(products[g], ones, load_staged_rhs=stage)
        rows = []
        for g in range(groups):
            out = pltpu.matmul_pop(products[g])
            rows += [out[0:1, :LANES], out[0:1, LANES:]]
        return jnp.concatenate(rows, axis=0)

    return pl.run_scoped(sums, [pltpu.ACC(g % 2)((16, HALF), f32) for g in range(groups)])


def squares(points):
    values = points.astype(f32)
    sq = values * values
    high = sq.astype(bf16)
    return lane_sums([high, (sq - high.astype(f32)).astype(bf16)])


def bias_columns(bias):
    high = bias.astype(bf16).astype(f32)
    rest = bias - high
    middle = rest.astype(bf16).astype(f32)
    low = rest - middle
    count = bias.shape[0]
    stacked = jnp.concatenate([high, middle, low, jnp.zeros((LANES - 3 * count, LANES), f32)], axis=0)
    return stacked.T.astype(bf16)


def combined(parts):
    highest = jnp.max(parts, axis=0)
    total = jnp.sum(jnp.exp2(parts - highest[None]), axis=0)
    return highest + jnp.log(total) * LOG2E


def half_bias(lse):
    return (-0.5 * EPS_REG / LOG2E) * (LOG2_N + lse)


def clear(acc_max, acc_sum):
    acc_max[...] = jnp.full(acc_max.shape, NEG_START, f32)
    acc_sum[...] = jnp.zeros(acc_sum.shape, f32)


def sweep(*operands):
    products = [[pltpu.ACC(m)((CHUNK, HALF), f32) for _ in range(CHUNKS)] for m in range(2)]
    pl.run_scoped(functools.partial(sweep_with, *operands), products)


def sweep_with(pairs_ref, count, kept_ref, sum_ref, bias, acc_max, acc_sum, even, odd, kept_first, saved, mxus):
    kept_bias = bias_columns(bias)
    lane = lax.broadcasted_iota(jnp.int32, (CHUNK, LANES), 1) & (bias.shape[0] - 1)
    ones = jnp.ones((HALF, LANES), bf16)
    zeros = jnp.zeros((CHUNK, LANES), bf16)
    buffers = (even, odd)

    def where(number):
        real = number < count
        pair = jnp.where(real, pairs_ref[jnp.minimum(number, PAIRS_MAX - 1)], 0)
        first, second = pair >> 2, pair & 3
        return (first, second) if kept_first else (second, first)

    def push(number, parity):
        _, place = where(number)
        for m in range(2):
            rows = sum_ref[pl.ds(pl.multiple_of(place * BLOCK + m * HALF, HALF), HALF), :]
            pltpu.matmul_push_rhs(jnp.concatenate([rows, ones], axis=1), parity, m, transpose=True)

    def issue(along, parity, j):
        rows = kept_ref[pl.ds(pl.multiple_of(along * BLOCK + j * CHUNK, CHUNK), CHUNK), :]
        start = j * CHUNK % LANES
        mine = jnp.where(lane == along * GROUPS + j * CHUNK // LANES, kept_bias[start:start + CHUNK], zeros)
        lhs = jnp.concatenate([rows, mine], axis=1)
        for m in range(2):
            pltpu.matmul_acc_lhs(mxus[m][j], lhs, load_staged_rhs=parity if j == 0 else None)

    def take(parity, j, peak):
        for m in range(2):
            out = pltpu.matmul_pop(mxus[m][j])
            buffers[parity][j * CHUNK:(j + 1) * CHUNK, m * HALF:(m + 1) * HALF] = out
            for r in range(0, CHUNK, 8):
                peak[m] = jnp.maximum(peak[m], out[r:r + 8])

    def add(number, parity, j, shift, partial):
        for r in range(j * CHUNK, (j + 1) * CHUNK, 8):
            terms = jnp.exp2((buffers[parity][r:r + 8, :] - shift) * SCALE)
            partial = partial + terms
            if saved is not None:
                saved[0][jnp.maximum(number, 0), r:r + 8, :] = terms
        return partial

    def settle(number, peak):
        _, place = where(number)
        block_max = jnp.max(jnp.concatenate(peak, axis=1), axis=0, keepdims=True)
        old_max = acc_max[pl.ds(place, 1), :]
        highest = jnp.where(number < count, jnp.maximum(old_max, block_max), old_max)
        acc_max[pl.ds(place, 1), :] = highest
        if saved is not None:
            saved[1][pl.ds(number, 1), :] = highest
        acc_sum[pl.ds(place, 1), :] = acc_sum[pl.ds(place, 1), :] * jnp.exp2((old_max - highest) * SCALE)
        return jnp.broadcast_to(highest, (8, BLOCK))

    def fold(number, partial):
        _, place = where(number)
        block_sum = jnp.where((number >= 0) & (number < count), jnp.sum(partial, axis=0, keepdims=True), 0.0)
        place = jnp.where(number >= 0, place, 0)
        acc_sum[pl.ds(place, 1), :] = acc_sum[pl.ds(place, 1), :] + block_sum

    lowest = jnp.full((8, HALF), NEG_START, f32)
    nothing = jnp.zeros((8, BLOCK), f32)

    def body(i, parity, carry):
        peak0, peak1, shift, partial = carry
        peak = [peak0, peak1]
        along, _ = where(i + 1)
        for j in range(CHUNKS):
            issue(along, 1 - parity, j)
            if j == PUSH_AT:
                push(i + 2, parity)
            if j < LAG:
                take(parity, j + CHUNKS - LAG, peak)
                partial = add(i - 1, 1 - parity, j + CHUNKS - LAG, shift, partial)
                if j == LAG - 1:
                    fold(i - 1, partial)
                    shift = settle(i, peak)
                    peak = [lowest, lowest]
                    partial = nothing
            else:
                take(1 - parity, j - LAG, peak)
                partial = add(i, parity, j - LAG, shift, partial)
        return (*peak, shift, partial)

    push(0, 0)
    along, _ = where(0)
    peak = [lowest, lowest]
    for j in range(CHUNKS):
        issue(along, 0, j)
        if j == PUSH_AT:
            push(1, 1)
        if j >= LAG:
            take(0, j - LAG, peak)

    def turn(k, carry):
        return body(2 * k + 1, 1, body(2 * k, 0, carry))

    turns = (count + 1) >> 1
    carry = lax.fori_loop(0, turns, turn, (*peak, nothing, nothing))
    peak0, peak1, shift, partial = carry
    for j in range(LAG):
        take(0, j + CHUNKS - LAG, [peak0, peak1])
        partial = add(2 * turns - 1, 1, j + CHUNKS - LAG, shift, partial)
    fold(2 * turns - 1, partial)
    for m in range(2):
        pltpu.matmul_acc_lhs(mxus[m][0], jnp.zeros((CHUNK, 2 * LANES), bf16), load_staged_rhs=1)
        pltpu.matmul_pop(mxus[m][0])


def finished(acc_max, acc_sum):
    total = acc_sum[...]
    lse = jnp.where(total > 0, acc_max[...] * SCALE + jnp.log(total) * LOG2E, NEG_START)
    return jnp.concatenate([lse[b:b + 1, q * LANES:(q + 1) * LANES] for b in range(4) for q in range(GROUPS)], axis=0)


def bits(list_row, y_from, c_from, y, c):
    pair = list_row.astype(jnp.int32)
    number = y_from * 4 + c_from * 2 + (pair & 1)
    mine = (pair >> 3 == c) & (((pair >> 1) & 3) == y)
    return jnp.where(mine, jnp.left_shift(jnp.ones_like(pair), number), 0).astype(f32)


def first_rows(own_ref, by1_ref, by2_ref, by3_ref, targets_ref, shared_ref, out_ref, sources_ref, source_squares_ref, target_squares_ref, kept_ref, *scratch):
    y, c = lax.axis_index("y"), lax.axis_index("c")
    kept = jnp.zeros((1, LANES), f32)
    for c_from in range(2):
        lists = shared_ref[c_from, 32:40, :]
        for by in range(4):
            kept = kept + bits(lists[by:by + 1, :], (y + 4 - by) & 3, c_from, y, c)
    kept_ref[...] = jnp.broadcast_to(kept, kept_ref.shape)
    for by, ref in enumerate((own_ref, by1_ref, by2_ref, by3_ref)):
        sources_ref[pl.ds(pl.multiple_of(((y + 4 - by) & 3) * BLOCK, BLOCK), BLOCK), :] = ref[0:BLOCK, :]
    source_squares_ref[...] = squares(own_ref[0:BLOCK, :])
    squared = squares(targets_ref[...])
    target_squares_ref[...] = squared
    rows = pl.ds(pl.multiple_of(y * 8, 8), 8)
    potential = jnp.concatenate([shared_ref[0, rows, :], shared_ref[1, rows, :]], axis=0)
    bias = 0.5 * (potential - squared)
    half_step(kept_ref, targets_ref, sources_ref, bias, False, *scratch)
    spread_out(out_ref, scratch)


def kept_pairs(kept_pairs_ref, chosen):
    kept = jnp.sum(kept_pairs_ref[0:1, :]).astype(jnp.int32)
    found = jnp.int32(0)
    for number in range(PAIRS_MAX):
        chosen[found] = number
        found = found + ((kept >> number) & 1)
    return kept, found


def half_step(kept_pairs_ref, kept_ref, sum_ref, bias, kept_first, acc_max, acc_sum, even, odd, chosen, saved=None):
    clear(acc_max, acc_sum)
    _, found = kept_pairs(kept_pairs_ref, chosen)
    sweep(chosen, found, kept_ref, sum_ref, bias, acc_max, acc_sum, even, odd, kept_first, saved)


def spread_out(out_ref, scratch):
    dense = finished(scratch[0], scratch[1])
    for k in range(out_ref.shape[0]):
        out_ref[k] = dense


def next_columns(kept_ref, sources_ref, targets_ref, parts_ref, out_ref, bias_ref, terms_ref, maxima_ref, *scratch):
    bias = half_bias(combined(parts_ref[...]))
    bias_ref[...] = bias
    half_step(kept_ref, sources_ref, targets_ref, bias, True, *scratch, (terms_ref, maxima_ref))
    spread_out(out_ref, scratch)


def in_kept_blocks(kept):
    block = lax.broadcasted_iota(jnp.int32, (16, LANES), 0) >> 2
    inside = jnp.zeros((16, LANES), jnp.int32)
    for b in range(4):
        inside = jnp.where(block == b, (kept >> (4 * b)) & 15, inside)
    return inside > 0


def any_of(condition):
    return jnp.max(jnp.where(condition, 1.0, 0.0)) > 0.5


def next_rows(kept_ref, sources_ref, targets_ref, old_bias_ref, terms_ref, maxima_ref, parts_ref, out_ref, acc_max, acc_sum, even, odd, chosen, rows_ref, lse_ref):
    lse = combined(parts_ref[...])
    kept, found = kept_pairs(kept_ref, chosen)
    for b in range(4):
        lse_ref[b:b + 1, :] = jnp.concatenate([lse[4 * b + q:4 * b + q + 1, :] for q in range(GROUPS)], axis=1)
    rows_ref[...] = jnp.zeros(rows_ref.shape, f32)

    def one(n, carry):
        pair = chosen[n]
        first, second = pair >> 2, pair & 3
        weight = jnp.exp2(maxima_ref[pl.ds(n, 1), :] * SCALE - lse_ref[pl.ds(second, 1), :])
        weight = jnp.broadcast_to(weight, (8, BLOCK))
        for r in range(0, BLOCK, 8):
            scaled = terms_ref[n, r:r + 8, :] * weight
            total = (scaled[:, 0:LANES] + scaled[:, LANES:2 * LANES]) + (scaled[:, 2 * LANES:3 * LANES] + scaled[:, 3 * LANES:])
            place = pl.ds(pl.multiple_of(first * BLOCK + r, 8), 8)
            rows_ref[place, :] = rows_ref[place, :] + total
        return carry

    lax.fori_loop(0, found, one, 0)
    total = rows_ref[...]
    high = total.astype(bf16)
    rest = total - high.astype(f32)
    middle = rest.astype(bf16)
    low = (rest - middle.astype(f32)).astype(bf16)
    sums = lane_sums([high, middle, low, jnp.zeros_like(low)])
    inside = in_kept_blocks(kept)
    bad = any_of(inside & (sums < SMALLEST))
    safe = jnp.where(inside, sums, 1.0)
    dense = jnp.where(inside, jnp.log(safe) * LOG2E - SCALE * old_bias_ref[...] - LOG2_N, NEG_START)

    @pl.when(jnp.logical_not(bad))
    def _():
        for k in range(out_ref.shape[0]):
            out_ref[k] = dense

    @pl.when(bad)
    def _():
        half_step(kept_ref, targets_ref, sources_ref, half_bias(lse), False, acc_max, acc_sum, even, odd, chosen)
        spread_out(out_ref, (acc_max, acc_sum))


def last_columns(kept_ref, sources_ref, targets_ref, source_squares_ref, target_squares_ref, old_bias_ref, terms_ref, maxima_ref, parts_ref, out_ref, all_bias, acc_max, acc_sum, even, odd, chosen, ratio_ref):
    bias = half_bias(combined(parts_ref[...]))
    all_bias[...] = bias
    own = all_bias[pl.ds(lax.axis_index("y") * GROUPS, GROUPS), :]
    out_ref[16:16 + GROUPS, :] = source_squares_ref[...] + 2.0 * own
    out_ref[16 + GROUPS:24, :] = jnp.zeros((8 - GROUPS, LANES), f32)
    offset = target_squares_ref[...] * (LOG2E / EPS_REG)
    kept, found = kept_pairs(kept_ref, chosen)
    inside = in_kept_blocks(kept)
    moved = SCALE * (bias - old_bias_ref[...])
    largest = jnp.max(jnp.where(inside, moved, NEG_START))
    bad = any_of(inside & (moved < largest - WIDEST))
    ratio = jnp.exp2(jnp.where(inside, moved - largest, 0.0))

    @pl.when(jnp.logical_not(bad))
    def _():
        for k in range(16):
            ratio_ref[k * LANES:(k + 1) * LANES, :] = jnp.broadcast_to(ratio[k:k + 1, :], (LANES, LANES)).T
        clear(acc_max, acc_sum)

        def one(n, carry):
            pair = chosen[n]
            first, second = pair >> 2, pair & 3
            partial = [jnp.zeros((8, BLOCK), f32), jnp.zeros((8, BLOCK), f32)]
            for r in range(0, BLOCK, 8):
                factor = ratio_ref[pl.ds(pl.multiple_of(first * BLOCK + r, 8), 8), :]
                partial[r // 8 % 2] = partial[r // 8 % 2] + terms_ref[n, r:r + 8, :] * jnp.concatenate([factor] * GROUPS, axis=1)
            block_sum = jnp.sum(partial[0] + partial[1], axis=0, keepdims=True)
            highest = maxima_ref[pl.ds(n, 1), :]
            old = jnp.exp2((acc_max[pl.ds(second, 1), :] - highest) * SCALE)
            acc_sum[pl.ds(second, 1), :] = acc_sum[pl.ds(second, 1), :] * old + block_sum
            acc_max[pl.ds(second, 1), :] = highest
            return carry

        lax.fori_loop(0, found, one, 0)
        out_ref[0:16, :] = finished(acc_max, acc_sum) + largest - offset

    @pl.when(bad)
    def _():
        half_step(kept_ref, sources_ref, targets_ref, bias, True, acc_max, acc_sum, even, odd, chosen)
        out_ref[0:16, :] = finished(acc_max, acc_sum) - offset


def both_cores(parts_ref, out_ref):
    rows = pl.ds(pl.multiple_of(lax.axis_index("c") * 8, 8), 8)
    lse = combined(jnp.stack([parts_ref[0, rows, :], parts_ref[1, rows, :]]))
    for k in range(out_ref.shape[0]):
        out_ref[k] = lse


def last_potentials(parts_ref, cores_ref, source_ref, target_ref):
    for b in range(2):
        source_ref[b * GROUPS:(b + 1) * GROUPS, :] = cores_ref[b, 16:16 + GROUPS, :]
    count = parts_ref.shape[0] // 4
    for y in range(4):
        lse = combined(parts_ref[y * count:(y + 1) * count])
        target_ref[y * 8:(y + 1) * 8, :] = 2.0 * half_bias(lse)


VMEM = pl.BlockSpec(memory_space=pltpu.VMEM)
PARAMS = pltpu.CompilerParams(vmem_limit_bytes=8 * 1024 * 1024)
WORK = [pltpu.VMEM((8, BLOCK), f32)] * 2 + [pltpu.VMEM((BLOCK, BLOCK), f32)] * 2 + [pltpu.SMEM((PAIRS_MAX,), jnp.int32)]


def spread(parts, axes):
    return lax.all_to_all(parts, axes, 0, 0, tiled=True)


def call(kernel, out_shape, operands, scratch):
    return pl.pallas_call(
        kernel,
        out_shape=out_shape,
        in_specs=[VMEM] * len(operands),
        out_specs=jax.tree.map(lambda _: VMEM, out_shape),
        scratch_shapes=scratch,
        compiler_params=PARAMS,
        cost_estimate=pl.CostEstimate(flops=1 << 30, bytes_accessed=1 << 22, transcendentals=1 << 20),
    )(*operands)


def per_device(source_points, target_points, initial_potential, pair_list, pair_count):
    n_y, n_z = lax.axis_size("y"), lax.axis_size("z")
    own = target_points.shape[0]
    tgt_rows = n_z * own // LANES
    c = lax.axis_index("c")

    def shape(*dims):
        return jax.ShapeDtypeStruct(dims, f32)

    def points(*dims):
        return jax.ShapeDtypeStruct(dims, bf16)

    listed = jnp.pad(pair_list.reshape(1, PAIRS_MAX).astype(bf16), ((0, 15), (0, LANES - PAIRS_MAX)), constant_values=-1)
    sources = jnp.concatenate([lax.dynamic_slice_in_dim(source_points, c * BLOCK, BLOCK, 0), listed], axis=0)
    by = [
        lax.ppermute(sources, "y", [(i, (i + k) % n_y) for i in range(n_y)]) for k in range(1, n_y)
    ]
    targets = spread(jnp.broadcast_to(target_points[None], (n_z, own, EMB)), "z").reshape(n_z * own, EMB)
    lists = [part[BLOCK:BLOCK + 1].astype(f32) for part in (sources, *by)]
    potential = initial_potential.reshape(n_y * tgt_rows, LANES)
    shared = lax.all_gather(jnp.concatenate([potential, *lists, jnp.zeros((4, LANES), f32)], axis=0), "c")
    targets = lax.all_gather(targets, "c", axis=0, tiled=True)
    row_shape = shape(16, 16, LANES)
    row_parts, sources, source_squares, target_squares, kept = call(
        first_rows,
        [
            row_shape,
            points(n_y * BLOCK, EMB),
            shape(GROUPS, LANES),
            shape(2 * tgt_rows, LANES),
            shape(8, LANES),
        ],
        (sources, *by, targets, shared),
        WORK,
    )
    row_parts = spread(row_parts, ("y", "x"))
    col_parts, bias, terms, maxima = call(
        next_columns,
        [row_shape, shape(16, LANES), shape(PAIRS_MAX, BLOCK, BLOCK), shape(PAIRS_MAX, BLOCK)],
        (kept, sources, targets, row_parts),
        WORK,
    )
    col_parts = spread(col_parts, ("z", "c"))
    row_parts = call(
        next_rows,
        row_shape,
        (kept, sources, targets, bias, terms, maxima, col_parts),
        WORK + [pltpu.VMEM((16 * LANES, LANES), f32), pltpu.VMEM((8, BLOCK), f32)],
    )
    row_parts = spread(row_parts, ("y", "x"))
    parts = call(
        last_columns,
        shape(24, LANES),
        (kept, sources, targets, source_squares, target_squares, bias, terms, maxima, row_parts),
        [pltpu.VMEM((16, LANES), f32)] + WORK + [pltpu.VMEM((16 * LANES, LANES), f32)],
    )
    parts = lax.all_gather(parts, "c")
    col_parts = call(both_cores, shape(n_y * n_z, tgt_rows, LANES), (parts,), [])
    col_parts = spread(col_parts, ("y", "z"))
    source_potential, target_potential = call(
        last_potentials, [shape(2 * GROUPS, LANES), shape(n_y * tgt_rows, LANES)], (col_parts, parts), []
    )
    return source_potential.reshape(-1), target_potential.reshape(-1)


def solution(mesh):
    fine = Mesh(mesh.devices.reshape(4, 8, 4, 2), ("y", "z", "x", "c"))
    src, tgt = ("y", "z"), ("x", "c")
    placed = (P(src, None), P(tgt + src, None), P(tgt), P(src, tgt, None), P(src, tgt))
    return jax.shard_map(
        per_device, mesh=fine, in_specs=placed, out_specs=(P(src), P(tgt)), check_vma=False
    )
```

```python
import functools
import math

import jax
import jax.numpy as jnp
from jax import lax
from jax.experimental import pallas as pl
from jax.experimental.pallas import tpu as pltpu
from jax.sharding import Mesh
from jax.sharding import PartitionSpec as P

BLOCK = 512
LANES = 128
EMB = 128
PAIRS_MAX = 16
NEG_START = -1e30
EPS_REG = 0.2
LOG2E = math.log2(math.e)
LOG2_N = math.log2(32768)
SMALLEST = 2.0 ** -85
WIDEST = 85.0
SCALE = 2.0 * LOG2E / EPS_REG
GROUPS = BLOCK // LANES
HALF = BLOCK // 2
CHUNK = 32
CHUNKS = BLOCK // CHUNK
LAG = 12
PUSH_AT = 4

bf16 = jnp.bfloat16
f32 = jnp.float32


def lane_sums(terms):
    ones = jnp.ones((16, 2 * EMB), bf16)
    groups = terms[0].shape[0] // HALF

    def sums(products):
        for k in range(0, len(terms), 2):
            parts = jnp.concatenate(terms[k:k + 2], axis=1)
            for g in range(groups):
                stage = g // 2 % 2
                pltpu.matmul_push_rhs(parts[g * HALF:(g + 1) * HALF], stage, g % 2, transpose=True)
                pltpu.matmul_acc_lhs(products[g], ones, load_staged_rhs=stage)
        rows = []
        for g in range(groups):
            out = pltpu.matmul_pop(products[g])
            rows += [out[0:1, :LANES], out[0:1, LANES:]]
        return jnp.concatenate(rows, axis=0)

    return pl.run_scoped(sums, [pltpu.ACC(g % 2)((16, HALF), f32) for g in range(groups)])


def squares(points):
    values = points.astype(f32)
    sq = values * values
    high = sq.astype(bf16)
    return lane_sums([high, (sq - high.astype(f32)).astype(bf16)])


def bias_columns(bias):
    high = bias.astype(bf16).astype(f32)
    rest = bias - high
    middle = rest.astype(bf16).astype(f32)
    low = rest - middle
    count = bias.shape[0]
    stacked = jnp.concatenate([high, middle, low, jnp.zeros((LANES - 3 * count, LANES), f32)], axis=0)
    return stacked.T.astype(bf16)


def combined(parts):
    highest = jnp.max(parts, axis=0)
    total = jnp.sum(jnp.exp2(parts - highest[None]), axis=0)
    return highest + jnp.log(total) * LOG2E


def half_bias(lse):
    return (-0.5 * EPS_REG / LOG2E) * (LOG2_N + lse)


def clear(acc_max, acc_sum):
    acc_max[...] = jnp.full(acc_max.shape, NEG_START, f32)
    acc_sum[...] = jnp.zeros(acc_sum.shape, f32)


def sweep(*operands):
    products = [[pltpu.ACC(m)((CHUNK, HALF), f32) for _ in range(CHUNKS)] for m in range(2)]
    pl.run_scoped(functools.partial(sweep_with, *operands), products)


def sweep_with(pairs_ref, count, kept_ref, sum_ref, bias, acc_max, acc_sum, even, odd, kept_first, saved, mxus):
    kept_bias = bias_columns(bias)
    lane = lax.broadcasted_iota(jnp.int32, (CHUNK, LANES), 1) & (bias.shape[0] - 1)
    ones = jnp.ones((HALF, LANES), bf16)
    zeros = jnp.zeros((CHUNK, LANES), bf16)
    buffers = (even, odd)

    def where(number):
        real = number < count
        pair = jnp.where(real, pairs_ref[jnp.clip(number, 0, PAIRS_MAX - 1)], 0)
        first, second = pair >> 2, pair & 3
        return (first, second) if kept_first else (second, first)

    def push(number, parity):
        _, place = where(number)
        for m in range(2):
            rows = sum_ref[pl.ds(pl.multiple_of(place * BLOCK + m * HALF, HALF), HALF), :]
            pltpu.matmul_push_rhs(jnp.concatenate([rows, ones], axis=1), parity, m, transpose=True)

    def issue(along, parity, j):
        rows = kept_ref[pl.ds(pl.multiple_of(along * BLOCK + j * CHUNK, CHUNK), CHUNK), :]
        start = j * CHUNK % LANES
        mine = jnp.where(lane == along * GROUPS + j * CHUNK // LANES, kept_bias[start:start + CHUNK], zeros)
        lhs = jnp.concatenate([rows, mine], axis=1)
        for m in range(2):
            pltpu.matmul_acc_lhs(mxus[m][j], lhs, load_staged_rhs=parity if j == 0 else None)

    def take(parity, j, peak):
        for m in range(2):
            out = pltpu.matmul_pop(mxus[m][j])
            buffers[parity][j * CHUNK:(j + 1) * CHUNK, m * HALF:(m + 1) * HALF] = out
            for r in range(0, CHUNK, 8):
                peak[m] = jnp.maximum(peak[m], out[r:r + 8])

    def add(number, parity, j, shift, partial):
        for r in range(j * CHUNK, (j + 1) * CHUNK, 8):
            terms = jnp.exp2((buffers[parity][r:r + 8, :] - shift) * SCALE)
            partial = partial + terms
            if saved is not None:
                saved[0][jnp.maximum(number, 0), r:r + 8, :] = terms
        return partial

    def settle(number, peak):
        _, place = where(number)
        block_max = jnp.max(jnp.concatenate(peak, axis=1), axis=0, keepdims=True)
        old_max = acc_max[pl.ds(place, 1), :]
        highest = jnp.where(number < count, jnp.maximum(old_max, block_max), old_max)
        acc_max[pl.ds(place, 1), :] = highest
        if saved is not None:
            saved[1][pl.ds(number, 1), :] = highest
        acc_sum[pl.ds(place, 1), :] = acc_sum[pl.ds(place, 1), :] * jnp.exp2((old_max - highest) * SCALE)
        return jnp.broadcast_to(highest, (8, BLOCK))

    def fold(number, partial):
        _, place = where(number)
        block_sum = jnp.where((number >= 0) & (number < count), jnp.sum(partial, axis=0, keepdims=True), 0.0)
        place = jnp.where(number >= 0, place, 0)
        acc_sum[pl.ds(place, 1), :] = acc_sum[pl.ds(place, 1), :] + block_sum

    lowest = jnp.full((8, HALF), NEG_START, f32)
    nothing = jnp.zeros((8, BLOCK), f32)

    def body(i, parity, carry):
        peak0, peak1, shift, partial = carry
        peak = [peak0, peak1]
        along, _ = where(i + 1)
        for j in range(CHUNKS):
            issue(along, 1 - parity, j)
            if j == PUSH_AT:
                push(i + 2, parity)
            if j < LAG:
                take(parity, j + CHUNKS - LAG, peak)
                partial = add(i - 1, 1 - parity, j + CHUNKS - LAG, shift, partial)
                if j == LAG - 1:
                    fold(i - 1, partial)
                    shift = settle(i, peak)
                    peak = [lowest, lowest]
                    partial = nothing
            else:
                take(1 - parity, j - LAG, peak)
                partial = add(i, parity, j - LAG, shift, partial)
        return (*peak, shift, partial)

    push(0, 0)
    along, _ = where(0)
    peak = [lowest, lowest]
    for j in range(CHUNKS):
        issue(along, 0, j)
        if j == PUSH_AT:
            push(1, 1)
        if j >= LAG:
            take(0, j - LAG, peak)

    def turn(k, carry):
        return body(2 * k + 1, 1, body(2 * k, 0, carry))

    turns = (count + 1) >> 1
    carry = lax.fori_loop(0, turns, turn, (*peak, nothing, nothing))
    peak0, peak1, shift, partial = carry
    for j in range(LAG):
        take(0, j + CHUNKS - LAG, [peak0, peak1])
        partial = add(2 * turns - 1, 1, j + CHUNKS - LAG, shift, partial)
    fold(2 * turns - 1, partial)
    for m in range(2):
        pltpu.matmul_acc_lhs(mxus[m][0], jnp.zeros((CHUNK, 2 * LANES), bf16), load_staged_rhs=1)
        pltpu.matmul_pop(mxus[m][0])


def finished(acc_max, acc_sum):
    total = acc_sum[...]
    lse = jnp.where(total > 0, acc_max[...] * SCALE + jnp.log(total) * LOG2E, NEG_START)
    return jnp.concatenate([lse[b:b + 1, q * LANES:(q + 1) * LANES] for b in range(4) for q in range(GROUPS)], axis=0)


def bits(list_row, y_from, c_from, y, c):
    pair = list_row.astype(jnp.int32)
    number = y_from * 4 + c_from * 2 + (pair & 1)
    mine = (pair >> 3 == c) & (((pair >> 1) & 3) == y)
    return jnp.where(mine, jnp.left_shift(jnp.ones_like(pair), number), 0).astype(f32)


def packed(own_ref, by1_ref, by2_ref, by3_ref, after_ref, out_ref):
    lists = [ref[BLOCK:BLOCK + 16, :].astype(f32)[0:1, :] for ref in (own_ref, by1_ref, by2_ref, by3_ref)]
    out_ref[...] = jnp.concatenate(lists + [jnp.zeros((4, LANES), f32)], axis=0)


def first_rows(own_ref, by1_ref, by2_ref, by3_ref, targets_ref, lists_ref, potential_ref, out_ref, sources_ref, source_squares_ref, target_squares_ref, kept_ref, *scratch):
    y, c = lax.axis_index("y"), lax.axis_index("c")
    kept = jnp.zeros((1, LANES), f32)
    for c_from in range(2):
        lists = lists_ref[c_from]
        for by in range(4):
            kept = kept + bits(lists[by:by + 1, :], (y + 4 - by) & 3, c_from, y, c)
    kept_ref[...] = jnp.broadcast_to(kept, kept_ref.shape)
    for by, ref in enumerate((own_ref, by1_ref, by2_ref, by3_ref)):
        sources_ref[pl.ds(pl.multiple_of(((y + 4 - by) & 3) * BLOCK, BLOCK), BLOCK), :] = ref[0:BLOCK, :]
    source_squares_ref[...] = squares(own_ref[0:BLOCK, :])
    squared = squares(targets_ref[...])
    target_squares_ref[...] = squared
    rows = pl.ds(pl.multiple_of(y * 8, 8), 8)
    potential = jnp.concatenate([potential_ref[0, rows, :], potential_ref[1, rows, :]], axis=0)
    bias = 0.5 * (potential - squared)
    half_step(kept_ref, targets_ref, sources_ref, bias, False, *scratch)
    spread_out(out_ref, scratch)


def kept_pairs(kept_pairs_ref, chosen):
    kept = jnp.sum(kept_pairs_ref[0:1, :]).astype(jnp.int32)
    found = jnp.int32(0)
    for number in range(PAIRS_MAX):
        chosen[found] = number
        found = found + ((kept >> number) & 1)
    return kept, found


def half_step(kept_pairs_ref, kept_ref, sum_ref, bias, kept_first, acc_max, acc_sum, even, odd, chosen, saved=None):
    clear(acc_max, acc_sum)
    _, found = kept_pairs(kept_pairs_ref, chosen)
    sweep(chosen, found, kept_ref, sum_ref, bias, acc_max, acc_sum, even, odd, kept_first, saved)


def spread_out(out_ref, scratch):
    dense = finished(scratch[0], scratch[1])
    for k in range(out_ref.shape[0]):
        out_ref[k] = dense


def next_columns(kept_ref, sources_ref, targets_ref, parts_ref, out_ref, bias_ref, terms_ref, maxima_ref, *scratch):
    bias = half_bias(combined(parts_ref[...]))
    bias_ref[...] = bias
    half_step(kept_ref, sources_ref, targets_ref, bias, True, *scratch, (terms_ref, maxima_ref))
    spread_out(out_ref, scratch)


def in_kept_blocks(kept):
    block = lax.broadcasted_iota(jnp.int32, (16, LANES), 0) >> 2
    inside = jnp.zeros((16, LANES), jnp.int32)
    for b in range(4):
        inside = jnp.where(block == b, (kept >> (4 * b)) & 15, inside)
    return inside > 0


def any_of(condition):
    return jnp.max(jnp.where(condition, 1.0, 0.0)) > 0.5


def next_rows(kept_ref, sources_ref, targets_ref, old_bias_ref, terms_ref, maxima_ref, parts_ref, out_ref, acc_max, acc_sum, even, odd, chosen, rows_ref, lse_ref):
    lse = combined(parts_ref[...])
    kept, found = kept_pairs(kept_ref, chosen)
    for b in range(4):
        lse_ref[b:b + 1, :] = jnp.concatenate([lse[4 * b + q:4 * b + q + 1, :] for q in range(GROUPS)], axis=1)
    rows_ref[...] = jnp.zeros(rows_ref.shape, f32)

    def one(n, carry):
        pair = chosen[n]
        first, second = pair >> 2, pair & 3
        weight = jnp.exp2(maxima_ref[pl.ds(n, 1), :] * SCALE - lse_ref[pl.ds(second, 1), :])
        weight = jnp.broadcast_to(weight, (8, BLOCK))
        for r in range(0, BLOCK, 8):
            scaled = terms_ref[n, r:r + 8, :] * weight
            total = (scaled[:, 0:LANES] + scaled[:, LANES:2 * LANES]) + (scaled[:, 2 * LANES:3 * LANES] + scaled[:, 3 * LANES:])
            place = pl.ds(pl.multiple_of(first * BLOCK + r, 8), 8)
            rows_ref[place, :] = rows_ref[place, :] + total
        return carry

    lax.fori_loop(0, found, one, 0)
    total = rows_ref[...]
    high = total.astype(bf16)
    rest = total - high.astype(f32)
    sums = lane_sums([high, rest.astype(bf16)])
    inside = in_kept_blocks(kept)
    bad = any_of(inside & (sums < SMALLEST))
    safe = jnp.where(inside, sums, 1.0)
    dense = jnp.where(inside, jnp.log(safe) * LOG2E - SCALE * old_bias_ref[...] - LOG2_N, NEG_START)

    @pl.when(jnp.logical_not(bad))
    def _():
        for k in range(out_ref.shape[0]):
            out_ref[k] = dense

    @pl.when(bad)
    def _():
        half_step(kept_ref, targets_ref, sources_ref, half_bias(lse), False, acc_max, acc_sum, even, odd, chosen)
        spread_out(out_ref, (acc_max, acc_sum))


def last_columns(kept_ref, sources_ref, targets_ref, source_squares_ref, target_squares_ref, old_bias_ref, terms_ref, maxima_ref, parts_ref, out_ref, all_bias, acc_max, acc_sum, even, odd, chosen, ratio_ref):
    bias = half_bias(combined(parts_ref[...]))
    all_bias[...] = bias
    own = all_bias[pl.ds(lax.axis_index("y") * GROUPS, GROUPS), :]
    out_ref[16:16 + GROUPS, :] = source_squares_ref[...] + 2.0 * own
    out_ref[16 + GROUPS:24, :] = jnp.zeros((8 - GROUPS, LANES), f32)
    offset = target_squares_ref[...] * (LOG2E / EPS_REG)
    kept, found = kept_pairs(kept_ref, chosen)
    inside = in_kept_blocks(kept)
    moved = SCALE * (bias - old_bias_ref[...])
    largest = jnp.max(jnp.where(inside, moved, NEG_START))
    bad = any_of(inside & (moved < largest - WIDEST))
    ratio = jnp.exp2(jnp.where(inside, moved - largest, 0.0))

    @pl.when(jnp.logical_not(bad))
    def _():
        for k in range(16):
            ratio_ref[k * LANES:(k + 1) * LANES, :] = jnp.broadcast_to(ratio[k:k + 1, :], (LANES, LANES)).T
        clear(acc_max, acc_sum)

        def one(n, carry):
            pair = chosen[n]
            first, second = pair >> 2, pair & 3
            partial = [jnp.zeros((8, BLOCK), f32), jnp.zeros((8, BLOCK), f32)]
            for r in range(0, BLOCK, 8):
                factor = ratio_ref[pl.ds(pl.multiple_of(first * BLOCK + r, 8), 8), :]
                partial[r // 8 % 2] = partial[r // 8 % 2] + terms_ref[n, r:r + 8, :] * jnp.concatenate([factor] * GROUPS, axis=1)
            block_sum = jnp.sum(partial[0] + partial[1], axis=0, keepdims=True)
            highest = maxima_ref[pl.ds(n, 1), :]
            old = jnp.exp2((acc_max[pl.ds(second, 1), :] - highest) * SCALE)
            acc_sum[pl.ds(second, 1), :] = acc_sum[pl.ds(second, 1), :] * old + block_sum
            acc_max[pl.ds(second, 1), :] = highest
            return carry

        lax.fori_loop(0, found, one, 0)
        out_ref[0:16, :] = finished(acc_max, acc_sum) + largest - offset

    @pl.when(bad)
    def _():
        half_step(kept_ref, sources_ref, targets_ref, bias, True, acc_max, acc_sum, even, odd, chosen)
        out_ref[0:16, :] = finished(acc_max, acc_sum) - offset


def both_cores(parts_ref, out_ref):
    rows = pl.ds(pl.multiple_of(lax.axis_index("c") * 8, 8), 8)
    lse = combined(jnp.stack([parts_ref[0, rows, :], parts_ref[1, rows, :]]))
    for k in range(out_ref.shape[0]):
        out_ref[k] = lse


def last_potentials(parts_ref, cores_ref, source_ref, target_ref):
    for b in range(2):
        source_ref[b * GROUPS:(b + 1) * GROUPS, :] = cores_ref[b, 16:16 + GROUPS, :]
    count = parts_ref.shape[0] // 4
    for y in range(4):
        lse = combined(parts_ref[y * count:(y + 1) * count])
        target_ref[y * 8:(y + 1) * 8, :] = 2.0 * half_bias(lse)


VMEM = pl.BlockSpec(memory_space=pltpu.VMEM)
PARAMS = pltpu.CompilerParams(vmem_limit_bytes=24 * 1024 * 1024)
WORK = [pltpu.VMEM((8, BLOCK), f32)] * 2 + [pltpu.VMEM((BLOCK, BLOCK), f32)] * 2 + [pltpu.SMEM((PAIRS_MAX,), jnp.int32)]


def spread(parts, axes):
    return lax.all_to_all(parts, axes, 0, 0, tiled=True)


def call(kernel, out_shape, operands, scratch):
    return pl.pallas_call(
        kernel,
        out_shape=out_shape,
        in_specs=[VMEM] * len(operands),
        out_specs=jax.tree.map(lambda _: VMEM, out_shape),
        scratch_shapes=scratch,
        compiler_params=PARAMS,
        cost_estimate=pl.CostEstimate(flops=1 << 30, bytes_accessed=1 << 22, transcendentals=1 << 20),
    )(*operands)


def per_device(source_points, target_points, initial_potential, pair_list, pair_count):
    n_y, n_z = lax.axis_size("y"), lax.axis_size("z")
    own = target_points.shape[0]
    tgt_rows = n_z * own // LANES
    c = lax.axis_index("c")

    def shape(*dims):
        return jax.ShapeDtypeStruct(dims, f32)

    def points(*dims):
        return jax.ShapeDtypeStruct(dims, bf16)

    listed = jnp.pad(pair_list.reshape(1, PAIRS_MAX).astype(bf16), ((0, 15), (0, LANES - PAIRS_MAX)), constant_values=-1)
    sources = jnp.concatenate([lax.dynamic_slice_in_dim(source_points, c * BLOCK, BLOCK, 0), listed], axis=0)
    by = [
        lax.ppermute(sources, "y", [(i, (i + k) % n_y) for i in range(n_y)]) for k in range(1, n_y)
    ]
    targets = spread(jnp.broadcast_to(target_points[None], (n_z, own, EMB)), "z").reshape(n_z * own, EMB)
    targets = lax.all_gather(targets, "c", axis=0, tiled=True)
    potential = lax.all_gather(initial_potential.reshape(n_y * tgt_rows, LANES), "c")
    lists = lax.all_gather(call(packed, shape(8, LANES), (sources, *by, targets), []), "c")
    row_shape = shape(16, 16, LANES)
    row_parts, sources, source_squares, target_squares, kept = call(
        first_rows,
        [
            row_shape,
            points(n_y * BLOCK, EMB),
            shape(GROUPS, LANES),
            shape(2 * tgt_rows, LANES),
            shape(8, LANES),
        ],
        (sources, *by, targets, lists, potential),
        WORK,
    )
    row_parts = spread(row_parts, ("y", "x"))
    col_parts, bias, terms, maxima = call(
        next_columns,
        [row_shape, shape(16, LANES), shape(PAIRS_MAX, BLOCK, BLOCK), shape(PAIRS_MAX, BLOCK)],
        (kept, sources, targets, row_parts),
        WORK,
    )
    col_parts = spread(col_parts, ("z", "c"))
    row_parts = call(
        next_rows,
        row_shape,
        (kept, sources, targets, bias, terms, maxima, col_parts),
        WORK + [pltpu.VMEM((16 * LANES, LANES), f32), pltpu.VMEM((8, BLOCK), f32)],
    )
    row_parts = spread(row_parts, ("y", "x"))
    parts = call(
        last_columns,
        shape(24, LANES),
        (kept, sources, targets, source_squares, target_squares, bias, terms, maxima, row_parts),
        [pltpu.VMEM((16, LANES), f32)] + WORK + [pltpu.VMEM((16 * LANES, LANES), f32)],
    )
    parts = lax.all_gather(parts, "c")
    col_parts = call(both_cores, shape(n_y * n_z, tgt_rows, LANES), (parts,), [])
    col_parts = spread(col_parts, ("y", "z"))
    source_potential, target_potential = call(
        last_potentials, [shape(2 * GROUPS, LANES), shape(n_y * tgt_rows, LANES)], (col_parts, parts), []
    )
    return source_potential.reshape(-1), target_potential.reshape(-1)


def solution(mesh):
    fine = Mesh(mesh.devices.reshape(4, 8, 4, 2), ("y", "z", "x", "c"))
    src, tgt = ("y", "z"), ("x", "c")
    placed = (P(src, None), P(tgt + src, None), P(tgt), P(src, tgt, None), P(src, tgt))
    return jax.shard_map(
        per_device, mesh=fine, in_specs=placed, out_specs=(P(src), P(tgt)), check_vma=False
    )
```

```python
import functools
import math

import jax
import jax.numpy as jnp
from jax import lax
from jax.experimental import pallas as pl
from jax.experimental.pallas import tpu as pltpu
from jax.sharding import Mesh
from jax.sharding import PartitionSpec as P

BLOCK = 512
LANES = 128
EMB = 128
PAIRS_MAX = 16
NEG_START = -1e30
EPS_REG = 0.2
LOG2E = math.log2(math.e)
LOG2_N = math.log2(32768)
SMALLEST = 2.0 ** -85
WIDEST = 85.0
SCALE = 2.0 * LOG2E / EPS_REG
GROUPS = BLOCK // LANES
HALF = BLOCK // 2
CHUNK = 32
CHUNKS = BLOCK // CHUNK
LAG = 12
PUSH_AT = 4

bf16 = jnp.bfloat16
f32 = jnp.float32


def lane_sums(terms):
    ones = jnp.ones((16, 2 * EMB), bf16)
    groups = terms[0].shape[0] // HALF

    def sums(products):
        for k in range(0, len(terms), 2):
            parts = jnp.concatenate(terms[k:k + 2], axis=1)
            for g in range(groups):
                stage = g // 2 % 2
                pltpu.matmul_push_rhs(parts[g * HALF:(g + 1) * HALF], stage, g % 2, transpose=True)
                pltpu.matmul_acc_lhs(products[g], ones, load_staged_rhs=stage)
        rows = []
        for g in range(groups):
            out = pltpu.matmul_pop(products[g])
            rows += [out[0:1, :LANES], out[0:1, LANES:]]
        return jnp.concatenate(rows, axis=0)

    return pl.run_scoped(sums, [pltpu.ACC(g % 2)((16, HALF), f32) for g in range(groups)])


def squares(points):
    values = points.astype(f32)
    sq = values * values
    high = sq.astype(bf16)
    return lane_sums([high, (sq - high.astype(f32)).astype(bf16)])


def bias_columns(bias):
    high = bias.astype(bf16).astype(f32)
    rest = bias - high
    middle = rest.astype(bf16).astype(f32)
    low = rest - middle
    count = bias.shape[0]
    stacked = jnp.concatenate([high, middle, low, jnp.zeros((LANES - 3 * count, LANES), f32)], axis=0)
    return stacked.T.astype(bf16)


def combined(parts):
    highest = jnp.max(parts, axis=0)
    total = jnp.sum(jnp.exp2(parts - highest[None]), axis=0)
    return highest + jnp.log(total) * LOG2E


def half_bias(lse):
    return (-0.5 * EPS_REG / LOG2E) * (LOG2_N + lse)


def clear(acc_max, acc_sum):
    acc_max[...] = jnp.full(acc_max.shape, NEG_START, f32)
    acc_sum[...] = jnp.zeros(acc_sum.shape, f32)


def sweep(*operands):
    products = [[pltpu.ACC(m)((CHUNK, HALF), f32) for _ in range(CHUNKS)] for m in range(2)]
    pl.run_scoped(functools.partial(sweep_with, *operands), products)


def sweep_with(pairs_ref, count, kept_ref, sum_ref, bias, acc_max, acc_sum, even, odd, kept_first, saved, mxus):
    kept_bias = bias_columns(bias)
    lane = lax.broadcasted_iota(jnp.int32, (CHUNK, LANES), 1) & (bias.shape[0] - 1)
    ones = jnp.ones((HALF, LANES), bf16)
    zeros = jnp.zeros((CHUNK, LANES), bf16)
    buffers = (even, odd)

    def where(number):
        real = number < count
        pair = jnp.where(real, pairs_ref[jnp.clip(number, 0, PAIRS_MAX - 1)], 0)
        first, second = pair >> 2, pair & 3
        return (first, second) if kept_first else (second, first)

    def push(number, parity):
        _, place = where(number)
        for m in range(2):
            rows = sum_ref[pl.ds(pl.multiple_of(place * BLOCK + m * HALF, HALF), HALF), :]
            pltpu.matmul_push_rhs(jnp.concatenate([rows, ones], axis=1), parity, m, transpose=True)

    def issue(along, parity, j):
        rows = kept_ref[pl.ds(pl.multiple_of(along * BLOCK + j * CHUNK, CHUNK), CHUNK), :]
        start = j * CHUNK % LANES
        mine = jnp.where(lane == along * GROUPS + j * CHUNK // LANES, kept_bias[start:start + CHUNK], zeros)
        lhs = jnp.concatenate([rows, mine], axis=1)
        for m in range(2):
            pltpu.matmul_acc_lhs(mxus[m][j], lhs, load_staged_rhs=parity if j == 0 else None)

    def take(parity, j, peak):
        for m in range(2):
            out = pltpu.matmul_pop(mxus[m][j])
            buffers[parity][j * CHUNK:(j + 1) * CHUNK, m * HALF:(m + 1) * HALF] = out
            for r in range(0, CHUNK, 8):
                peak[m] = jnp.maximum(peak[m], out[r:r + 8])

    def add(number, parity, j, shift, partial):
        for r in range(j * CHUNK, (j + 1) * CHUNK, 8):
            terms = jnp.exp2((buffers[parity][r:r + 8, :] - shift) * SCALE)
            partial = partial + terms
            if saved is not None:
                saved[0][jnp.maximum(number, 0), r:r + 8, :] = terms
        return partial

    def settle(number, peak):
        _, place = where(number)
        block_max = jnp.max(jnp.concatenate(peak, axis=1), axis=0, keepdims=True)
        old_max = acc_max[pl.ds(place, 1), :]
        highest = jnp.where(number < count, jnp.maximum(old_max, block_max), old_max)
        acc_max[pl.ds(place, 1), :] = highest
        if saved is not None:
            saved[1][pl.ds(number, 1), :] = highest
        acc_sum[pl.ds(place, 1), :] = acc_sum[pl.ds(place, 1), :] * jnp.exp2((old_max - highest) * SCALE)
        return jnp.broadcast_to(highest, (8, BLOCK))

    def fold(number, partial):
        _, place = where(number)
        block_sum = jnp.where((number >= 0) & (number < count), jnp.sum(partial, axis=0, keepdims=True), 0.0)
        place = jnp.where(number >= 0, place, 0)
        acc_sum[pl.ds(place, 1), :] = acc_sum[pl.ds(place, 1), :] + block_sum

    lowest = jnp.full((8, HALF), NEG_START, f32)
    nothing = jnp.zeros((8, BLOCK), f32)

    def body(i, parity, carry):
        peak0, peak1, shift, partial = carry
        peak = [peak0, peak1]
        along, _ = where(i + 1)
        for j in range(CHUNKS):
            issue(along, 1 - parity, j)
            if j == PUSH_AT:
                push(i + 2, parity)
            if j < LAG:
                take(parity, j + CHUNKS - LAG, peak)
                partial = add(i - 1, 1 - parity, j + CHUNKS - LAG, shift, partial)
                if j == LAG - 1:
                    fold(i - 1, partial)
                    shift = settle(i, peak)
                    peak = [lowest, lowest]
                    partial = nothing
            else:
                take(1 - parity, j - LAG, peak)
                partial = add(i, parity, j - LAG, shift, partial)
        return (*peak, shift, partial)

    push(0, 0)
    along, _ = where(0)
    peak = [lowest, lowest]
    for j in range(CHUNKS):
        issue(along, 0, j)
        if j == PUSH_AT:
            push(1, 1)
        if j >= LAG:
            take(0, j - LAG, peak)

    def turn(k, carry):
        return body(2 * k + 1, 1, body(2 * k, 0, carry))

    def close(last, parity, carry):
        *_, shift, partial = carry
        for j in range(LAG):
            for m in range(2):
                pltpu.matmul_pop(mxus[m][j + CHUNKS - LAG])
            partial = add(last, parity, j + CHUNKS - LAG, shift, partial)
        fold(last, partial)
        for m in range(2):
            pltpu.matmul_acc_lhs(mxus[m][0], jnp.zeros((CHUNK, 2 * LANES), bf16), load_staged_rhs=parity)
            pltpu.matmul_pop(mxus[m][0])

    turns = count >> 1
    carry = lax.fori_loop(0, turns, turn, (*peak, nothing, nothing))
    odd_count = (count & 1) == 1

    @pl.when(odd_count)
    def _():
        close(count - 1, 0, body(count - 1, 0, carry))

    @pl.when(jnp.logical_not(odd_count))
    def _():
        close(count - 1, 1, carry)


def finished(acc_max, acc_sum):
    total = acc_sum[...]
    lse = jnp.where(total > 0, acc_max[...] * SCALE + jnp.log(total) * LOG2E, NEG_START)
    return jnp.concatenate([lse[b:b + 1, q * LANES:(q + 1) * LANES] for b in range(4) for q in range(GROUPS)], axis=0)


def bits(list_row, y_from, c_from, y, c):
    pair = list_row.astype(jnp.int32)
    number = y_from * 4 + c_from * 2 + (pair & 1)
    mine = (pair >> 3 == c) & (((pair >> 1) & 3) == y)
    return jnp.where(mine, jnp.left_shift(jnp.ones_like(pair), number), 0).astype(f32)


def packed(own_ref, by1_ref, by2_ref, by3_ref, targets_ref, out_ref):
    lists = [ref[BLOCK:BLOCK + 16, :].astype(f32)[0:1, :] for ref in (own_ref, by1_ref, by2_ref, by3_ref)]
    out_ref[0:8, :] = jnp.concatenate(lists + [jnp.zeros((4, LANES), f32)], axis=0)
    rows = pl.ds(pl.multiple_of(lax.axis_index("c") * 2 * BLOCK, 2 * BLOCK), 2 * BLOCK)
    out_ref[8:16, :] = squares(targets_ref[rows, :])


def first_rows(own_ref, by1_ref, by2_ref, by3_ref, targets_ref, lists_ref, potential_ref, out_ref, sources_ref, source_squares_ref, target_squares_ref, kept_ref, *scratch):
    y, c = lax.axis_index("y"), lax.axis_index("c")
    kept = jnp.zeros((1, LANES), f32)
    for c_from in range(2):
        lists = lists_ref[c_from, 0:8, :]
        for by in range(4):
            kept = kept + bits(lists[by:by + 1, :], (y + 4 - by) & 3, c_from, y, c)
    kept_ref[...] = jnp.broadcast_to(kept, kept_ref.shape)
    for by, ref in enumerate((own_ref, by1_ref, by2_ref, by3_ref)):
        sources_ref[pl.ds(pl.multiple_of(((y + 4 - by) & 3) * BLOCK, BLOCK), BLOCK), :] = ref[0:BLOCK, :]
    source_squares_ref[...] = squares(own_ref[0:BLOCK, :])
    squared = jnp.concatenate([lists_ref[0, 8:16, :], lists_ref[1, 8:16, :]], axis=0)
    target_squares_ref[...] = squared
    rows = pl.ds(pl.multiple_of(y * 8, 8), 8)
    potential = jnp.concatenate([potential_ref[0, rows, :], potential_ref[1, rows, :]], axis=0)
    bias = 0.5 * (potential - squared)
    half_step(kept_ref, targets_ref, sources_ref, bias, False, *scratch)
    spread_out(out_ref, scratch)


def kept_pairs(kept_pairs_ref, chosen):
    kept = jnp.sum(kept_pairs_ref[0:1, :]).astype(jnp.int32)
    found = jnp.int32(0)
    for number in range(PAIRS_MAX):
        chosen[found] = number
        found = found + ((kept >> number) & 1)
    return kept, found


def half_step(kept_pairs_ref, kept_ref, sum_ref, bias, kept_first, acc_max, acc_sum, even, odd, chosen, saved=None):
    clear(acc_max, acc_sum)
    _, found = kept_pairs(kept_pairs_ref, chosen)
    sweep(chosen, found, kept_ref, sum_ref, bias, acc_max, acc_sum, even, odd, kept_first, saved)


def spread_out(out_ref, scratch):
    dense = finished(scratch[0], scratch[1])
    for k in range(out_ref.shape[0]):
        out_ref[k] = dense


def next_columns(kept_ref, sources_ref, targets_ref, parts_ref, out_ref, bias_ref, terms_ref, maxima_ref, *scratch):
    bias = half_bias(combined(parts_ref[...]))
    bias_ref[...] = bias
    half_step(kept_ref, sources_ref, targets_ref, bias, True, *scratch, (terms_ref, maxima_ref))
    spread_out(out_ref, scratch)


def in_kept_blocks(kept):
    block = lax.broadcasted_iota(jnp.int32, (16, LANES), 0) >> 2
    inside = jnp.zeros((16, LANES), jnp.int32)
    for b in range(4):
        inside = jnp.where(block == b, (kept >> (4 * b)) & 15, inside)
    return inside > 0


def any_of(condition):
    return jnp.max(jnp.where(condition, 1.0, 0.0)) > 0.5


def next_rows(kept_ref, sources_ref, targets_ref, old_bias_ref, terms_ref, maxima_ref, parts_ref, out_ref, acc_max, acc_sum, even, odd, chosen, rows_ref, lse_ref):
    lse = combined(parts_ref[...])
    kept, found = kept_pairs(kept_ref, chosen)
    for b in range(4):
        lse_ref[b:b + 1, :] = jnp.concatenate([lse[4 * b + q:4 * b + q + 1, :] for q in range(GROUPS)], axis=1)
    rows_ref[...] = jnp.zeros(rows_ref.shape, f32)

    def one(n, carry):
        pair = chosen[n]
        first, second = pair >> 2, pair & 3
        weight = jnp.exp2(maxima_ref[pl.ds(n, 1), :] * SCALE - lse_ref[pl.ds(second, 1), :])
        weight = jnp.broadcast_to(weight, (8, BLOCK))
        for r in range(0, BLOCK, 8):
            scaled = terms_ref[n, r:r + 8, :] * weight
            total = (scaled[:, 0:LANES] + scaled[:, LANES:2 * LANES]) + (scaled[:, 2 * LANES:3 * LANES] + scaled[:, 3 * LANES:])
            place = pl.ds(pl.multiple_of(first * BLOCK + r, 8), 8)
            rows_ref[place, :] = rows_ref[place, :] + total
        return carry

    lax.fori_loop(0, found, one, 0)
    total = rows_ref[...]
    high = total.astype(bf16)
    rest = total - high.astype(f32)
    sums = lane_sums([high, rest.astype(bf16)])
    inside = in_kept_blocks(kept)
    bad = any_of(inside & (sums < SMALLEST))
    safe = jnp.where(inside, sums, 1.0)
    dense = jnp.where(inside, jnp.log(safe) * LOG2E - SCALE * old_bias_ref[...] - LOG2_N, NEG_START)

    @pl.when(jnp.logical_not(bad))
    def _():
        for k in range(out_ref.shape[0]):
            out_ref[k] = dense

    @pl.when(bad)
    def _():
        half_step(kept_ref, targets_ref, sources_ref, half_bias(lse), False, acc_max, acc_sum, even, odd, chosen)
        spread_out(out_ref, (acc_max, acc_sum))


def last_columns(kept_ref, sources_ref, targets_ref, source_squares_ref, target_squares_ref, old_bias_ref, terms_ref, maxima_ref, parts_ref, out_ref, all_bias, acc_max, acc_sum, even, odd, chosen, ratio_ref):
    bias = half_bias(combined(parts_ref[...]))
    all_bias[...] = bias
    own = all_bias[pl.ds(lax.axis_index("y") * GROUPS, GROUPS), :]
    out_ref[16:16 + GROUPS, :] = source_squares_ref[...] + 2.0 * own
    out_ref[16 + GROUPS:24, :] = jnp.zeros((8 - GROUPS, LANES), f32)
    offset = target_squares_ref[...] * (LOG2E / EPS_REG)
    kept, found = kept_pairs(kept_ref, chosen)
    inside = in_kept_blocks(kept)
    moved = SCALE * (bias - old_bias_ref[...])
    largest = jnp.max(jnp.where(inside, moved, NEG_START))
    bad = any_of(inside & (moved < largest - WIDEST))
    ratio = jnp.exp2(jnp.where(inside, moved - largest, 0.0))

    @pl.when(jnp.logical_not(bad))
    def _():
        for k in range(16):
            ratio_ref[k * LANES:(k + 1) * LANES, :] = jnp.broadcast_to(ratio[k:k + 1, :], (LANES, LANES)).T
        clear(acc_max, acc_sum)

        def one(n, carry):
            pair = chosen[n]
            first, second = pair >> 2, pair & 3
            partial = [jnp.zeros((8, BLOCK), f32), jnp.zeros((8, BLOCK), f32)]
            for r in range(0, BLOCK, 8):
                factor = ratio_ref[pl.ds(pl.multiple_of(first * BLOCK + r, 8), 8), :]
                partial[r // 8 % 2] = partial[r // 8 % 2] + terms_ref[n, r:r + 8, :] * jnp.concatenate([factor] * GROUPS, axis=1)
            block_sum = jnp.sum(partial[0] + partial[1], axis=0, keepdims=True)
            highest = maxima_ref[pl.ds(n, 1), :]
            old = jnp.exp2((acc_max[pl.ds(second, 1), :] - highest) * SCALE)
            acc_sum[pl.ds(second, 1), :] = acc_sum[pl.ds(second, 1), :] * old + block_sum
            acc_max[pl.ds(second, 1), :] = highest
            return carry

        lax.fori_loop(0, found, one, 0)
        out_ref[0:16, :] = finished(acc_max, acc_sum) + largest - offset

    @pl.when(bad)
    def _():
        half_step(kept_ref, sources_ref, targets_ref, bias, True, acc_max, acc_sum, even, odd, chosen)
        out_ref[0:16, :] = finished(acc_max, acc_sum) - offset


def both_cores(parts_ref, out_ref):
    rows = pl.ds(pl.multiple_of(lax.axis_index("c") * 8, 8), 8)
    lse = combined(jnp.stack([parts_ref[0, rows, :], parts_ref[1, rows, :]]))
    for k in range(out_ref.shape[0]):
        out_ref[k] = lse


def last_potentials(parts_ref, cores_ref, source_ref, target_ref):
    for b in range(2):
        source_ref[b * GROUPS:(b + 1) * GROUPS, :] = cores_ref[b, 16:16 + GROUPS, :]
    count = parts_ref.shape[0] // 4
    for y in range(4):
        lse = combined(parts_ref[y * count:(y + 1) * count])
        target_ref[y * 8:(y + 1) * 8, :] = 2.0 * half_bias(lse)


VMEM = pl.BlockSpec(memory_space=pltpu.VMEM)
PARAMS = pltpu.CompilerParams(vmem_limit_bytes=24 * 1024 * 1024)
WORK = [pltpu.VMEM((8, BLOCK), f32)] * 2 + [pltpu.VMEM((BLOCK, BLOCK), f32)] * 2 + [pltpu.SMEM((PAIRS_MAX,), jnp.int32)]


def spread(parts, axes):
    return lax.all_to_all(parts, axes, 0, 0, tiled=True)


def call(kernel, out_shape, operands, scratch):
    return pl.pallas_call(
        kernel,
        out_shape=out_shape,
        in_specs=[VMEM] * len(operands),
        out_specs=jax.tree.map(lambda _: VMEM, out_shape),
        scratch_shapes=scratch,
        compiler_params=PARAMS,
        cost_estimate=pl.CostEstimate(flops=1 << 30, bytes_accessed=1 << 22, transcendentals=1 << 20),
    )(*operands)


def per_device(source_points, target_points, initial_potential, pair_list, pair_count):
    n_y, n_z = lax.axis_size("y"), lax.axis_size("z")
    own = target_points.shape[0]
    tgt_rows = n_z * own // LANES
    c = lax.axis_index("c")

    def shape(*dims):
        return jax.ShapeDtypeStruct(dims, f32)

    def points(*dims):
        return jax.ShapeDtypeStruct(dims, bf16)

    listed = jnp.pad(pair_list.reshape(1, PAIRS_MAX).astype(bf16), ((0, 15), (0, LANES - PAIRS_MAX)), constant_values=-1)
    sources = jnp.concatenate([lax.dynamic_slice_in_dim(source_points, c * BLOCK, BLOCK, 0), listed], axis=0)
    by = [
        lax.ppermute(sources, "y", [(i, (i + k) % n_y) for i in range(n_y)]) for k in range(1, n_y)
    ]
    targets = spread(jnp.broadcast_to(target_points[None], (n_z, own, EMB)), "z").reshape(n_z * own, EMB)
    targets = lax.all_gather(targets, "c", axis=0, tiled=True)
    potential = lax.all_gather(initial_potential.reshape(n_y * tgt_rows, LANES), "c")
    lists = lax.all_gather(call(packed, shape(16, LANES), (sources, *by, targets), []), "c")
    row_shape = shape(16, 16, LANES)
    row_parts, sources, source_squares, target_squares, kept = call(
        first_rows,
        [
            row_shape,
            points(n_y * BLOCK, EMB),
            shape(GROUPS, LANES),
            shape(2 * tgt_rows, LANES),
            shape(8, LANES),
        ],
        (sources, *by, targets, lists, potential),
        WORK,
    )
    row_parts = spread(row_parts, ("y", "x"))
    col_parts, bias, terms, maxima = call(
        next_columns,
        [row_shape, shape(16, LANES), shape(PAIRS_MAX, BLOCK, BLOCK), shape(PAIRS_MAX, BLOCK)],
        (kept, sources, targets, row_parts),
        WORK,
    )
    col_parts = spread(col_parts, ("z", "c"))
    row_parts = call(
        next_rows,
        row_shape,
        (kept, sources, targets, bias, terms, maxima, col_parts),
        WORK + [pltpu.VMEM((16 * LANES, LANES), f32), pltpu.VMEM((8, BLOCK), f32)],
    )
    row_parts = spread(row_parts, ("y", "x"))
    parts = call(
        last_columns,
        shape(24, LANES),
        (kept, sources, targets, source_squares, target_squares, bias, terms, maxima, row_parts),
        [pltpu.VMEM((16, LANES), f32)] + WORK + [pltpu.VMEM((16 * LANES, LANES), f32)],
    )
    parts = lax.all_gather(parts, "c")
    col_parts = call(both_cores, shape(n_y * n_z, tgt_rows, LANES), (parts,), [])
    col_parts = spread(col_parts, ("y", "z"))
    source_potential, target_potential = call(
        last_potentials, [shape(2 * GROUPS, LANES), shape(n_y * tgt_rows, LANES)], (col_parts, parts), []
    )
    return source_potential.reshape(-1), target_potential.reshape(-1)


def solution(mesh):
    fine = Mesh(mesh.devices.reshape(4, 8, 4, 2), ("y", "z", "x", "c"))
    src, tgt = ("y", "z"), ("x", "c")
    placed = (P(src, None), P(tgt + src, None), P(tgt), P(src, tgt, None), P(src, tgt))
    return jax.shard_map(
        per_device, mesh=fine, in_specs=placed, out_specs=(P(src), P(tgt)), check_vma=False
    )
```

```python
import functools
import math

import jax
import jax.numpy as jnp
from jax import lax
from jax.experimental import pallas as pl
from jax.experimental.pallas import tpu as pltpu
from jax.sharding import Mesh
from jax.sharding import PartitionSpec as P

BLOCK = 512
LANES = 128
EMB = 128
PAIRS_MAX = 16
NEG_START = -1e30
EPS_REG = 0.2
LOG2E = math.log2(math.e)
LOG2_N = math.log2(32768)
SMALLEST = 2.0 ** -85
WIDEST = 85.0
SCALE = 2.0 * LOG2E / EPS_REG
GROUPS = BLOCK // LANES
HALF = BLOCK // 2
CHUNK = 32
CHUNKS = BLOCK // CHUNK
LAG = 12
PUSH_AT = 4

bf16 = jnp.bfloat16
f32 = jnp.float32


def lane_sums(terms):
    ones = jnp.ones((16, 2 * EMB), bf16)
    groups = terms[0].shape[0] // HALF

    def sums(products):
        for k in range(0, len(terms), 2):
            parts = jnp.concatenate(terms[k:k + 2], axis=1)
            for g in range(groups):
                stage = g // 2 % 2
                pltpu.matmul_push_rhs(parts[g * HALF:(g + 1) * HALF], stage, g % 2, transpose=True)
                pltpu.matmul_acc_lhs(products[g], ones, load_staged_rhs=stage)
        rows = []
        for g in range(groups):
            out = pltpu.matmul_pop(products[g])
            rows += [out[0:1, :LANES], out[0:1, LANES:]]
        return jnp.concatenate(rows, axis=0)

    return pl.run_scoped(sums, [pltpu.ACC(g % 2)((16, HALF), f32) for g in range(groups)])


def squares(points):
    values = points.astype(f32)
    sq = values * values
    high = sq.astype(bf16)
    return lane_sums([high, (sq - high.astype(f32)).astype(bf16)])


def bias_columns(bias):
    high = bias.astype(bf16).astype(f32)
    rest = bias - high
    middle = rest.astype(bf16).astype(f32)
    low = rest - middle
    count = bias.shape[0]
    stacked = jnp.concatenate([high, middle, low, jnp.zeros((LANES - 3 * count, LANES), f32)], axis=0)
    return stacked.T.astype(bf16)


def combined(parts):
    highest = jnp.max(parts, axis=0)
    total = jnp.sum(jnp.exp2(parts - highest[None]), axis=0)
    return highest + jnp.log(total) * LOG2E


def half_bias(lse):
    return (-0.5 * EPS_REG / LOG2E) * (LOG2_N + lse)


def clear(acc_max, acc_sum):
    acc_max[...] = jnp.full(acc_max.shape, NEG_START, f32)
    acc_sum[...] = jnp.zeros(acc_sum.shape, f32)


def sweep(*operands):
    products = [[pltpu.ACC(m)((CHUNK, HALF), f32) for _ in range(CHUNKS)] for m in range(2)]
    pl.run_scoped(functools.partial(sweep_with, *operands), products)


def sweep_with(pairs_ref, count, kept_ref, sum_ref, bias, acc_max, acc_sum, even, odd, kept_first, saved, mxus):
    kept_bias = bias_columns(bias)
    lane = lax.broadcasted_iota(jnp.int32, (CHUNK, LANES), 1) & (bias.shape[0] - 1)
    ones = jnp.ones((HALF, LANES), bf16)
    zeros = jnp.zeros((CHUNK, LANES), bf16)
    buffers = (even, odd)

    def where(number):
        real = number < count
        pair = jnp.where(real, pairs_ref[jnp.clip(number, 0, PAIRS_MAX - 1)], 0)
        first, second = pair >> 2, pair & 3
        return (first, second) if kept_first else (second, first)

    def push(number, parity):
        _, place = where(number)
        for m in range(2):
            rows = sum_ref[pl.ds(pl.multiple_of(place * BLOCK + m * HALF, HALF), HALF), :]
            pltpu.matmul_push_rhs(jnp.concatenate([rows, ones], axis=1), parity, m, transpose=True)

    def issue(along, parity, j):
        rows = kept_ref[pl.ds(pl.multiple_of(along * BLOCK + j * CHUNK, CHUNK), CHUNK), :]
        start = j * CHUNK % LANES
        mine = jnp.where(lane == along * GROUPS + j * CHUNK // LANES, kept_bias[start:start + CHUNK], zeros)
        lhs = jnp.concatenate([rows, mine], axis=1)
        for m in range(2):
            pltpu.matmul_acc_lhs(mxus[m][j], lhs, load_staged_rhs=parity if j == 0 else None)

    def take(parity, j, peak):
        for m in range(2):
            out = pltpu.matmul_pop(mxus[m][j])
            buffers[parity][j * CHUNK:(j + 1) * CHUNK, m * HALF:(m + 1) * HALF] = out
            for r in range(0, CHUNK, 8):
                peak[m] = jnp.maximum(peak[m], out[r:r + 8])

    def add(number, parity, j, shift, partial):
        for r in range(j * CHUNK, (j + 1) * CHUNK, 8):
            terms = jnp.exp2((buffers[parity][r:r + 8, :] - shift) * SCALE)
            partial = partial + terms
            if saved is not None:
                saved[0][jnp.maximum(number, 0), r:r + 8, :] = terms
        return partial

    def settle(number, peak):
        _, place = where(number)
        block_max = jnp.max(jnp.concatenate(peak, axis=1), axis=0, keepdims=True)
        old_max = acc_max[pl.ds(place, 1), :]
        highest = jnp.where(number < count, jnp.maximum(old_max, block_max), old_max)
        acc_max[pl.ds(place, 1), :] = highest
        if saved is not None:
            saved[1][pl.ds(number, 1), :] = highest
        acc_sum[pl.ds(place, 1), :] = acc_sum[pl.ds(place, 1), :] * jnp.exp2((old_max - highest) * SCALE)
        return jnp.broadcast_to(highest, (8, BLOCK))

    def fold(number, partial):
        _, place = where(number)
        block_sum = jnp.where((number >= 0) & (number < count), jnp.sum(partial, axis=0, keepdims=True), 0.0)
        place = jnp.where(number >= 0, place, 0)
        acc_sum[pl.ds(place, 1), :] = acc_sum[pl.ds(place, 1), :] + block_sum

    lowest = jnp.full((8, HALF), NEG_START, f32)
    nothing = jnp.zeros((8, BLOCK), f32)

    def body(i, parity, carry):
        peak0, peak1, shift, partial = carry
        peak = [peak0, peak1]
        along, _ = where(i + 1)
        for j in range(CHUNKS):
            issue(along, 1 - parity, j)
            if j == PUSH_AT:
                push(i + 2, parity)
            if j < LAG:
                take(parity, j + CHUNKS - LAG, peak)
                partial = add(i - 1, 1 - parity, j + CHUNKS - LAG, shift, partial)
                if j == LAG - 1:
                    fold(i - 1, partial)
                    shift = settle(i, peak)
                    peak = [lowest, lowest]
                    partial = nothing
            else:
                take(1 - parity, j - LAG, peak)
                partial = add(i, parity, j - LAG, shift, partial)
        return (*peak, shift, partial)

    push(0, 0)
    along, _ = where(0)
    peak = [lowest, lowest]
    for j in range(CHUNKS):
        issue(along, 0, j)
        if j == PUSH_AT:
            push(1, 1)
        if j >= LAG:
            take(0, j - LAG, peak)

    def turn(k, carry):
        return body(2 * k + 1, 1, body(2 * k, 0, carry))

    def close(last, parity, carry):
        *_, shift, partial = carry
        for j in range(LAG):
            for m in range(2):
                pltpu.matmul_pop(mxus[m][j + CHUNKS - LAG])
            partial = add(last, parity, j + CHUNKS - LAG, shift, partial)
        fold(last, partial)
        for m in range(2):
            pltpu.matmul_acc_lhs(mxus[m][0], jnp.zeros((CHUNK, 2 * LANES), bf16), load_staged_rhs=parity)
            pltpu.matmul_pop(mxus[m][0])

    turns = count >> 1
    carry = lax.fori_loop(0, turns, turn, (*peak, nothing, nothing))
    odd_count = (count & 1) == 1

    @pl.when(odd_count)
    def _():
        close(count - 1, 0, body(count - 1, 0, carry))

    @pl.when(jnp.logical_not(odd_count))
    def _():
        close(count - 1, 1, carry)


def finished(acc_max, acc_sum):
    total = acc_sum[...]
    lse = jnp.where(total > 0, acc_max[...] * SCALE + jnp.log(total) * LOG2E, NEG_START)
    return jnp.concatenate([lse[b:b + 1, q * LANES:(q + 1) * LANES] for b in range(4) for q in range(GROUPS)], axis=0)


def bits(list_row, y_from, c_from, y, c):
    pair = list_row.astype(jnp.int32)
    number = y_from * 4 + c_from * 2 + (pair & 1)
    mine = (pair >> 3 == c) & (((pair >> 1) & 3) == y)
    return jnp.where(mine, jnp.left_shift(jnp.ones_like(pair), number), 0).astype(f32)


def packed(own_ref, by1_ref, by2_ref, by3_ref, after_ref, out_ref):
    lists = [ref[BLOCK:BLOCK + 16, :].astype(f32)[0:1, :] for ref in (own_ref, by1_ref, by2_ref, by3_ref)]
    out_ref[...] = jnp.concatenate(lists + [jnp.zeros((4, LANES), f32)], axis=0)


def first_rows(own_ref, by1_ref, by2_ref, by3_ref, targets_ref, lists_ref, potential_ref, out_ref, sources_ref, source_squares_ref, target_squares_ref, kept_ref, *scratch):
    y, c = lax.axis_index("y"), lax.axis_index("c")
    kept = jnp.zeros((1, LANES), f32)
    for c_from in range(2):
        lists = lists_ref[c_from]
        for by in range(4):
            kept = kept + bits(lists[by:by + 1, :], (y + 4 - by) & 3, c_from, y, c)
    kept_ref[...] = jnp.broadcast_to(kept, kept_ref.shape)
    for by, ref in enumerate((own_ref, by1_ref, by2_ref, by3_ref)):
        sources_ref[pl.ds(pl.multiple_of(((y + 4 - by) & 3) * BLOCK, BLOCK), BLOCK), :] = ref[0:BLOCK, :]
    source_squares_ref[...] = squares(own_ref[0:BLOCK, :])
    squared = squares(targets_ref[...])
    target_squares_ref[...] = squared
    rows = pl.ds(pl.multiple_of(y * 8, 8), 8)
    potential = jnp.concatenate([potential_ref[0, rows, :], potential_ref[1, rows, :]], axis=0)
    bias = 0.5 * (potential - squared)
    half_step(kept_ref, targets_ref, sources_ref, bias, False, *scratch)
    spread_out(out_ref, scratch)


def kept_pairs(kept_pairs_ref, chosen):
    kept = jnp.sum(kept_pairs_ref[0:1, :]).astype(jnp.int32)
    found = jnp.int32(0)
    for number in range(PAIRS_MAX):
        chosen[found] = number
        found = found + ((kept >> number) & 1)
    return kept, found


def half_step(kept_pairs_ref, kept_ref, sum_ref, bias, kept_first, acc_max, acc_sum, even, odd, chosen, saved=None):
    clear(acc_max, acc_sum)
    _, found = kept_pairs(kept_pairs_ref, chosen)
    sweep(chosen, found, kept_ref, sum_ref, bias, acc_max, acc_sum, even, odd, kept_first, saved)


def spread_out(out_ref, scratch):
    dense = finished(scratch[0], scratch[1])
    for k in range(out_ref.shape[0]):
        out_ref[k] = dense


def next_columns(kept_ref, sources_ref, targets_ref, parts_ref, out_ref, bias_ref, terms_ref, maxima_ref, *scratch):
    bias = half_bias(combined(parts_ref[...]))
    bias_ref[...] = bias
    half_step(kept_ref, sources_ref, targets_ref, bias, True, *scratch, (terms_ref, maxima_ref))
    spread_out(out_ref, scratch)


def in_kept_blocks(kept):
    block = lax.broadcasted_iota(jnp.int32, (16, LANES), 0) >> 2
    inside = jnp.zeros((16, LANES), jnp.int32)
    for b in range(4):
        inside = jnp.where(block == b, (kept >> (4 * b)) & 15, inside)
    return inside > 0


def any_of(condition):
    return jnp.max(jnp.where(condition, 1.0, 0.0)) > 0.5


def next_rows(kept_ref, sources_ref, targets_ref, old_bias_ref, terms_ref, maxima_ref, parts_ref, out_ref, acc_max, acc_sum, even, odd, chosen, rows_ref, lse_ref):
    lse = combined(parts_ref[...])
    kept, found = kept_pairs(kept_ref, chosen)
    for b in range(4):
        lse_ref[b:b + 1, :] = jnp.concatenate([lse[4 * b + q:4 * b + q + 1, :] for q in range(GROUPS)], axis=1)
    rows_ref[...] = jnp.zeros(rows_ref.shape, f32)

    def one(n, carry):
        pair = chosen[n]
        first, second = pair >> 2, pair & 3
        weight = jnp.exp2(maxima_ref[pl.ds(n, 1), :] * SCALE - lse_ref[pl.ds(second, 1), :])
        weight = jnp.broadcast_to(weight, (8, BLOCK))
        for r in range(0, BLOCK, 8):
            scaled = terms_ref[n, r:r + 8, :] * weight
            total = (scaled[:, 0:LANES] + scaled[:, LANES:2 * LANES]) + (scaled[:, 2 * LANES:3 * LANES] + scaled[:, 3 * LANES:])
            place = pl.ds(pl.multiple_of(first * BLOCK + r, 8), 8)
            rows_ref[place, :] = rows_ref[place, :] + total
        return carry

    lax.fori_loop(0, found, one, 0)
    total = rows_ref[...]
    high = total.astype(bf16)
    rest = total - high.astype(f32)
    sums = lane_sums([high, rest.astype(bf16)])
    inside = in_kept_blocks(kept)
    bad = any_of(inside & (sums < SMALLEST))
    safe = jnp.where(inside, sums, 1.0)
    dense = jnp.where(inside, jnp.log(safe) * LOG2E - SCALE * old_bias_ref[...] - LOG2_N, NEG_START)

    @pl.when(jnp.logical_not(bad))
    def _():
        for k in range(out_ref.shape[0]):
            out_ref[k] = dense

    @pl.when(bad)
    def _():
        half_step(kept_ref, targets_ref, sources_ref, half_bias(lse), False, acc_max, acc_sum, even, odd, chosen)
        spread_out(out_ref, (acc_max, acc_sum))


def last_columns(kept_ref, sources_ref, targets_ref, source_squares_ref, target_squares_ref, old_bias_ref, terms_ref, maxima_ref, parts_ref, out_ref, all_bias, acc_max, acc_sum, even, odd, chosen, ratio_ref):
    bias = half_bias(combined(parts_ref[...]))
    all_bias[...] = bias
    own = all_bias[pl.ds(lax.axis_index("y") * GROUPS, GROUPS), :]
    out_ref[16:16 + GROUPS, :] = source_squares_ref[...] + 2.0 * own
    out_ref[16 + GROUPS:24, :] = jnp.zeros((8 - GROUPS, LANES), f32)
    offset = target_squares_ref[...] * (LOG2E / EPS_REG)
    kept, found = kept_pairs(kept_ref, chosen)
    inside = in_kept_blocks(kept)
    moved = SCALE * (bias - old_bias_ref[...])
    largest = jnp.max(jnp.where(inside, moved, NEG_START))
    bad = any_of(inside & (moved < largest - WIDEST))
    ratio = jnp.exp2(jnp.where(inside, moved - largest, 0.0))

    @pl.when(jnp.logical_not(bad))
    def _():
        for k in range(16):
            ratio_ref[k * LANES:(k + 1) * LANES, :] = jnp.broadcast_to(ratio[k:k + 1, :], (LANES, LANES)).T
        clear(acc_max, acc_sum)

        def one(n, carry):
            pair = chosen[n]
            first, second = pair >> 2, pair & 3
            partial = [jnp.zeros((8, BLOCK), f32), jnp.zeros((8, BLOCK), f32)]
            for r in range(0, BLOCK, 8):
                factor = ratio_ref[pl.ds(pl.multiple_of(first * BLOCK + r, 8), 8), :]
                partial[r // 8 % 2] = partial[r // 8 % 2] + terms_ref[n, r:r + 8, :] * jnp.concatenate([factor] * GROUPS, axis=1)
            block_sum = jnp.sum(partial[0] + partial[1], axis=0, keepdims=True)
            highest = maxima_ref[pl.ds(n, 1), :]
            old = jnp.exp2((acc_max[pl.ds(second, 1), :] - highest) * SCALE)
            acc_sum[pl.ds(second, 1), :] = acc_sum[pl.ds(second, 1), :] * old + block_sum
            acc_max[pl.ds(second, 1), :] = highest
            return carry

        lax.fori_loop(0, found, one, 0)
        out_ref[0:16, :] = finished(acc_max, acc_sum) + largest - offset

    @pl.when(bad)
    def _():
        half_step(kept_ref, sources_ref, targets_ref, bias, True, acc_max, acc_sum, even, odd, chosen)
        out_ref[0:16, :] = finished(acc_max, acc_sum) - offset


def both_cores(parts_ref, out_ref):
    rows = pl.ds(pl.multiple_of(lax.axis_index("c") * 8, 8), 8)
    lse = combined(jnp.stack([parts_ref[0, rows, :], parts_ref[1, rows, :]]))
    for k in range(out_ref.shape[0]):
        out_ref[k] = lse


def last_potentials(parts_ref, cores_ref, source_ref, target_ref):
    for b in range(2):
        source_ref[b * GROUPS:(b + 1) * GROUPS, :] = cores_ref[b, 16:16 + GROUPS, :]
    for y in range(4):
        lse = combined(jnp.stack([parts_ref[k] for k in range(y, parts_ref.shape[0], 4)]))
        target_ref[y * 8:(y + 1) * 8, :] = 2.0 * half_bias(lse)


VMEM = pl.BlockSpec(memory_space=pltpu.VMEM)
PARAMS = pltpu.CompilerParams(vmem_limit_bytes=24 * 1024 * 1024)
WORK = [pltpu.VMEM((8, BLOCK), f32)] * 2 + [pltpu.VMEM((BLOCK, BLOCK), f32)] * 2 + [pltpu.SMEM((PAIRS_MAX,), jnp.int32)]


def spread(parts, axes):
    return lax.all_to_all(parts, axes, 0, 0, tiled=True)


def call(kernel, out_shape, operands, scratch):
    return pl.pallas_call(
        kernel,
        out_shape=out_shape,
        in_specs=[VMEM] * len(operands),
        out_specs=jax.tree.map(lambda _: VMEM, out_shape),
        scratch_shapes=scratch,
        compiler_params=PARAMS,
        cost_estimate=pl.CostEstimate(flops=1 << 30, bytes_accessed=1 << 22, transcendentals=1 << 20),
    )(*operands)


def per_device(source_points, target_points, initial_potential, pair_list, pair_count):
    n_y, n_z = lax.axis_size("y"), lax.axis_size("z")
    own = target_points.shape[0]
    tgt_rows = n_z * own // LANES
    c = lax.axis_index("c")

    def shape(*dims):
        return jax.ShapeDtypeStruct(dims, f32)

    def points(*dims):
        return jax.ShapeDtypeStruct(dims, bf16)

    listed = jnp.pad(pair_list.reshape(1, PAIRS_MAX).astype(bf16), ((0, 15), (0, LANES - PAIRS_MAX)), constant_values=-1)
    sources = jnp.concatenate([lax.dynamic_slice_in_dim(source_points, c * BLOCK, BLOCK, 0), listed], axis=0)
    by = [
        lax.ppermute(sources, "y", [(i, (i + k) % n_y) for i in range(n_y)]) for k in range(1, n_y)
    ]
    targets = spread(jnp.broadcast_to(target_points[None], (n_z, own, EMB)), "z").reshape(n_z * own, EMB)
    targets = lax.all_gather(targets, "c", axis=0, tiled=True)
    potential = lax.all_gather(initial_potential.reshape(n_y * tgt_rows, LANES), "c")
    lists = lax.all_gather(call(packed, shape(8, LANES), (sources, *by, targets), []), "c")
    row_shape = shape(16, 16, LANES)
    row_parts, sources, source_squares, target_squares, kept = call(
        first_rows,
        [
            row_shape,
            points(n_y * BLOCK, EMB),
            shape(GROUPS, LANES),
            shape(2 * tgt_rows, LANES),
            shape(8, LANES),
        ],
        (sources, *by, targets, lists, potential),
        WORK,
    )
    row_parts = spread(row_parts, ("y", "x"))
    col_parts, bias, terms, maxima = call(
        next_columns,
        [row_shape, shape(16, LANES), shape(PAIRS_MAX, BLOCK, BLOCK), shape(PAIRS_MAX, BLOCK)],
        (kept, sources, targets, row_parts),
        WORK,
    )
    col_parts = spread(col_parts, ("z", "c"))
    row_parts = call(
        next_rows,
        row_shape,
        (kept, sources, targets, bias, terms, maxima, col_parts),
        WORK + [pltpu.VMEM((16 * LANES, LANES), f32), pltpu.VMEM((8, BLOCK), f32)],
    )
    row_parts = spread(row_parts, ("y", "x"))
    parts = call(
        last_columns,
        shape(24, LANES),
        (kept, sources, targets, source_squares, target_squares, bias, terms, maxima, row_parts),
        [pltpu.VMEM((16, LANES), f32)] + WORK + [pltpu.VMEM((16 * LANES, LANES), f32)],
    )
    parts = lax.all_gather(parts, "c")
    col_parts = call(both_cores, shape(n_y * n_z, tgt_rows, LANES), (parts,), [])
    col_parts = spread(col_parts, ("z", "y"))
    source_potential, target_potential = call(
        last_potentials, [shape(2 * GROUPS, LANES), shape(n_y * tgt_rows, LANES)], (col_parts, parts), []
    )
    return source_potential.reshape(-1), target_potential.reshape(-1)


def solution(mesh):
    fine = Mesh(mesh.devices.reshape(4, 8, 4, 2), ("y", "z", "x", "c"))
    src, tgt = ("y", "z"), ("x", "c")
    placed = (P(src, None), P(tgt + src, None), P(tgt), P(src, tgt, None), P(src, tgt))
    return jax.shard_map(
        per_device, mesh=fine, in_specs=placed, out_specs=(P(src), P(tgt)), check_vma=False
    )
```

```python
import functools
import math

import jax
import jax.numpy as jnp
from jax import lax
from jax.experimental import pallas as pl
from jax.experimental.pallas import tpu as pltpu
from jax.sharding import Mesh
from jax.sharding import PartitionSpec as P

BLOCK = 512
LANES = 128
EMB = 128
PAIRS_MAX = 16
NEG_START = -1e30
EPS_REG = 0.2
LOG2E = math.log2(math.e)
LOG2_N = math.log2(32768)
SMALLEST = 2.0 ** -85
WIDEST = 85.0
SCALE = 2.0 * LOG2E / EPS_REG
GROUPS = BLOCK // LANES
HALF = BLOCK // 2
CHUNK = 32
CHUNKS = BLOCK // CHUNK
LAG = 12
PUSH_AT = 4

bf16 = jnp.bfloat16
f32 = jnp.float32


def lane_sums(terms):
    ones = jnp.ones((16, 2 * EMB), bf16)
    groups = terms[0].shape[0] // HALF

    def sums(products):
        for k in range(0, len(terms), 2):
            parts = jnp.concatenate(terms[k:k + 2], axis=1)
            for g in range(groups):
                stage = g // 2 % 2
                pltpu.matmul_push_rhs(parts[g * HALF:(g + 1) * HALF], stage, g % 2, transpose=True)
                pltpu.matmul_acc_lhs(products[g], ones, load_staged_rhs=stage)
        rows = []
        for g in range(groups):
            out = pltpu.matmul_pop(products[g])
            rows += [out[0:1, :LANES], out[0:1, LANES:]]
        return jnp.concatenate(rows, axis=0)

    return pl.run_scoped(sums, [pltpu.ACC(g % 2)((16, HALF), f32) for g in range(groups)])


def squares(points):
    values = points.astype(f32)
    sq = values * values
    high = sq.astype(bf16)
    return lane_sums([high, (sq - high.astype(f32)).astype(bf16)])


def bias_columns(bias):
    high = bias.astype(bf16).astype(f32)
    rest = bias - high
    middle = rest.astype(bf16).astype(f32)
    low = rest - middle
    count = bias.shape[0]
    stacked = jnp.concatenate([high, middle, low, jnp.zeros((LANES - 3 * count, LANES), f32)], axis=0)
    return stacked.T.astype(bf16)


def combined(parts):
    highest = jnp.max(parts, axis=0)
    total = jnp.sum(jnp.exp2(parts - highest[None]), axis=0)
    return highest + jnp.log(total) * LOG2E


def half_bias(lse):
    return (-0.5 * EPS_REG / LOG2E) * (LOG2_N + lse)


def clear(acc_max, acc_sum):
    acc_max[...] = jnp.full(acc_max.shape, NEG_START, f32)
    acc_sum[...] = jnp.zeros(acc_sum.shape, f32)


def sweep(*operands):
    products = [[pltpu.ACC(m)((CHUNK, HALF), f32) for _ in range(CHUNKS)] for m in range(2)]
    pl.run_scoped(functools.partial(sweep_with, *operands), products)


def sweep_with(pairs_ref, count, kept_ref, sum_ref, bias, acc_max, acc_sum, even, odd, kept_first, saved, mxus):
    kept_bias = bias_columns(bias)
    lane = lax.broadcasted_iota(jnp.int32, (CHUNK, LANES), 1) & (bias.shape[0] - 1)
    ones = jnp.ones((HALF, LANES), bf16)
    zeros = jnp.zeros((CHUNK, LANES), bf16)
    buffers = (even, odd)

    def where(number):
        real = number < count
        pair = jnp.where(real, pairs_ref[jnp.clip(number, 0, PAIRS_MAX - 1)], 0)
        first, second = pair >> 2, pair & 3
        return (first, second) if kept_first else (second, first)

    def push(number, parity):
        _, place = where(number)
        for m in range(2):
            rows = sum_ref[pl.ds(pl.multiple_of(place * BLOCK + m * HALF, HALF), HALF), :]
            pltpu.matmul_push_rhs(jnp.concatenate([rows, ones], axis=1), parity, m, transpose=True)

    def issue(along, parity, j):
        rows = kept_ref[pl.ds(pl.multiple_of(along * BLOCK + j * CHUNK, CHUNK), CHUNK), :]
        start = j * CHUNK % LANES
        mine = jnp.where(lane == along * GROUPS + j * CHUNK // LANES, kept_bias[start:start + CHUNK], zeros)
        lhs = jnp.concatenate([rows, mine], axis=1)
        for m in range(2):
            pltpu.matmul_acc_lhs(mxus[m][j], lhs, load_staged_rhs=parity if j == 0 else None)

    def take(parity, j, peak):
        for m in range(2):
            out = pltpu.matmul_pop(mxus[m][j])
            buffers[parity][j * CHUNK:(j + 1) * CHUNK, m * HALF:(m + 1) * HALF] = out
            for r in range(0, CHUNK, 8):
                peak[m] = jnp.maximum(peak[m], out[r:r + 8])

    def add(number, parity, j, shift, partial):
        for r in range(j * CHUNK, (j + 1) * CHUNK, 8):
            terms = jnp.exp2((buffers[parity][r:r + 8, :] - shift) * SCALE)
            partial = partial + terms
            if saved is not None:
                saved[0][jnp.maximum(number, 0), r:r + 8, :] = terms
        return partial

    def settle(number, peak):
        _, place = where(number)
        block_max = jnp.max(jnp.concatenate(peak, axis=1), axis=0, keepdims=True)
        old_max = acc_max[pl.ds(place, 1), :]
        highest = jnp.where(number < count, jnp.maximum(old_max, block_max), old_max)
        acc_max[pl.ds(place, 1), :] = highest
        if saved is not None:
            saved[1][pl.ds(number, 1), :] = highest
        acc_sum[pl.ds(place, 1), :] = acc_sum[pl.ds(place, 1), :] * jnp.exp2((old_max - highest) * SCALE)
        return jnp.broadcast_to(highest, (8, BLOCK))

    def fold(number, partial):
        _, place = where(number)
        block_sum = jnp.where((number >= 0) & (number < count), jnp.sum(partial, axis=0, keepdims=True), 0.0)
        place = jnp.where(number >= 0, place, 0)
        acc_sum[pl.ds(place, 1), :] = acc_sum[pl.ds(place, 1), :] + block_sum

    lowest = jnp.full((8, HALF), NEG_START, f32)
    nothing = jnp.zeros((8, BLOCK), f32)

    def body(i, parity, carry):
        peak0, peak1, shift, partial = carry
        peak = [peak0, peak1]
        along, _ = where(i + 1)
        for j in range(CHUNKS):
            issue(along, 1 - parity, j)
            if j == PUSH_AT:
                push(i + 2, parity)
            if j < LAG:
                take(parity, j + CHUNKS - LAG, peak)
                partial = add(i - 1, 1 - parity, j + CHUNKS - LAG, shift, partial)
                if j == LAG - 1:
                    fold(i - 1, partial)
                    shift = settle(i, peak)
                    peak = [lowest, lowest]
                    partial = nothing
            else:
                take(1 - parity, j - LAG, peak)
                partial = add(i, parity, j - LAG, shift, partial)
        return (*peak, shift, partial)

    push(0, 0)
    along, _ = where(0)
    peak = [lowest, lowest]
    for j in range(CHUNKS):
        issue(along, 0, j)
        if j == PUSH_AT:
            push(1, 1)
        if j >= LAG:
            take(0, j - LAG, peak)

    def turn(k, carry):
        return body(2 * k + 1, 1, body(2 * k, 0, carry))

    def close(last, parity, carry):
        *_, shift, partial = carry
        for j in range(LAG):
            for m in range(2):
                pltpu.matmul_pop(mxus[m][j + CHUNKS - LAG])
            partial = add(last, parity, j + CHUNKS - LAG, shift, partial)
        fold(last, partial)
        for m in range(2):
            pltpu.matmul_acc_lhs(mxus[m][0], jnp.zeros((CHUNK, 2 * LANES), bf16), load_staged_rhs=parity)
            pltpu.matmul_pop(mxus[m][0])

    turns = count >> 1
    carry = lax.fori_loop(0, turns, turn, (*peak, nothing, nothing))
    odd_count = (count & 1) == 1

    @pl.when(odd_count)
    def _():
        close(count - 1, 0, body(count - 1, 0, carry))

    @pl.when(jnp.logical_not(odd_count))
    def _():
        close(count - 1, 1, carry)


def finished(acc_max, acc_sum):
    total = acc_sum[...]
    lse = jnp.where(total > 0, acc_max[...] * SCALE + jnp.log(total) * LOG2E, NEG_START)
    return jnp.concatenate([lse[b:b + 1, q * LANES:(q + 1) * LANES] for b in range(4) for q in range(GROUPS)], axis=0)


def bits(list_row, y_from, c_from, y, c):
    pair = list_row.astype(jnp.int32)
    number = y_from * 4 + c_from * 2 + (pair & 1)
    mine = (pair >> 3 == c) & (((pair >> 1) & 3) == y)
    return jnp.where(mine, jnp.left_shift(jnp.ones_like(pair), number), 0).astype(f32)


def packed(own_ref, by1_ref, by2_ref, by3_ref, after_ref, out_ref):
    lists = [ref[BLOCK:BLOCK + 16, :].astype(f32)[0:1, :] for ref in (own_ref, by1_ref, by2_ref, by3_ref)]
    out_ref[...] = jnp.concatenate(lists + [jnp.zeros((4, LANES), f32)], axis=0)


def first_rows(own_ref, by1_ref, by2_ref, by3_ref, targets_ref, lists_ref, potential_ref, out_ref, sources_ref, source_squares_ref, target_squares_ref, kept_ref, *scratch):
    y, c = lax.axis_index("y"), lax.axis_index("c")
    kept = jnp.zeros((1, LANES), f32)
    for c_from in range(2):
        lists = lists_ref[c_from]
        for by in range(4):
            kept = kept + bits(lists[by:by + 1, :], (y + 4 - by) & 3, c_from, y, c)
    kept_ref[...] = jnp.broadcast_to(kept, kept_ref.shape)
    for by, ref in enumerate((own_ref, by1_ref, by2_ref, by3_ref)):
        sources_ref[pl.ds(pl.multiple_of(((y + 4 - by) & 3) * BLOCK, BLOCK), BLOCK), :] = ref[0:BLOCK, :]
    source_squares_ref[...] = squares(own_ref[0:BLOCK, :])
    squared = squares(targets_ref[...])
    target_squares_ref[...] = squared
    rows = pl.ds(pl.multiple_of(y * 8, 8), 8)
    potential = jnp.concatenate([potential_ref[0, rows, :], potential_ref[1, rows, :]], axis=0)
    bias = 0.5 * (potential - squared)
    half_step(kept_ref, targets_ref, sources_ref, bias, False, *scratch)
    spread_out(out_ref, scratch)


def kept_pairs(kept_pairs_ref, chosen):
    kept = jnp.sum(kept_pairs_ref[0:1, :]).astype(jnp.int32)
    found = jnp.int32(0)
    for number in range(PAIRS_MAX):
        chosen[found] = number
        found = found + ((kept >> number) & 1)
    return kept, found


def half_step(kept_pairs_ref, kept_ref, sum_ref, bias, kept_first, acc_max, acc_sum, even, odd, chosen, saved=None):
    clear(acc_max, acc_sum)
    _, found = kept_pairs(kept_pairs_ref, chosen)
    sweep(chosen, found, kept_ref, sum_ref, bias, acc_max, acc_sum, even, odd, kept_first, saved)


def spread_out(out_ref, scratch):
    dense = finished(scratch[0], scratch[1])
    for k in range(out_ref.shape[0]):
        out_ref[k] = dense


def next_columns(kept_ref, sources_ref, targets_ref, parts_ref, out_ref, bias_ref, terms_ref, maxima_ref, *scratch):
    bias = half_bias(combined(parts_ref[...]))
    bias_ref[...] = bias
    half_step(kept_ref, sources_ref, targets_ref, bias, True, *scratch, (terms_ref, maxima_ref))
    spread_out(out_ref, scratch)


def in_kept_blocks(kept):
    block = lax.broadcasted_iota(jnp.int32, (16, LANES), 0) >> 2
    inside = jnp.zeros((16, LANES), jnp.int32)
    for b in range(4):
        inside = jnp.where(block == b, (kept >> (4 * b)) & 15, inside)
    return inside > 0


def any_of(condition):
    return jnp.max(jnp.where(condition, 1.0, 0.0)) > 0.5


def next_rows(kept_ref, sources_ref, targets_ref, old_bias_ref, terms_ref, maxima_ref, parts_ref, out_ref, acc_max, acc_sum, even, odd, chosen, rows_ref, lse_ref):
    lse = combined(parts_ref[...])
    kept, found = kept_pairs(kept_ref, chosen)
    for b in range(4):
        lse_ref[b:b + 1, :] = jnp.concatenate([lse[4 * b + q:4 * b + q + 1, :] for q in range(GROUPS)], axis=1)
    rows_ref[...] = jnp.zeros(rows_ref.shape, f32)

    def one(n, carry):
        pair = chosen[n]
        first, second = pair >> 2, pair & 3
        weight = jnp.exp2(maxima_ref[pl.ds(n, 1), :] * SCALE - lse_ref[pl.ds(second, 1), :])
        weight = jnp.broadcast_to(weight, (8, BLOCK))
        for r in range(0, BLOCK, 8):
            scaled = terms_ref[n, r:r + 8, :] * weight
            total = (scaled[:, 0:LANES] + scaled[:, LANES:2 * LANES]) + (scaled[:, 2 * LANES:3 * LANES] + scaled[:, 3 * LANES:])
            place = pl.ds(pl.multiple_of(first * BLOCK + r, 8), 8)
            rows_ref[place, :] = rows_ref[place, :] + total
        return carry

    lax.fori_loop(0, found, one, 0)
    total = rows_ref[...]
    high = total.astype(bf16)
    rest = total - high.astype(f32)
    sums = lane_sums([high, rest.astype(bf16)])
    inside = in_kept_blocks(kept)
    bad = any_of(inside & (sums < SMALLEST))
    safe = jnp.where(inside, sums, 1.0)
    dense = jnp.where(inside, jnp.log(safe) * LOG2E - SCALE * old_bias_ref[...] - LOG2_N, NEG_START)

    @pl.when(jnp.logical_not(bad))
    def _():
        for k in range(out_ref.shape[0]):
            out_ref[k] = dense

    @pl.when(bad)
    def _():
        half_step(kept_ref, targets_ref, sources_ref, half_bias(lse), False, acc_max, acc_sum, even, odd, chosen)
        spread_out(out_ref, (acc_max, acc_sum))


def last_columns(kept_ref, sources_ref, targets_ref, source_squares_ref, target_squares_ref, old_bias_ref, terms_ref, maxima_ref, parts_ref, out_ref, all_bias, acc_max, acc_sum, even, odd, chosen, ratio_ref):
    bias = half_bias(combined(parts_ref[...]))
    all_bias[...] = bias
    own = all_bias[pl.ds(lax.axis_index("y") * GROUPS, GROUPS), :]
    out_ref[16:16 + GROUPS, :] = source_squares_ref[...] + 2.0 * own
    out_ref[16 + GROUPS:24, :] = jnp.zeros((8 - GROUPS, LANES), f32)
    offset = target_squares_ref[...] * (LOG2E / EPS_REG)
    kept, found = kept_pairs(kept_ref, chosen)
    inside = in_kept_blocks(kept)
    moved = SCALE * (bias - old_bias_ref[...])
    largest = jnp.max(jnp.where(inside, moved, NEG_START))
    bad = any_of(inside & (moved < largest - WIDEST))
    ratio = jnp.exp2(jnp.where(inside, moved - largest, 0.0))

    @pl.when(jnp.logical_not(bad))
    def _():
        for k in range(16):
            ratio_ref[k * LANES:(k + 1) * LANES, :] = jnp.broadcast_to(ratio[k:k + 1, :], (LANES, LANES)).T
        clear(acc_max, acc_sum)

        def one(n, carry):
            pair = chosen[n]
            first, second = pair >> 2, pair & 3
            partial = [jnp.zeros((8, BLOCK), f32), jnp.zeros((8, BLOCK), f32)]
            for r in range(0, BLOCK, 8):
                factor = ratio_ref[pl.ds(pl.multiple_of(first * BLOCK + r, 8), 8), :]
                partial[r // 8 % 2] = partial[r // 8 % 2] + terms_ref[n, r:r + 8, :] * jnp.concatenate([factor] * GROUPS, axis=1)
            block_sum = jnp.sum(partial[0] + partial[1], axis=0, keepdims=True)
            highest = maxima_ref[pl.ds(n, 1), :]
            old = jnp.exp2((acc_max[pl.ds(second, 1), :] - highest) * SCALE)
            acc_sum[pl.ds(second, 1), :] = acc_sum[pl.ds(second, 1), :] * old + block_sum
            acc_max[pl.ds(second, 1), :] = highest
            return carry

        lax.fori_loop(0, found, one, 0)
        out_ref[0:16, :] = finished(acc_max, acc_sum) + largest - offset

    @pl.when(bad)
    def _():
        half_step(kept_ref, sources_ref, targets_ref, bias, True, acc_max, acc_sum, even, odd, chosen)
        out_ref[0:16, :] = finished(acc_max, acc_sum) - offset


def both_cores(parts_ref, out_ref):
    rows = pl.ds(pl.multiple_of(lax.axis_index("c") * 8, 8), 8)
    lse = combined(jnp.stack([parts_ref[0, rows, :], parts_ref[1, rows, :]]))
    for k in range(out_ref.shape[0]):
        out_ref[k] = lse


def last_potentials(parts_ref, cores_ref, source_ref, target_ref):
    for b in range(2):
        source_ref[b * GROUPS:(b + 1) * GROUPS, :] = cores_ref[b, 16:16 + GROUPS, :]
    count = parts_ref.shape[0] // 4
    for y in range(4):
        lse = combined(parts_ref[y * count:(y + 1) * count])
        target_ref[y * 8:(y + 1) * 8, :] = 2.0 * half_bias(lse)


VMEM = pl.BlockSpec(memory_space=pltpu.VMEM)
PARAMS = pltpu.CompilerParams(vmem_limit_bytes=24 * 1024 * 1024)
WORK = [pltpu.VMEM((8, BLOCK), f32)] * 2 + [pltpu.VMEM((BLOCK, BLOCK), f32)] * 2 + [pltpu.SMEM((PAIRS_MAX,), jnp.int32)]


def spread(parts, axes):
    return lax.all_to_all(parts, axes, 0, 0, tiled=True)


def call(kernel, out_shape, operands, scratch):
    return pl.pallas_call(
        kernel,
        out_shape=out_shape,
        in_specs=[VMEM] * len(operands),
        out_specs=jax.tree.map(lambda _: VMEM, out_shape),
        scratch_shapes=scratch,
        compiler_params=PARAMS,
        cost_estimate=pl.CostEstimate(flops=1 << 30, bytes_accessed=1 << 22, transcendentals=1 << 20),
    )(*operands)


def per_device(source_points, target_points, initial_potential, pair_list, pair_count):
    n_y, n_z = lax.axis_size("y"), lax.axis_size("z")
    own = target_points.shape[0]
    tgt_rows = n_z * own // LANES
    c = lax.axis_index("c")

    def shape(*dims):
        return jax.ShapeDtypeStruct(dims, f32)

    def points(*dims):
        return jax.ShapeDtypeStruct(dims, bf16)

    listed = jnp.pad(pair_list.reshape(1, PAIRS_MAX).astype(bf16), ((0, 15), (0, LANES - PAIRS_MAX)), constant_values=-1)
    sources = jnp.concatenate([lax.dynamic_slice_in_dim(source_points, c * BLOCK, BLOCK, 0), listed], axis=0)
    by = [
        lax.ppermute(sources, "y", [(i, (i + k) % n_y) for i in range(n_y)]) for k in range(1, n_y)
    ]
    targets = spread(jnp.broadcast_to(target_points[None], (n_z, own, EMB)), "z").reshape(n_z * own, EMB)
    targets = lax.all_gather(targets, "c", axis=0, tiled=True)
    potential = lax.all_gather(initial_potential.reshape(n_y * tgt_rows, LANES), "c")
    lists = lax.all_gather(call(packed, shape(8, LANES), (sources, *by, targets), []), "c")
    row_shape = shape(16, 16, LANES)
    row_parts, sources, source_squares, target_squares, kept = call(
        first_rows,
        [
            row_shape,
            points(n_y * BLOCK, EMB),
            shape(GROUPS, LANES),
            shape(2 * tgt_rows, LANES),
            shape(8, LANES),
        ],
        (sources, *by, targets, lists, potential),
        WORK,
    )
    row_parts = spread(row_parts, ("y", "x"))
    col_parts, bias, terms, maxima = call(
        next_columns,
        [row_shape, shape(16, LANES), shape(PAIRS_MAX, BLOCK, BLOCK), shape(PAIRS_MAX, BLOCK)],
        (kept, sources, targets, row_parts),
        WORK,
    )
    col_parts = spread(col_parts, ("z", "c"))
    row_parts = call(
        next_rows,
        row_shape,
        (kept, sources, targets, bias, terms, maxima, col_parts),
        WORK + [pltpu.VMEM((16 * LANES, LANES), f32), pltpu.VMEM((8, BLOCK), f32)],
    )
    row_parts = spread(row_parts, ("y", "x"))
    parts = call(
        last_columns,
        shape(24, LANES),
        (kept, sources, targets, source_squares, target_squares, bias, terms, maxima, row_parts),
        [pltpu.VMEM((16, LANES), f32)] + WORK + [pltpu.VMEM((16 * LANES, LANES), f32)],
    )
    parts = lax.all_gather(parts, "c")
    col_parts = call(both_cores, shape(n_y * n_z, tgt_rows, LANES), (parts,), [])
    col_parts = spread(col_parts, ("y", "z"))
    source_potential, target_potential = call(
        last_potentials, [shape(2 * GROUPS, LANES), shape(n_y * tgt_rows, LANES)], (col_parts, parts), []
    )
    return source_potential.reshape(-1), target_potential.reshape(-1)


def solution(mesh):
    fine = Mesh(mesh.devices.reshape(4, 8, 4, 2), ("y", "z", "x", "c"))
    src, tgt = ("y", "z"), ("x", "c")
    placed = (P(src, None), P(tgt + src, None), P(tgt), P(src, tgt, None), P(src, tgt))
    return jax.shard_map(
        per_device, mesh=fine, in_specs=placed, out_specs=(P(src), P(tgt)), check_vma=False
    )
```
